128 devices in a mesh: gx: 8 (over x, core), gy: 16 (over y, z).
Axes of the slice: x: 4, y: 4, z: 4, core: 2. Of those that a mesh axis runs over, the one named last changes fastest.
Arguments:
- flow_state: float32 [6, 256, 32768], P(None, 'gx', 'gy'), may hold values from -6 to 6
- drag_coefficient: float32 [256, 32768], P('gx', 'gy'), may hold values from 0.05 to 0.5
- wet_mask: int32 [256, 32768], P('gx', 'gy'), may hold values 0 or 1
- target_elem: int32 [256, 32768], P('gx', 'gy'), may hold values from 0 to 32767, as said below
- target_node: int32 [256, 32768], P('gx', 'gy'), may hold values from 0 to 24
- displacement: float32 [3, 5, 5, 5, 2, 16, 2048], P(None, None, None, None, None, 'gx', 'gy'), as said below
- previous: float32 [3, 5, 5, 5, 2, 16, 2048], P(None, None, None, None, None, 'gx', 'gy'), as said below
- density: float32 [2, 16, 2048], P(None, 'gx', 'gy'), may hold values from 1 to 3
- lame_first: float32 [2, 16, 2048], P(None, 'gx', 'gy'), may hold values from 1 to 4
- shear_modulus: float32 [2, 16, 2048], P(None, 'gx', 'gy'), may hold values from 0.5 to 2
Outputs:
- flow_final: float32 [6, 256, 32768], P(None, 'gx', 'gy')
- displacement_next: float32 [3, 5, 5, 5, 2, 16, 2048], P(None, None, None, None, None, 'gx', 'gy')
- displacement_last: float32 [3, 5, 5, 5, 2, 16, 2048], P(None, None, None, None, None, 'gx', 'gy')
The draws below stay inside these ranges and needn't reach their ends.
Inputs may be any that keep to these rules, and one draw needn't show every extreme that they name: `target_elem`: each cell's element lies at most one element row and one element column outside the 2 x 128 block of elements that shares the cell's device; the value is element row times 2048 plus element column. `displacement`: a grid point shared by adjacent elements holds the same value in every copy. `previous`: a grid point shared by adjacent elements holds the same value in every copy.
All inputs are finite; a program needn't handle non-finite values. No bound on the sum of `wet_mask` on one device may be relied on, other than what follows from the above.
Results may differ from the reference program's by a relative error of at most 0.00021.
Values sent between devices are 32-bit elements; how exact they have to be, the bound alone decides.
A program may use at most 192 MiB of HBM per device.

```python
import math
import jax
import jax.numpy as jnp
import numpy as np
from jax import lax

ELZ = 2
CPE = 16
FLOW_STEPS = 4
SOLID_STEPS = 2
EXG = 16
EYG = 2048
SR = 256
SC = 32768


def element_view(grid):
    x_index = jnp.arange(5).reshape(5, 1, 1, 1, 1, 1) + 4 * jnp.arange(EXG).reshape(1, 1, 1, 1, EXG, 1)
    y_index = jnp.arange(5).reshape(1, 5, 1, 1, 1, 1) + 4 * jnp.arange(EYG).reshape(1, 1, 1, 1, 1, EYG)
    z_index = jnp.arange(5).reshape(1, 1, 5, 1, 1, 1) + 4 * jnp.arange(ELZ).reshape(1, 1, 1, ELZ, 1, 1)
    return grid[:, x_index, y_index, z_index]


def consistent_field(key):
    shape = (3, 4 * EXG + 1, 4 * EYG + 1, 4 * ELZ + 1)
    grid = jax.random.normal(key, shape, jnp.float32)
    return element_view(grid).astype(jnp.float32)


def draw_displacement(key, part):
    return consistent_field(jax.random.fold_in(key, 11))


def draw_previous(key, part):
    return consistent_field(jax.random.fold_in(key, 23))


def draw_target_elem(key, part):
    elem_rows = (jnp.arange(SR, dtype=jnp.int32) // CPE)[:, None]
    elem_cols = (jnp.arange(SC, dtype=jnp.int32) // CPE)[None, :]
    jitter_rows = jax.random.randint(jax.random.fold_in(key, 5), (SR, SC), -1, 2)
    jitter_cols = jax.random.randint(jax.random.fold_in(key, 7), (SR, SC), -1, 2)
    rows_hit = jnp.clip(elem_rows + jitter_rows, 0, EXG - 1)
    cols_hit = jnp.clip(elem_cols + jitter_cols, 0, EYG - 1)
    return (rows_hit * EYG + cols_hit).astype(jnp.int32)


def set_ends(entries, rng, least, top_value):
    shape = entries.shape
    index_at = [jax.random.randint(jax.random.fold_in(rng, axis), (), 0, shape[axis]) for axis in range(len(shape))]
    entries = entries.at[tuple(index_at)].set(least)
    longest = shape.index(max(shape))
    index_at[longest] = (index_at[longest] + 1) % shape[longest]
    return entries.at[tuple(index_at)].set(top_value)


def shard_levels(stream_key, shape, cuts, low, top_value):
    factor_of = 1.0
    for dim, parts in cuts:
        heights = jax.random.uniform(jax.random.fold_in(jax.random.fold_in(stream_key, 6), dim), (parts,), jnp.float32, low / len(cuts), top_value / len(cuts))
        factor_of = factor_of * jnp.repeat(jnp.exp(heights), shape[dim] // parts).reshape((-1,) + (1,) * (len(shape) - 1 - dim))
    return factor_of


def gaussian(stream_key, shape, scale, most, shards=(), kind=jnp.bfloat16):
    loudness = shard_levels(stream_key, shape, shards, -0.22, 0.18) if shards else 1.0
    values = jax.random.normal(stream_key, shape, jnp.float32) * scale * loudness
    return jnp.minimum(jnp.maximum(values, -most), most).astype(kind)


def setup_inputs(seed: int = 0) -> dict:
    seeds = jax.random.split(jax.random.key(seed), 11)
    return {
        "flow_state": gaussian(seeds[0], (6, SR, SC), 1.0, 6.0, ((1, 8), (2, 16)), jnp.float32),
        "drag_coefficient": jnp.clip(jnp.exp(math.log(0.5) - 2.3025851 * jax.random.uniform(seeds[1], (SR, SC), jnp.float32) ** shard_levels(seeds[1], (SR, SC), ((0, 8), (1, 16)), -0.2, 0.2)), 0.05, 0.5),
        "wet_mask": set_ends((jax.random.randint(seeds[2], (SR, SC), 0, 2) < 1).astype(jnp.int32), jax.random.fold_in(seeds[2], 1), 0, 1),
        "target_elem": draw_target_elem(jax.random.fold_in(seeds[10], 71), 0),
        "target_node": set_ends(jax.random.randint(seeds[4], (SR, SC), 0, 25), jax.random.fold_in(seeds[4], 1), 0, 24).astype(jnp.int32),
        "displacement": draw_displacement(jax.random.fold_in(seeds[10], 71), 0),
        "previous": draw_previous(jax.random.fold_in(seeds[10], 71), 0),
        "density": jnp.clip(jnp.exp(math.log(3.0) - 1.0986123 * jax.random.uniform(seeds[7], (ELZ, EXG, EYG), jnp.float32) ** shard_levels(seeds[7], (ELZ, EXG, EYG), ((1, 8), (2, 16)), -0.2, 0.2)), 1.0, 3.0),
        "lame_first": jnp.clip(jnp.exp(math.log(4.0) - 1.3862944 * jax.random.uniform(seeds[8], (ELZ, EXG, EYG), jnp.float32) ** shard_levels(seeds[8], (ELZ, EXG, EYG), ((1, 8), (2, 16)), -0.2, 0.2)), 1.0, 4.0),
        "shear_modulus": jnp.clip(jnp.exp(math.log(2.0) - 1.3862944 * jax.random.uniform(seeds[9], (ELZ, EXG, EYG), jnp.float32) ** shard_levels(seeds[9], (ELZ, EXG, EYG), ((1, 8), (2, 16)), -0.2, 0.2)), 0.5, 2.0),
    }


gll_points = np.array([-1.0, -np.sqrt(3.0 / 7.0), 0.0, np.sqrt(3.0 / 7.0), 1.0])
gll_weights = np.array([0.1, 49.0 / 90.0, 32.0 / 45.0, 49.0 / 90.0, 0.1])
flow_dt = 0.4
diffusion = 0.2
coupling = 0.5
upper_gravity = 0.8
density_ratio = 0.7
speed_floor = 0.0001
load_factor = 4.0
solid_dt = 0.04

def legendre_four(x):
    return (35.0 * x ** 4 - 30.0 * x ** 2 + 3.0) / 8.0

def derivative_table():
    result = np.zeros((5, 5))
    for i in range(5):
        for j in range(5):
            if i != j:
                result[i, j] = legendre_four(gll_points[i]) / legendre_four(gll_points[j]) / (gll_points[i] - gll_points[j])
    result[0, 0] = -5.0
    result[4, 4] = 5.0
    return result

def pressures(fields, buoyancy):
    press_one = buoyancy * (fields[0] + fields[1])
    press_two = upper_gravity * (density_ratio * fields[0] + fields[1])
    return jnp.concatenate([fields, press_one[None], press_two[None]], axis=0)

def advance(center, padded, drag_coefficient):
    ahead_x = padded[:, 2:, 1:-1]
    behind_x = padded[:, :-2, 1:-1]
    ahead_y = padded[:, 1:-1, 2:]
    behind_y = padded[:, 1:-1, :-2]
    slope_x = 0.5 * (ahead_x - behind_x)
    slope_y = 0.5 * (ahead_y - behind_y)
    spread = ahead_x + behind_x + ahead_y + behind_y - 4.0 * center
    flow_speed = jnp.sqrt(center[2] * center[2] + center[3] * center[3] + speed_floor)
    dense_depth = center[0] - flow_dt * (slope_x[2] + slope_y[3]) + diffusion * spread[0]
    light_depth = center[1] - flow_dt * (slope_x[4] + slope_y[5]) + diffusion * spread[1]
    dense_xmom = center[2] - flow_dt * (slope_x[6] + drag_coefficient * flow_speed * center[2] + coupling * (center[2] - center[4])) + diffusion * spread[2]
    dense_ymom = center[3] - flow_dt * (slope_y[6] + drag_coefficient * flow_speed * center[3] + coupling * (center[3] - center[5])) + diffusion * spread[3]
    light_xmom = center[4] - flow_dt * (slope_x[7] + coupling * (center[4] - center[2])) + diffusion * spread[4]
    light_ymom = center[5] - flow_dt * (slope_y[7] + coupling * (center[5] - center[3])) + diffusion * spread[5]
    return jnp.stack([dense_depth, light_depth, dense_xmom, dense_ymom, light_xmom, light_ymom])

def basal_traction(fields, buoyancy, drag_coefficient):
    flow_speed = jnp.sqrt(fields[2] * fields[2] + fields[3] * fields[3] + speed_floor)
    press_one = buoyancy * (fields[0] + fields[1])
    rubbing = load_factor * drag_coefficient * flow_speed
    return jnp.stack([rubbing * fields[2], rubbing * fields[3], -load_factor * press_one]).reshape(3, -1)

def weights_cube():
    cube = gll_weights.reshape(5, 1, 1) * gll_weights.reshape(1, 5, 1) * gll_weights.reshape(1, 1, 5)
    return jnp.asarray(cube.reshape(5, 5, 5, 1, 1, 1), jnp.float32)

def internal_force(values, lame_first, shear_modulus):
    highest = lax.Precision.HIGHEST
    table = jnp.asarray(derivative_table(), jnp.float32)
    weights_3d = weights_cube()
    gradients = [jnp.einsum('pa,iabczxy->ipbczxy', table, values, precision=highest), jnp.einsum('pb,iabczxy->iapczxy', table, values, precision=highest), jnp.einsum('pc,iabczxy->iabpzxy', table, values, precision=highest)]
    divergence = gradients[0][0] + gradients[1][1] + gradients[2][2]
    forces = []
    for i in range(3):
        weighted = []
        for j in range(3):
            stress = shear_modulus * (gradients[j][i] + gradients[i][j])
            if i == j:
                stress = stress + lame_first * divergence
            weighted.append(weights_3d * stress)
        pulled = jnp.einsum('pa,pbczxy->abczxy', table, weighted[0], precision=highest)
        pulled = pulled + jnp.einsum('pb,apczxy->abczxy', table, weighted[1], precision=highest)
        pulled = pulled + jnp.einsum('pc,abpzxy->abczxy', table, weighted[2], precision=highest)
        forces.append(-pulled)
    return jnp.stack(forces)

def assemble(values):
    summed = values[:, 4, :, :, :, :-1, :] + values[:, 0, :, :, :, 1:, :]
    values = values.at[:, 4, :, :, :, :-1, :].set(summed).at[:, 0, :, :, :, 1:, :].set(summed)
    summed = values[:, :, 4, :, :, :, :-1] + values[:, :, 0, :, :, :, 1:]
    values = values.at[:, :, 4, :, :, :, :-1].set(summed).at[:, :, 0, :, :, :, 1:].set(summed)
    summed = values[:, :, :, 4, :-1] + values[:, :, :, 0, 1:]
    values = values.at[:, :, :, 4, :-1].set(summed).at[:, :, :, 0, 1:].set(summed)
    return values

def reference(flow_state, drag_coefficient, wet_mask, target_elem, target_node, displacement, previous, density, lame_first, shear_modulus):
    buoyancy = 1.0 - 0.6 * wet_mask.astype(jnp.float32)
    fields = flow_state
    for counter in range(FLOW_STEPS):
        stacked = pressures(fields, buoyancy)
        padded = jnp.pad(stacked, ((0, 0), (1, 1), (1, 1)))
        fields = advance(stacked, padded, drag_coefficient)
    traction = basal_traction(fields, buoyancy, drag_coefficient)
    slot_index = (target_node.reshape(-1) * (EXG * EYG) + target_elem.reshape(-1)).astype(jnp.int32)
    surface_load = jnp.zeros((3, 25 * EXG * EYG), jnp.float32).at[:, slot_index].add(traction)
    surface_load = surface_load.reshape(3, 5, 5, EXG, EYG)
    masses = assemble(density[None, None, None, None] * weights_cube()[None])
    current = displacement
    for counter in range(SOLID_STEPS):
        force = internal_force(current, lame_first, shear_modulus)
        force = force.at[:, :, :, 0, 0].add(surface_load)
        acceleration = assemble(force) / masses
        advanced = 2.0 * current - previous + solid_dt * solid_dt * acceleration
        previous = current
        current = advanced
    return (fields, current, previous)
```

```python
import jax
import jax.numpy as jnp
import numpy as np
from jax import lax
from jax.experimental import pallas as pl
from jax.experimental.pallas import tpu as pltpu
from jax.sharding import PartitionSpec as P

FLOW_STEPS = 4
SOLID_STEPS = 2


gll_points = np.array([-1.0, -np.sqrt(3.0 / 7.0), 0.0, np.sqrt(3.0 / 7.0), 1.0])
gll_weights = np.array([0.1, 49.0 / 90.0, 32.0 / 45.0, 49.0 / 90.0, 0.1])
flow_dt = 0.4
diffusion = 0.2
coupling = 0.5
upper_gravity = 0.8
density_ratio = 0.7
speed_floor = 0.0001
load_factor = 4.0
solid_dt = 0.04


def extended(block, sides, width):
    for axis, dim in sides:
        count = lax.axis_size(axis)
        forward = [(i, i + 1) for i in range(count - 1)]
        backward = [(target, source) for source, target in forward]
        low = lax.ppermute(
            lax.slice_in_dim(block, block.shape[dim] - width, None, axis=dim), axis, forward
        )
        high = lax.ppermute(lax.slice_in_dim(block, 0, width, axis=dim), axis, backward)
        block = jnp.concatenate([low, block, high], axis=dim)
    return block


def legendre_four(x):
    return (35.0 * x**4 - 30.0 * x**2 + 3.0) / 8.0


def derivative_table():
    result = np.zeros((5, 5))
    for i in range(5):
        for j in range(5):
            if i != j:
                result[i, j] = (
                    legendre_four(gll_points[i])
                    / legendre_four(gll_points[j])
                    / (gll_points[i] - gll_points[j])
                )
    result[0, 0] = -5.0
    result[4, 4] = 5.0
    return result


def flow_body(
    drag_ref, wet_ref, elem_ref, node_ref, flow_any,
    xlo_ref, xhi_ref, ylo_ref, yhi_ref, corner_ref,
    out_any, table_ref,
    ext, drag, buoy, scale, tract, row_slot, col_slot, sems,
):
    rows, cols = drag_ref.shape
    wide = cols + 128
    tall = rows + 8
    at_x, at_y = lax.axis_index("gx"), lax.axis_index("gy")
    last_x, last_y = lax.axis_size("gx") - 1, lax.axis_size("gy") - 1
    own_in = pltpu.make_async_copy(flow_any, ext.at[0, :, 0:rows, 0:cols], sems.at[0])
    own_in.start()

    def wetness(x):
        return 1.0 - 0.6 * x

    sub = lax.broadcasted_iota(jnp.int32, (8, 128), 0)
    lane = lax.broadcasted_iota(jnp.int32, (8, 128), 1)
    up_half = sub < 4
    left_half = lane < 64

    def zero_rows(tile):
        tile = jnp.where(up_half & (at_x == last_x), 0.0, tile)
        return jnp.where(jnp.logical_not(up_half) & (at_x == 0), 0.0, tile)

    def zero_cols(tile):
        tile = jnp.where(left_half & (at_y == last_y), 0.0, tile)
        return jnp.where(jnp.logical_not(left_half) & (at_y == 0), 0.0, tile)

    def place(k, r, c, tile):
        if k < 6:
            ext[0, k, r, c] = tile
        elif k == 6:
            drag[r, c] = tile
        else:
            buoy[r, c] = wetness(tile)

    tail = pl.ds(cols, 128)
    foot = pl.ds(rows, 8)
    ones = jnp.full((8, 128), 0.2, jnp.float32)
    row_scale = zero_rows(ones)
    col_scale = zero_cols(ones)

    def halo_rows(t, carry):
        at = pl.ds(pl.multiple_of(t * 128, 128), 128)
        for k in range(8):
            tile = jnp.where(up_half, xhi_ref[k, :, at], xlo_ref[k, :, at])
            place(k, foot, at, zero_rows(tile))
        for r in range(0, rows, 8):
            scale[r : r + 8, at] = ones
        scale[foot, at] = row_scale
        return carry

    lax.fori_loop(0, cols // 128, halo_rows, 0)
    for k in range(8):
        for r in range(0, rows, 8):
            tile = jnp.where(left_half, yhi_ref[k, r : r + 8, :], ylo_ref[k, r : r + 8, :])
            place(k, pl.ds(r, 8), tail, zero_cols(tile))
        tile = jnp.where(
            up_half,
            jnp.where(left_half, corner_ref[3, k], corner_ref[2, k]),
            jnp.where(left_half, corner_ref[1, k], corner_ref[0, k]),
        )
        place(k, foot, tail, zero_cols(zero_rows(tile)))
    for r in range(0, rows, 8):
        scale[r : r + 8, tail] = col_scale
    scale[foot, tail] = zero_cols(row_scale)

    def own_cells(t, carry):
        at = pl.ds(pl.multiple_of(t * 128, 128), 128)
        drag[0:rows, at] = drag_ref[:, at]
        buoy[0:rows, at] = wetness(wet_ref[:, at].astype(jnp.float32))
        e = elem_ref[:, at]
        n = node_ref[:, at]
        surface_cols = 128 * (last_y + 1)
        er = e // surface_cols
        lx = er - 2 * at_x + 1
        ly = (e - er * surface_cols) - 128 * at_y + 1
        inside = (ly >= 1) & (ly <= 128)
        a = jnp.where(inside, 2 * n + (lx & 1), 50)
        b = jnp.where(
            inside,
            (lx >> 1) * 128 + ly - 1,
            jnp.where(ly == 0, 0, 128) + 4 * n + lx,
        )
        row_slot[:, at] = a.astype(jnp.float32)
        col_slot[:, at] = b.astype(jnp.float32)
        return carry

    lax.fori_loop(0, cols // 128, own_cells, 0)
    own_in.wait()

    lanes = lax.broadcasted_iota(jnp.int32, (tall, 128), 1)
    first_lane = lanes == 0
    last_lane = lanes == 127
    tiles = wide // 128

    def press(f0, f1, b):
        return b * (f0 + f1), upper_gravity * density_ratio * f0 + upper_gravity * f1

    def step(s, carry):
        now = s % 2
        later = 1 - now

        def tile_step(t, carry):
            at = pl.ds(pl.multiple_of(t * 128, 128), 128)
            t_hi = jnp.where(t == tiles - 1, 0, t + 1)
            t_lo = jnp.where(t == 0, tiles - 1, t - 1)
            at_hi = pl.ds(pl.multiple_of(t_hi * 128, 128), 128)
            at_lo = pl.ds(pl.multiple_of(t_lo * 128, 128), 128)
            f = [ext[now, k, :, at] for k in range(6)]
            b = buoy[:, at]
            one, two = press(f[0], f[1], b)
            sums = [None] * 6

            def add(k, value):
                sums[k] = value if sums[k] is None else sums[k] + value

            for ahead in (True, False):
                by = tall - 1 if ahead else 1
                def rolled(x):
                    return pltpu.roll(x, by, 0)
                sg = -1.0 if ahead else 1.0
                def mix(x, y):
                    return x - y if ahead else x + y
                add(0, rolled(mix(f[0], f[2])))
                add(1, rolled(mix(f[1], f[4])))
                add(2, rolled(mix(f[2], one)))
                add(3, rolled(f[3]))
                add(4, rolled(mix(f[4], two)))
                add(5, rolled(f[5]))
            for ahead in (True, False):
                by = 127 if ahead else 1
                edge = first_lane if ahead else last_lane
                other = at_hi if ahead else at_lo
                g = [jnp.where(edge, ext[now, k, :, other], f[k]) for k in range(6)]
                gb = jnp.where(edge, buoy[:, other], b)
                g_one, g_two = press(g[0], g[1], gb)
                def rolled(x):
                    return pltpu.roll(x, by, 1)
                def mix(x, y):
                    return x - y if ahead else x + y
                add(0, rolled(mix(g[0], g[3])))
                add(1, rolled(mix(g[1], g[5])))
                add(2, rolled(g[2]))
                add(3, rolled(mix(g[3], g_one)))
                add(4, rolled(g[4]))
                add(5, rolled(mix(g[5], g_two)))
            speed = jnp.sqrt(f[2] * f[2] + f[3] * f[3] + speed_floor)
            rub = 2.0 * drag[:, at] * speed
            k = scale[:, at]
            ext[later, 0, :, at] = k * (f[0] + sums[0])
            ext[later, 1, :, at] = k * (f[1] + sums[1])
            ext[later, 2, :, at] = k * (sums[2] + f[4] - rub * f[2])
            ext[later, 3, :, at] = k * (sums[3] + f[5] - rub * f[3])
            ext[later, 4, :, at] = k * (sums[4] + f[2])
            ext[later, 5, :, at] = k * (sums[5] + f[3])
            return carry

        return lax.fori_loop(0, tiles, tile_step, carry)

    lax.fori_loop(0, FLOW_STEPS, step, 0)
    own_out = pltpu.make_async_copy(ext.at[0, :, 0:rows, 0:cols], out_any, sems.at[1])
    own_out.start()

    def pull(t, carry):
        at = pl.ds(pl.multiple_of(t * 128, 128), 128)
        f = [ext[0, k, 0:rows, at] for k in range(4)]
        rub = load_factor * drag[0:rows, at] * jnp.sqrt(f[2] * f[2] + f[3] * f[3] + speed_floor)
        tract[0, :, at] = rub * f[2]
        tract[1, :, at] = rub * f[3]
        tract[2, :, at] = -load_factor * (buoy[0:rows, at] * (f[0] + f[1]))
        return carry

    lax.fori_loop(0, cols // 128, pull, 0)

    table_ref[...] = jnp.zeros_like(table_ref)
    count = lax.broadcasted_iota(jnp.int32, (16, cols), 0).astype(jnp.float32).astype(jnp.bfloat16)

    def spread(r, carry):
        line = pl.ds(r, 1)

        def wide16(x):
            return jnp.broadcast_to(x, (16, cols)).astype(jnp.bfloat16)

        parts = []
        for k in range(3):
            value = tract[k, line, :]
            high = value.astype(jnp.bfloat16).astype(jnp.float32)
            parts.append(wide16(value))
            parts.append(wide16(value - high))
        a = wide16(row_slot[line, :])
        b = wide16(col_slot[line, :])
        zero = jnp.zeros((16, cols), jnp.bfloat16)
        one = jnp.ones((16, cols), jnp.bfloat16)
        hits = [a == count + jnp.bfloat16(16 * m) for m in range(4)]
        left = jnp.concatenate([jnp.where(h, p, zero) for p in parts for h in hits], axis=0)
        right = jnp.concatenate(
            [jnp.where(b == count + jnp.bfloat16(16 * m), one, zero) for m in range(16)], axis=0
        )
        got = lax.dot_general(
            left, right, (((1,), (1,)), ((), ())), preferred_element_type=jnp.float32
        )
        table_ref[...] += got
        return carry

    lax.fori_loop(0, rows, spread, 0)
    own_out.wait()


def flow_call(flow, drag, wet, elem, node, xlo, xhi, ylo, yhi, corner):
    rows, cols = drag.shape
    tall, wide = rows + 8, cols + 128
    vmem = pl.BlockSpec(memory_space=pltpu.VMEM)
    hbm = pl.BlockSpec(memory_space=pl.ANY)
    return pl.pallas_call(
        flow_body,
        out_shape=(
            jax.ShapeDtypeStruct((6, rows, cols), jnp.float32),
            jax.ShapeDtypeStruct((384, 256), jnp.float32),
        ),
        in_specs=[vmem] * 4 + [hbm] + [vmem] * 5,
        out_specs=(hbm, vmem),
        scratch_shapes=[
            pltpu.VMEM((2, 6, tall, wide), jnp.float32),
            pltpu.VMEM((tall, wide), jnp.float32),
            pltpu.VMEM((tall, wide), jnp.float32),
            pltpu.VMEM((tall, wide), jnp.float32),
            pltpu.VMEM((3, rows, cols), jnp.float32),
            pltpu.VMEM((rows, cols), jnp.float32),
            pltpu.VMEM((rows, cols), jnp.float32),
            pltpu.SemaphoreType.DMA((2,)),
        ],
        compiler_params=pltpu.CompilerParams(vmem_limit_bytes=48 * 2**20),
    )(drag, wet, elem, node, flow, xlo, xhi, ylo, yhi, corner)


def weights_cube():
    cube = (
        gll_weights.reshape(5, 1, 1) * gll_weights.reshape(1, 5, 1) * gll_weights.reshape(1, 1, 5)
    )
    return jnp.asarray(cube.reshape(5, 5, 5, 1, 1, 1), jnp.float32)


def internal_force(values, lame_first, shear_modulus):
    highest = lax.Precision.HIGHEST
    table = jnp.asarray(derivative_table(), jnp.float32)
    weights_3d = weights_cube()
    gradients = [
        jnp.einsum("pa,iabczxy->ipbczxy", table, values, precision=highest),
        jnp.einsum("pb,iabczxy->iapczxy", table, values, precision=highest),
        jnp.einsum("pc,iabczxy->iabpzxy", table, values, precision=highest),
    ]
    divergence = gradients[0][0] + gradients[1][1] + gradients[2][2]
    forces = []
    for i in range(3):
        weighted = []
        for j in range(3):
            stress = shear_modulus * (gradients[j][i] + gradients[i][j])
            if i == j:
                stress = stress + lame_first * divergence
            weighted.append(weights_3d * stress)
        pulled = jnp.einsum("pa,pbczxy->abczxy", table, weighted[0], precision=highest)
        pulled = pulled + jnp.einsum("pb,apczxy->abczxy", table, weighted[1], precision=highest)
        pulled = pulled + jnp.einsum("pc,abpzxy->abczxy", table, weighted[2], precision=highest)
        forces.append(-pulled)
    return jnp.stack(forces)


def assemble(values):
    boundary = jnp.stack([values[:, 0, :, :, :, 0, :], values[:, 4, :, :, :, -1, :]])
    summed = values[:, 4, :, :, :, :-1, :] + values[:, 0, :, :, :, 1:, :]
    values = values.at[:, 4, :, :, :, :-1, :].set(summed).at[:, 0, :, :, :, 1:, :].set(summed)
    beyond = extended(boundary, (("gx", 0),), 1)
    values = values.at[:, 0, :, :, :, 0, :].add(beyond[0]).at[:, 4, :, :, :, -1, :].add(beyond[3])
    boundary = jnp.stack([values[:, :, 0, :, :, :, 0], values[:, :, 4, :, :, :, -1]])
    summed = values[:, :, 4, :, :, :, :-1] + values[:, :, 0, :, :, :, 1:]
    values = values.at[:, :, 4, :, :, :, :-1].set(summed).at[:, :, 0, :, :, :, 1:].set(summed)
    beyond = extended(boundary, (("gy", 0),), 1)
    values = values.at[:, :, 0, :, :, :, 0].add(beyond[0]).at[:, :, 4, :, :, :, -1].add(beyond[3])
    summed = values[:, :, :, 4, :-1] + values[:, :, :, 0, 1:]
    values = values.at[:, :, :, 4, :-1].set(summed).at[:, :, :, 0, 1:].set(summed)
    return values


def per_device(
    flow_state,
    drag_coefficient,
    wet_mask,
    target_elem,
    target_node,
    displacement,
    previous,
    density,
    lame_first,
    shear_modulus,
):
    stacked = jnp.concatenate(
        [flow_state, drag_coefficient[None], wet_mask.astype(jnp.float32)[None]], axis=0
    )
    ring_x, ring_y = lax.axis_size("gx"), lax.axis_size("gy")

    def moved(x, axis, count, by):
        return lax.ppermute(x, axis, [(i, (i + by) % count) for i in range(count)])

    x_lo = moved(stacked[:, -8:, :], "gx", ring_x, 1)
    x_hi = moved(stacked[:, :8, :], "gx", ring_x, -1)
    y_lo = moved(stacked[:, :, -128:], "gy", ring_y, 1)
    y_hi = moved(stacked[:, :, :128], "gy", ring_y, -1)
    corner_lo = moved(jnp.stack([x_lo[:, :, -128:], x_hi[:, :, -128:]]), "gy", ring_y, 1)
    corner_hi = moved(jnp.stack([x_lo[:, :, :128], x_hi[:, :, :128]]), "gy", ring_y, -1)
    corner = jnp.stack([corner_lo[0], corner_hi[0], corner_lo[1], corner_hi[1]])
    fields, slots = flow_call(
        flow_state, drag_coefficient, wet_mask, target_elem, target_node,
        x_lo, x_hi, y_lo, y_hi, corner,
    )
    block_rows = displacement.shape[5]
    slots = slots.reshape(3, 2, 64, 256).sum(axis=1)
    middle = slots[:, :50].reshape(3, 25, 2, 2, 128).transpose(0, 1, 3, 2, 4).reshape(3, 25, 4, 128)
    sides = slots[:, 50].reshape(3, 2, 128)[:, :, :100].reshape(3, 2, 25, 4)
    load_table = jnp.concatenate([sides[:, 0, :, :, None], middle, sides[:, 1, :, :, None]], axis=3)
    beyond = extended(load_table, (("gx", 2), ("gy", 3)), 1)
    own_loads = load_table[:, :, 1:-1, 1:-1]
    own_loads = own_loads.at[:, :, 0, :].add(beyond[:, :, 0, 2:-2])
    own_loads = own_loads.at[:, :, -1, :].add(beyond[:, :, -1, 2:-2])
    own_loads = own_loads.at[:, :, :, 0].add(beyond[:, :, 2:-2, 0])
    own_loads = own_loads.at[:, :, :, -1].add(beyond[:, :, 2:-2, -1])
    own_loads = own_loads.at[:, :, 0, 0].add(beyond[:, :, 0, 0])
    own_loads = own_loads.at[:, :, 0, -1].add(beyond[:, :, 0, -1])
    own_loads = own_loads.at[:, :, -1, 0].add(beyond[:, :, -1, 0])
    own_loads = own_loads.at[:, :, -1, -1].add(beyond[:, :, -1, -1])
    surface_load = own_loads.reshape(3, 5, 5, block_rows, displacement.shape[6])
    masses = assemble(density[None, None, None, None] * weights_cube()[None])
    current = displacement
    for counter in range(SOLID_STEPS):
        force = internal_force(current, lame_first, shear_modulus)
        force = force.at[:, :, :, 0, 0].add(surface_load)
        acceleration = assemble(force) / masses
        advanced = 2.0 * current - previous + solid_dt * solid_dt * acceleration
        previous = current
        current = advanced
    return (fields, current, previous)


def solution(mesh):
    return jax.shard_map(
        per_device,
        mesh=mesh,
        in_specs=(
            P(None, "gx", "gy"),
            P("gx", "gy"),
            P("gx", "gy"),
            P("gx", "gy"),
            P("gx", "gy"),
            P(None, None, None, None, None, "gx", "gy"),
            P(None, None, None, None, None, "gx", "gy"),
            P(None, "gx", "gy"),
            P(None, "gx", "gy"),
            P(None, "gx", "gy"),
        ),
        out_specs=(
            P(None, "gx", "gy"),
            P(None, None, None, None, None, "gx", "gy"),
            P(None, None, None, None, None, "gx", "gy"),
        ),
        check_vma=False,
    )
```

```python
import jax
import jax.numpy as jnp
import numpy as np
from jax import lax
from jax.experimental import pallas as pl
from jax.experimental.pallas import tpu as pltpu
from jax.sharding import PartitionSpec as P

FLOW_STEPS = 4
SOLID_STEPS = 2


gll_points = np.array([-1.0, -np.sqrt(3.0 / 7.0), 0.0, np.sqrt(3.0 / 7.0), 1.0])
gll_weights = np.array([0.1, 49.0 / 90.0, 32.0 / 45.0, 49.0 / 90.0, 0.1])
flow_dt = 0.4
diffusion = 0.2
coupling = 0.5
upper_gravity = 0.8
density_ratio = 0.7
speed_floor = 0.0001
load_factor = 4.0
solid_dt = 0.04


def legendre_four(x):
    return (35.0 * x**4 - 30.0 * x**2 + 3.0) / 8.0


def derivative_table():
    result = np.zeros((5, 5))
    for i in range(5):
        for j in range(5):
            if i != j:
                result[i, j] = (
                    legendre_four(gll_points[i])
                    / legendre_four(gll_points[j])
                    / (gll_points[i] - gll_points[j])
                )
    result[0, 0] = -5.0
    result[4, 4] = 5.0
    return result


def flow_body(
    drag_ref, wet_ref, elem_ref, node_ref, flow_any,
    *refs,
):
    got = (refs[0:5], refs[5:10], refs[10:15])
    out_any, own_ref, beyond_ref, sides_ref = refs[15:19]
    ext, drag, buoy, scale, tract, row_slot, col_slot, table_ref, sems = refs[19:]
    rows, cols = drag_ref.shape
    wide = cols + 128
    tall = rows + 8
    at_x, at_y = lax.axis_index("gx"), lax.axis_index("gy")
    last_x, last_y = lax.axis_size("gx") - 1, lax.axis_size("gy") - 1
    own_in = pltpu.make_async_copy(flow_any, ext.at[0, :, 0:rows, 0:cols], sems.at[0])
    own_in.start()

    def wetness(x):
        return 1.0 - 0.6 * x

    sub = lax.broadcasted_iota(jnp.int32, (8, 128), 0)
    lane = lax.broadcasted_iota(jnp.int32, (8, 128), 1)
    up_half = sub < 4
    left_half = lane < 64

    def zero_rows(tile):
        tile = jnp.where(up_half & (at_x == last_x), 0.0, tile)
        return jnp.where(jnp.logical_not(up_half) & (at_x == 0), 0.0, tile)

    def zero_cols(tile):
        tile = jnp.where(left_half & (at_y == last_y), 0.0, tile)
        return jnp.where(jnp.logical_not(left_half) & (at_y == 0), 0.0, tile)

    def received(k, n, *at):
        if k < 6:
            return got[0][n][(k, *at)]
        tile = got[k - 5][n][at]
        return tile if k == 6 else tile.astype(jnp.float32)

    def place(k, r, c, tile):
        if k < 6:
            ext[0, k, r, c] = tile
        elif k == 6:
            drag[r, c] = tile
        else:
            buoy[r, c] = wetness(tile)

    tail = pl.ds(cols, 128)
    foot = pl.ds(rows, 8)
    ones = jnp.full((8, 128), 0.2, jnp.float32)
    row_scale = zero_rows(ones)
    col_scale = zero_cols(ones)

    def halo_rows(t, carry):
        at = pl.ds(pl.multiple_of(t * 128, 128), 128)
        for k in range(8):
            place(k, foot, at, zero_rows(received(k, 0, slice(None), at)))
        for r in range(0, rows, 8):
            scale[r : r + 8, at] = ones
        scale[foot, at] = row_scale
        return carry

    lax.fori_loop(0, cols // 128, halo_rows, 0)
    for k in range(8):
        for r in range(0, rows, 8):
            at = (slice(r, r + 8), slice(None))
            tile = jnp.where(left_half, received(k, 2, *at), received(k, 1, *at))
            place(k, pl.ds(r, 8), tail, zero_cols(tile))
        at = (slice(None), slice(None))
        tile = jnp.where(left_half, received(k, 4, *at), received(k, 3, *at))
        place(k, foot, tail, zero_cols(zero_rows(tile)))
    for r in range(0, rows, 8):
        scale[r : r + 8, tail] = col_scale
    scale[foot, tail] = zero_cols(row_scale)

    def own_cells(t, carry):
        at = pl.ds(pl.multiple_of(t * 128, 128), 128)
        drag[0:rows, at] = drag_ref[:, at]
        buoy[0:rows, at] = wetness(wet_ref[:, at].astype(jnp.float32))
        e = elem_ref[:, at]
        n = node_ref[:, at]
        surface_cols = 128 * (last_y + 1)
        er = e // surface_cols
        lx = er - 2 * at_x + 1
        ly = (e - er * surface_cols) - 128 * at_y + 1
        inside = (ly >= 1) & (ly <= 128)
        own_row = (lx == 1) | (lx == 2)
        half = jnp.where(own_row, 0, 1)
        line = 2 * n + jnp.where(lx >= 2, 1, 0)
        a = jnp.where(inside, line, 50)
        b = jnp.where(
            inside,
            half * 128 + ly - 1,
            jnp.where(ly == 0, 0, 128) + 64 * half + line,
        )
        row_slot[:, at] = a.astype(jnp.float32)
        col_slot[:, at] = b.astype(jnp.float32)
        return carry

    lax.fori_loop(0, cols // 128, own_cells, 0)
    own_in.wait()

    lanes = lax.broadcasted_iota(jnp.int32, (tall, 128), 1)
    first_lane = lanes == 0
    last_lane = lanes == 127
    tiles = wide // 128

    def press(f0, f1, b):
        return b * (f0 + f1), upper_gravity * density_ratio * f0 + upper_gravity * f1

    def step(s, carry):
        now = s % 2
        later = 1 - now

        def tile_step(t, carry):
            at = pl.ds(pl.multiple_of(t * 128, 128), 128)
            t_hi = jnp.where(t == tiles - 1, 0, t + 1)
            t_lo = jnp.where(t == 0, tiles - 1, t - 1)
            at_hi = pl.ds(pl.multiple_of(t_hi * 128, 128), 128)
            at_lo = pl.ds(pl.multiple_of(t_lo * 128, 128), 128)
            f = [ext[now, k, :, at] for k in range(6)]
            b = buoy[:, at]
            one, two = press(f[0], f[1], b)
            sums = [None] * 6

            def add(k, value):
                sums[k] = value if sums[k] is None else sums[k] + value

            for ahead in (True, False):
                by = tall - 1 if ahead else 1
                def rolled(x):
                    return pltpu.roll(x, by, 0)
                sg = -1.0 if ahead else 1.0
                def mix(x, y):
                    return x - y if ahead else x + y
                add(0, rolled(mix(f[0], f[2])))
                add(1, rolled(mix(f[1], f[4])))
                add(2, rolled(mix(f[2], one)))
                add(3, rolled(f[3]))
                add(4, rolled(mix(f[4], two)))
                add(5, rolled(f[5]))
            for ahead in (True, False):
                by = 127 if ahead else 1
                edge = first_lane if ahead else last_lane
                other = at_hi if ahead else at_lo
                g = [jnp.where(edge, ext[now, k, :, other], f[k]) for k in range(6)]
                gb = jnp.where(edge, buoy[:, other], b)
                g_one, g_two = press(g[0], g[1], gb)
                def rolled(x):
                    return pltpu.roll(x, by, 1)
                def mix(x, y):
                    return x - y if ahead else x + y
                add(0, rolled(mix(g[0], g[3])))
                add(1, rolled(mix(g[1], g[5])))
                add(2, rolled(g[2]))
                add(3, rolled(mix(g[3], g_one)))
                add(4, rolled(g[4]))
                add(5, rolled(mix(g[5], g_two)))
            speed = jnp.sqrt(f[2] * f[2] + f[3] * f[3] + speed_floor)
            rub = 2.0 * drag[:, at] * speed
            k = scale[:, at]
            ext[later, 0, :, at] = k * (f[0] + sums[0])
            ext[later, 1, :, at] = k * (f[1] + sums[1])
            ext[later, 2, :, at] = k * (sums[2] + f[4] - rub * f[2])
            ext[later, 3, :, at] = k * (sums[3] + f[5] - rub * f[3])
            ext[later, 4, :, at] = k * (sums[4] + f[2])
            ext[later, 5, :, at] = k * (sums[5] + f[3])
            return carry

        return lax.fori_loop(0, tiles, tile_step, carry)

    lax.fori_loop(0, FLOW_STEPS, step, 0)
    own_out = pltpu.make_async_copy(ext.at[0, :, 0:rows, 0:cols], out_any, sems.at[1])
    own_out.start()

    def pull(t, carry):
        at = pl.ds(pl.multiple_of(t * 128, 128), 128)
        f = [ext[0, k, 0:rows, at] for k in range(4)]
        rub = load_factor * drag[0:rows, at] * jnp.sqrt(f[2] * f[2] + f[3] * f[3] + speed_floor)
        tract[0, :, at] = rub * f[2]
        tract[1, :, at] = rub * f[3]
        tract[2, :, at] = -load_factor * (buoy[0:rows, at] * (f[0] + f[1]))
        return carry

    lax.fori_loop(0, cols // 128, pull, 0)

    table_ref[...] = jnp.zeros_like(table_ref)
    count = lax.broadcasted_iota(jnp.int32, (16, cols), 0).astype(jnp.float32).astype(jnp.bfloat16)

    def spread(r, carry):
        line = pl.ds(r, 1)

        def wide16(x):
            return jnp.broadcast_to(x, (16, cols)).astype(jnp.bfloat16)

        parts = []
        for k in range(3):
            value = tract[k, line, :]
            high = value.astype(jnp.bfloat16).astype(jnp.float32)
            parts.append(wide16(value))
            parts.append(wide16(value - high))
        a = wide16(row_slot[line, :])
        b = wide16(col_slot[line, :])
        zero = jnp.zeros((16, cols), jnp.bfloat16)
        one = jnp.ones((16, cols), jnp.bfloat16)
        hits = [a == count + jnp.bfloat16(16 * m) for m in range(4)]
        left = jnp.concatenate([jnp.where(h, p, zero) for p in parts for h in hits], axis=0)
        right = jnp.concatenate(
            [jnp.where(b == count + jnp.bfloat16(16 * m), one, zero) for m in range(16)], axis=0
        )
        got = lax.dot_general(
            left, right, (((1,), (1,)), ((), ())), preferred_element_type=jnp.float32
        )
        table_ref[...] += got
        return carry

    lax.fori_loop(0, rows, spread, 0)
    table = [table_ref[128 * k : 128 * k + 64] + table_ref[128 * k + 64 : 128 * k + 128] for k in range(3)]
    load_parts(table, own_ref, beyond_ref, sides_ref)
    own_out.wait()


def flow_call(flow, drag, wet, elem, node, halos):
    rows, cols = drag.shape
    tall, wide = rows + 8, cols + 128
    vmem = pl.BlockSpec(memory_space=pltpu.VMEM)
    hbm = pl.BlockSpec(memory_space=pl.ANY)
    return pl.pallas_call(
        flow_body,
        out_shape=(shape(6, rows, cols), shape(3, 56, 128), shape(3, 56, 128), shape(8, 128)),
        in_specs=[vmem] * 4 + [hbm] + [vmem] * 15,
        out_specs=(hbm, vmem, vmem, vmem),
        scratch_shapes=[
            pltpu.VMEM((2, 6, tall, wide), jnp.float32),
            pltpu.VMEM((tall, wide), jnp.float32),
            pltpu.VMEM((tall, wide), jnp.float32),
            pltpu.VMEM((tall, wide), jnp.float32),
            pltpu.VMEM((3, rows, cols), jnp.float32),
            pltpu.VMEM((rows, cols), jnp.float32),
            pltpu.VMEM((rows, cols), jnp.float32),
            pltpu.VMEM((384, 256), jnp.float32),
            pltpu.SemaphoreType.DMA((2,)),
        ],
        compiler_params=pltpu.CompilerParams(vmem_limit_bytes=48 * 2**20),
    )(drag, wet, elem, node, flow, *halos)


def line(matrix, s):
    even = [s[0] + s[4], s[1] + s[3]]
    odd = [s[0] - s[4], s[1] - s[3]]
    out = [None] * 5
    for a in range(2):
        half_sum = [0.5 * (matrix[a, p] - matrix[a, 4 - p]) for p in range(2)]
        half_diff = [0.5 * (matrix[a, p] + matrix[a, 4 - p]) for p in range(2)]
        x = float(half_sum[0]) * odd[0] + float(half_sum[1]) * odd[1]
        y = float(half_diff[0]) * even[0] + float(half_diff[1]) * even[1] + float(matrix[a, 2]) * s[2]
        out[a] = x + y
        out[4 - a] = x - y
    out[2] = float(matrix[2, 0]) * odd[0] + float(matrix[2, 1]) * odd[1]
    return out


def lane_row():
    lane = lax.broadcasted_iota(jnp.int32, (4, 128), 1)
    row = lax.broadcasted_iota(jnp.int32, (4, 128), 0)
    return lane, row


def internal_local(u_ref, lame_ref, shear_ref, stress, force):
    table = derivative_table()

    def slope_x(m, carry):
        for i in range(3):
            lines = line(table, [u_ref[i * 125 + a * 25 + m] for a in range(5)])
            for a in range(5):
                stress[i * 125 + a * 25 + m] = lines[a]
        return carry

    lax.fori_loop(0, 25, slope_x, 0)

    def plane(a, carry):
        weight = jnp.where(
            (a == 0) | (a == 4),
            np.float32(gll_weights[0]),
            jnp.where(a == 2, np.float32(gll_weights[2]), np.float32(gll_weights[1])),
        )
        lame = lame_ref[...] * -weight
        shear = shear_ref[...] * -weight

        def at(i, b, c):
            return i * 125 + a * 25 + b * 5 + c

        slope_y, slope_z = [], []
        for i in range(3):
            u = [[u_ref[at(i, b, c)] for c in range(5)] for b in range(5)]
            along_y = [line(table, [u[b][c] for b in range(5)]) for c in range(5)]
            slope_y.append([[along_y[c][b] for c in range(5)] for b in range(5)])
            slope_z.append([line(table, u[b]) for b in range(5)])
        pull_y = [[[None] * 5 for b in range(5)] for i in range(3)]
        pull_z = [[[None] * 5 for b in range(5)] for i in range(3)]
        for b in range(5):
            for c in range(5):
                w = np.float32(gll_weights[b] * gll_weights[c])
                g = [[stress[at(i, b, c)], slope_y[i][b][c], slope_z[i][b][c]] for i in range(3)]
                mu = shear * w
                twice = mu + mu
                spread = (lame * w) * (g[0][0] + g[1][1] + g[2][2])
                s00 = spread + twice * g[0][0]
                s11 = spread + twice * g[1][1]
                s22 = spread + twice * g[2][2]
                s01 = mu * (g[0][1] + g[1][0])
                s02 = mu * (g[0][2] + g[2][0])
                s12 = mu * (g[1][2] + g[2][1])
                stress[at(0, b, c)] = s00
                stress[at(1, b, c)] = s01
                stress[at(2, b, c)] = s02
                for i, (s_y, s_z) in enumerate(((s01, s02), (s11, s12), (s12, s22))):
                    pull_y[i][b][c] = s_y
                    pull_z[i][b][c] = s_z
        for i in range(3):
            along_y = [line(table.T, [pull_y[i][b][c] for b in range(5)]) for c in range(5)]
            for b in range(5):
                along_z = line(table.T, pull_z[i][b])
                for c in range(5):
                    force[at(i, b, c)] = along_y[c][b] + along_z[c]
        return carry

    lax.fori_loop(0, 5, plane, 0)
    lane, row = lane_row()
    low_x = row % 2 == 0
    low_z = row < 2

    def close_x(m, carry):
        for i in range(3):
            pulled = line(table.T, [stress[i * 125 + a * 25 + m] for a in range(5)])
            f = [force[i * 125 + a * 25 + m] + pulled[a] for a in range(5)]
            near = f[0] + jnp.where(low_x, 0.0, pltpu.roll(f[4], 1, 0))
            far = f[4] + jnp.where(low_x, pltpu.roll(f[0], 3, 0), 0.0)
            for a, value in enumerate((near, f[1], f[2], f[3], far)):
                force[i * 125 + a * 25 + m] = value
        return carry

    lax.fori_loop(0, 25, close_x, 0)

    def close_yz(ia, carry):
        base = ia * 25
        f = [[force[base + b * 5 + c] for c in range(5)] for b in range(5)]
        for c in range(5):
            near, far = f[0][c], f[4][c]
            f[0][c] = near + jnp.where(lane == 0, 0.0, pltpu.roll(far, 1, 1))
            f[4][c] = far + jnp.where(lane == 127, 0.0, pltpu.roll(near, 127, 1))
        for b in range(5):
            near, far = f[b][0], f[b][4]
            f[b][0] = near + jnp.where(low_z, 0.0, pltpu.roll(far, 2, 0))
            f[b][4] = far + jnp.where(low_z, pltpu.roll(near, 2, 0), 0.0)
        for b in range(5):
            for c in range(5):
                if b in (0, 4) or c in (0, 4):
                    force[base + b * 5 + c] = f[b][c]
        return carry

    lax.fori_loop(0, 15, close_yz, 0)


def pack_faces(force, face_x, face_y):
    lane, row = lane_row()
    low_x = row % 2 == 0

    def pack_x(m, carry):
        for i in range(3):
            face_x[i * 25 + m] = jnp.where(low_x, force[i * 125 + m], force[i * 125 + 100 + m])
        return carry

    lax.fori_loop(0, 25, pack_x, 0)
    ends = [jnp.zeros((4, 128), jnp.float32)] * 2
    for a in range(5):
        for i in range(3):
            for c in range(5):
                q = a * 15 + i * 5 + c
                n = i * 125 + a * 25 + c
                ends[0] = jnp.where(lane == q, pltpu.roll(force[n], q, 1), ends[0])
                ends[1] = jnp.where(lane == q, pltpu.roll(force[n + 20], q + 1, 1), ends[1])
    face_y[0] = ends[0]
    face_y[1] = ends[1]


def open_edges():
    at_x, at_y = lax.axis_index("gx"), lax.axis_index("gy")
    has = {-1: at_x > 0, 1: at_x < lax.axis_size("gx") - 1}
    has_y = {-1: at_y > 0, 1: at_y < lax.axis_size("gy") - 1}
    return has, has_y


def add_faces(force, got_x, got_y):
    has_x, has_y = open_edges()
    lane, row = lane_row()
    low_x = row % 2 == 0

    def add_x(m, carry):
        for i in range(3):
            low = jnp.where(low_x & has_x[-1], pltpu.roll(got_x[0][i * 25 + m], 3, 0), 0.0)
            high = jnp.where(low_x | jnp.logical_not(has_x[1]), 0.0, pltpu.roll(got_x[1][i * 25 + m], 1, 0))
            force[i * 125 + m] += low
            force[i * 125 + 100 + m] += high
        return carry

    lax.fori_loop(0, 25, add_x, 0)
    first, final = lane < 15, (lane >= 60) & (lane < 75)
    columns = []
    for side, end in ((-1, 1), (1, 0)):
        straight = got_y[0, side][end]
        low = pltpu.roll(pltpu.roll(got_y[-1, side][end], 68, 1), 3, 0)
        high = pltpu.roll(pltpu.roll(got_y[1, side][end], 60, 1), 1, 0)
        total = straight + jnp.where(first & low_x & has_x[-1], low, 0.0)
        total = total + jnp.where(final & jnp.logical_not(low_x) & has_x[1], high, 0.0)
        columns.append(jnp.where(has_y[side], total, 0.0))
    for a in range(5):
        for i in range(3):
            for c in range(5):
                q = a * 15 + i * 5 + c
                n = i * 125 + a * 25 + c
                force[n] += jnp.where(lane == 0, pltpu.roll(columns[0], (128 - q) % 128, 1), 0.0)
                force[n + 20] += jnp.where(lane == 127, pltpu.roll(columns[1], 127 - q, 1), 0.0)


def inverse_masses(density_ref, around, inverse):
    has_x, has_y = open_edges()
    lane, row = lane_row()
    low_x = row % 2 == 0
    low_z = row < 2

    def beside(mine, left, right):
        left = jnp.where(has_y[-1], left, 0.0)
        right = jnp.where(has_y[1], right, 0.0)
        before = jnp.where(lane == 0, pltpu.roll(left, 1, 1), pltpu.roll(mine, 1, 1))
        after = jnp.where(lane == 127, pltpu.roll(right, 127, 1), pltpu.roll(mine, 127, 1))
        return mine + before, mine, mine + after

    mine = beside(density_ref[...], around[0, -1][...], around[0, 1][...])
    low = beside(around[-1, 0][...], around[-1, -1][...], around[-1, 1][...])
    high = beside(around[1, 0][...], around[1, -1][...], around[1, 1][...])
    for b in range(3):
        lo = jnp.where(has_x[-1], low[b], 0.0)
        hi = jnp.where(has_x[1], high[b], 0.0)
        before = mine[b] + jnp.where(low_x, pltpu.roll(lo, 3, 0), pltpu.roll(mine[b], 1, 0))
        after = mine[b] + jnp.where(low_x, pltpu.roll(mine[b], 3, 0), pltpu.roll(hi, 1, 0))
        for a, value in enumerate((before, mine[b], after)):
            top = value + jnp.where(low_z, 0.0, pltpu.roll(value, 2, 0))
            bottom = value + jnp.where(low_z, pltpu.roll(value, 2, 0), 0.0)
            for c, total in enumerate((top, value, bottom)):
                inverse[a * 9 + b * 3 + c] = (solid_dt * solid_dt) / total


def kind(node):
    return 0 if node == 0 else 2 if node == 4 else 1


def advance_solid(force, load, inverse, now_ref, before_ref, out_ref):
    def component(i, carry):
        for a in range(5):
            for b in range(5):
                for c in range(5):
                    n = a * 25 + b * 5 + c
                    f = force[i * 125 + n]
                    if c == 0:
                        f = f + load[i * 25 + a * 5 + b]
                    w = np.float32(1.0 / (gll_weights[a] * gll_weights[b] * gll_weights[c]))
                    step = (inverse[kind(a) * 9 + kind(b) * 3 + kind(c)] * w) * f
                    at = i * 125 + n
                    out_ref[at] = (now_ref[at] + now_ref[at] - before_ref[at]) + step
        return carry

    lax.fori_loop(0, 3, component, 0)


def load_grid():
    row = lax.broadcasted_iota(jnp.int32, (56, 128), 0)
    lane = lax.broadcasted_iota(jnp.int32, (56, 128), 1)
    return row, lane


def rows_up(x, by):
    return jnp.concatenate([x[by:], jnp.zeros((by, 128), jnp.float32)], axis=0)


def rows_down(x, by):
    return jnp.concatenate([jnp.zeros((by, 128), jnp.float32), x[:-by]], axis=0)


def masks_x():
    row, lane = load_grid()
    even = row % 2 == 0
    odd = row % 2 == 1
    return (row < 10) & even, (row < 10) & odd, (row >= 40) & (row < 50) & even, (row >= 40) & (row < 50) & odd


def masks_y():
    row, lane = load_grid()
    place = row % 10
    return (place < 2) & (row < 50), (place >= 8) & (row < 50), lane == 0, lane == 127


def join_x(x):
    near_even, near_odd, far_even, far_odd = masks_x()
    return (
        x
        + jnp.where(near_odd, pltpu.roll(rows_up(x, 40), 1, 0), 0.0)
        + jnp.where(far_even, pltpu.roll(rows_down(x, 40), 55, 0), 0.0)
    )


def join_x_wide(own, halo):
    near_even, near_odd, far_even, far_odd = masks_x()
    own_new = join_x(own)
    own_new = own_new + jnp.where(near_even, rows_up(halo, 40), 0.0)
    own_new = own_new + jnp.where(far_odd, rows_down(halo, 40), 0.0)
    halo_new = halo + jnp.where(far_even, rows_down(own, 40), 0.0)
    halo_new = halo_new + jnp.where(near_odd, rows_up(own, 40), 0.0)
    return own_new, halo_new


def join_y(x, sides):
    near, far, first, final = masks_y()
    before, after = pltpu.roll(x, 1, 1), pltpu.roll(x, 127, 1)
    fill_before = 0.0 if sides is None else pltpu.roll(sides, 1, 1)
    fill_after = 0.0 if sides is None else pltpu.roll(sides, 127, 1)
    out = x + jnp.where(near, rows_up(jnp.where(first, fill_before, before), 8), 0.0)
    out = out + jnp.where(far, rows_down(jnp.where(final, fill_after, after), 8), 0.0)
    if sides is None:
        return out
    new = sides + jnp.where(far & final, rows_down(after, 8), 0.0)
    new = new + jnp.where(near & first, rows_up(before, 8), 0.0)
    return out, new


def columns_from(tile):
    row, lane = load_grid()
    turned = jnp.concatenate([tile, jnp.zeros((120, 128), jnp.float32)], axis=0).T
    out = []
    for k in range(3):
        halves = []
        for h in range(2):
            part = turned[64 * h : 64 * h + 56]
            left = pltpu.roll(part, 127 - 2 * k, 1)
            right = pltpu.roll(part, (128 - 2 * k - 1) % 128, 1)
            value = jnp.where(lane == 127, left, jnp.where(lane == 0, right, 0.0))
            halves.append(jnp.where(row < 50, value, 0.0))
        out.append(halves)
    return out


def columns_to(columns):
    lane = lax.broadcasted_iota(jnp.int32, (128, 128), 1)
    total = jnp.zeros((128, 128), jnp.float32)
    for k in range(3):
        pad = jnp.zeros((8, 128), jnp.float32)
        x = jnp.concatenate([columns[k][0], pad, columns[k][1], pad], axis=0)
        total = jnp.where(lane == 2 * k, pltpu.roll(x, 2 * k + 1, 1), total)
        total = jnp.where(lane == 2 * k + 1, pltpu.roll(x, 2 * k + 1, 1), total)
    return total.T[:8]


def load_parts(table, own_ref, beyond_ref, sides_ref):
    row, lane = load_grid()
    line_of = lax.broadcasted_iota(jnp.int32, (8, 128), 0)
    raw = jnp.zeros((8, 128), jnp.float32)
    for k in range(3):
        for side in range(2):
            last = jnp.broadcast_to(table[k][50:51, 128 * side : 128 * side + 128], (8, 128))
            raw = jnp.where(line_of == 2 * k + side, last, raw)
    columns = columns_from(raw)
    new_columns = []
    for k in range(3):
        own = jnp.where(row < 50, table[k][:56, :128], 0.0)
        halo = jnp.where(row < 50, table[k][:56, 128:], 0.0)
        own, halo = join_x_wide(own, halo)
        sides = join_x_wide(columns[k][0], columns[k][1])
        own, side_own = join_y(own, sides[0])
        halo, side_halo = join_y(halo, sides[1])
        own_ref[k] = own
        beyond_ref[k] = halo
        new_columns.append((side_own, side_halo))
    sides_ref[...] = columns_to(new_columns)


def load_total(own_ref, got_x, got_y, load):
    has_x, has_y = open_edges()
    row, lane = load_grid()
    even = row % 2 == 0
    tile_lane = lax.broadcasted_iota(jnp.int32, (8, 128), 1)
    tile_row = lax.broadcasted_iota(jnp.int32, (8, 128), 0)
    ends = []
    for side in (-1, 1):
        low = jnp.where(has_x[-1], pltpu.roll(got_y[-1, side][...], 127, 1), 0.0)
        high = jnp.where(has_x[1], pltpu.roll(got_y[1, side][...], 1, 1), 0.0)
        tile = jnp.where(tile_lane < 64, got_y[0, side][...], jnp.where(tile_lane % 2 == 0, low, high))
        ends.append(jnp.where(has_y[side], tile, 0.0))
    columns = columns_from(jnp.where(tile_row % 2 == 0, ends[1], ends[0]))
    for k in range(3):
        low = jnp.where(has_x[-1], pltpu.roll(got_x[0][k], 55, 0), 0.0)
        high = jnp.where(has_x[1], pltpu.roll(got_x[1][k], 1, 0), 0.0)
        rows = jnp.where(even, low, high) + join_y(columns[k][1], None)
        total = own_ref[k] + join_x(jnp.where(row < 50, rows, 0.0)) + join_y(columns[k][0], None)
        for n in range(25):
            load[k * 25 + n] = jnp.concatenate(
                [total[2 * n : 2 * n + 2], jnp.zeros((2, 128), jnp.float32)], axis=0
            )


AROUND = [(-1, 0), (1, 0), (0, -1), (0, 1), (-1, -1), (-1, 1), (1, -1), (1, 1)]
ASIDE = AROUND[2:]


def swap(collective_id, operands, outs, messages):
    count = len(messages)

    def body(*refs):
        ins, out_refs = refs[: len(operands)], refs[len(operands) : len(operands) + len(outs)]
        sent, come = refs[len(operands) + len(outs) :]
        at_x, at_y = lax.axis_index("gx"), lax.axis_index("gy")
        size_x, size_y = lax.axis_size("gx"), lax.axis_size("gy")

        def device(move):
            return ((at_x + move[0] + size_x) % size_x, (at_y + move[1] + size_y) % size_y)

        barrier = pltpu.get_barrier_semaphore()
        for move in AROUND:
            pl.semaphore_signal(barrier, inc=1, device_id=device(move), device_id_type=pl.DeviceIdType.MESH)
        pl.semaphore_wait(barrier, len(AROUND))
        copies = []
        for n, (source, source_index, target, target_index, move) in enumerate(messages):
            copies.append(
                pltpu.make_async_remote_copy(
                    src_ref=ins[source].at[source_index] if source_index is not None else ins[source],
                    dst_ref=out_refs[target].at[target_index] if target_index is not None else out_refs[target],
                    send_sem=sent.at[n],
                    recv_sem=come.at[n],
                    device_id=device(move),
                    device_id_type=pl.DeviceIdType.MESH,
                )
            )
            copies[-1].start()
        for copy in copies:
            copy.wait()

    return pl.pallas_call(
        body,
        out_shape=tuple(outs),
        in_specs=[pl.BlockSpec(memory_space=pl.ANY)] * len(operands),
        out_specs=tuple([pl.BlockSpec(memory_space=pl.ANY)] * len(outs)),
        scratch_shapes=[pltpu.SemaphoreType.DMA((count,)), pltpu.SemaphoreType.DMA((count,))],
        compiler_params=pltpu.CompilerParams(collective_id=collective_id, has_side_effects=True),
    )(*operands)


def shape(*dims, kind=jnp.float32):
    return jax.ShapeDtypeStruct(dims, kind)


def local(body, operands, outs, scratch):
    vmem = pl.BlockSpec(memory_space=pltpu.VMEM)
    return pl.pallas_call(
        body,
        out_shape=tuple(outs),
        in_specs=[vmem] * len(operands),
        out_specs=tuple([vmem] * len(outs)),
        scratch_shapes=[pltpu.VMEM(dims, jnp.float32) for dims in scratch],
        compiler_params=pltpu.CompilerParams(vmem_limit_bytes=48 * 2**20),
    )(*operands)


def first_body(u_ref, lame_ref, shear_ref, density_ref, *refs):
    around = {move: refs[n] for n, move in enumerate(AROUND)}
    force, face_x, face_y, inverse, stress = refs[8:]
    inverse_masses(density_ref, around, inverse)
    internal_local(u_ref, lame_ref, shear_ref, stress, force)
    pack_faces(force, face_x, face_y)


def middle_body(force0, u_ref, before_ref, lame_ref, shear_ref, inverse, own_ref, *refs):
    face_got_x, load_got_x = refs[0:2], refs[2:4]
    face_got_y = {move: refs[4 + n] for n, move in enumerate(ASIDE)}
    load_got_y = {move: refs[10 + n] for n, move in enumerate(ASIDE)}
    u_next, force, face_x, face_y, load, stress = refs[16:]
    load_total(own_ref, load_got_x, load_got_y, load)
    force[...] = force0[...]
    add_faces(force, face_got_x, face_got_y)
    advance_solid(force, load, inverse, u_ref, before_ref, u_next)
    internal_local(u_next, lame_ref, shear_ref, stress, force)
    pack_faces(force, face_x, face_y)


def last_body(force1, u_ref, before_ref, inverse, load, *refs):
    face_got_x = refs[0:2]
    face_got_y = {move: refs[2 + n] for n, move in enumerate(ASIDE)}
    u_next, force = refs[8:]
    force[...] = force1[...]
    add_faces(force, face_got_x, face_got_y)
    advance_solid(force, load, inverse, u_ref, before_ref, u_next)


def per_device(
    flow_state,
    drag_coefficient,
    wet_mask,
    target_elem,
    target_node,
    displacement,
    previous,
    density,
    lame_first,
    shear_modulus,
):
    rows, cols = drag_coefficient.shape
    u = displacement.reshape(375, 4, 128)
    before = previous.reshape(375, 4, 128)
    density, lame, shear = (x.reshape(4, 128) for x in (density, lame_first, shear_modulus))
    edge_rows = {-1: pl.ds(0, 4), 1: pl.ds(rows - 4, 4)}
    edge_cols = {-1: pl.ds(0, 128), 1: pl.ds(cols - 128, 128)}
    place_rows = {-1: pl.ds(0, 4), 1: pl.ds(4, 4)}
    outs, messages = [], []
    for source, lead in ((0, (6,)), (1, ()), (2, ())):
        kind_of = jnp.int32 if source == 2 else jnp.float32
        every = (slice(None),) * len(lead)
        base = len(outs)
        outs += [shape(*lead, 8, cols, kind=kind_of)]
        outs += [shape(*lead, rows, 128, kind=kind_of)] * 2
        outs += [shape(*lead, 8, 128, kind=kind_of)] * 2
        for dx, dy in AROUND:
            row_in = edge_rows.get(dx, pl.ds(0, rows))
            row_out = place_rows.get(dx, pl.ds(0, rows))
            col_in = edge_cols.get(dy, pl.ds(0, cols))
            where = 0 if dy == 0 else (1 if dx == 0 else 3) + (0 if dy == 1 else 1)
            messages.append(
                (source, every + (row_in, col_in), base + where,
                 every + (row_out, pl.ds(0, cols if dy == 0 else 128)), (dx, dy))
            )
    base = len(outs)
    outs += [shape(4, 128)] * 8
    for n, (dx, dy) in enumerate(AROUND):
        messages.append((3, None, base + AROUND.index((-dx, -dy)), None, (dx, dy)))
    got = swap(1, [flow_state, drag_coefficient, wet_mask, density], outs, messages)

    full = (375, 4, 128)
    force, face_x, face_y, inverse = local(
        first_body,
        [u, lame, shear, density, *got[15:]],
        [shape(*full), shape(75, 4, 128), shape(2, 4, 128), shape(27, 4, 128)],
        [full],
    )
    fields, own, beyond, sides = flow_call(
        flow_state, drag_coefficient, wet_mask, target_elem, target_node, got[:15]
    )
    faces = [shape(75, 4, 128)] * 2
    face_messages = [(0, None, 1, None, (-1, 0)), (0, None, 0, None, (1, 0))]
    sent_loads = [(2, None, 3, None, (-1, 0)), (2, None, 2, None, (1, 0))]
    side_messages = [
        (1, None, 4 + ASIDE.index((-dx, -dy)), None, (dx, dy)) for dx, dy in ASIDE
    ] + [(3, None, 10 + ASIDE.index((-dx, -dy)), None, (dx, dy)) for dx, dy in ASIDE]
    got = swap(
        2,
        [face_x, face_y, beyond, sides],
        faces + [shape(3, 56, 128)] * 2 + [shape(2, 4, 128)] * 6 + [shape(8, 128)] * 6,
        face_messages + sent_loads + side_messages,
    )
    u_one, force, face_x, face_y, load = local(
        middle_body,
        [force, u, before, lame, shear, inverse, own, *got],
        [shape(*full), shape(*full), shape(75, 4, 128), shape(2, 4, 128), shape(75, 4, 128)],
        [full],
    )
    got = swap(
        3,
        [face_x, face_y],
        faces + [shape(2, 4, 128)] * 6,
        face_messages
        + [(1, None, 2 + ASIDE.index((-dx, -dy)), None, (dx, dy)) for dx, dy in ASIDE],
    )
    (u_two,) = local(
        last_body,
        [force, u_one, u, inverse, load, *got],
        [shape(*full)],
        [full],
    )
    return (fields, u_two.reshape(displacement.shape), u_one.reshape(displacement.shape))


def solution(mesh):
    return jax.shard_map(
        per_device,
        mesh=mesh,
        in_specs=(
            P(None, "gx", "gy"),
            P("gx", "gy"),
            P("gx", "gy"),
            P("gx", "gy"),
            P("gx", "gy"),
            P(None, None, None, None, None, "gx", "gy"),
            P(None, None, None, None, None, "gx", "gy"),
            P(None, "gx", "gy"),
            P(None, "gx", "gy"),
            P(None, "gx", "gy"),
        ),
        out_specs=(
            P(None, "gx", "gy"),
            P(None, None, None, None, None, "gx", "gy"),
            P(None, None, None, None, None, "gx", "gy"),
        ),
        check_vma=False,
    )
```

```python
import jax
import jax.numpy as jnp
import numpy as np
from jax import lax
from jax.experimental import pallas as pl
from jax.experimental.pallas import tpu as pltpu
from jax.sharding import PartitionSpec as P

FLOW_STEPS = 4
SOLID_STEPS = 2


gll_points = np.array([-1.0, -np.sqrt(3.0 / 7.0), 0.0, np.sqrt(3.0 / 7.0), 1.0])
gll_weights = np.array([0.1, 49.0 / 90.0, 32.0 / 45.0, 49.0 / 90.0, 0.1])
flow_dt = 0.4
diffusion = 0.2
coupling = 0.5
upper_gravity = 0.8
density_ratio = 0.7
speed_floor = 0.0001
load_factor = 4.0
solid_dt = 0.04


def legendre_four(x):
    return (35.0 * x**4 - 30.0 * x**2 + 3.0) / 8.0


def derivative_table():
    result = np.zeros((5, 5))
    for i in range(5):
        for j in range(5):
            if i != j:
                result[i, j] = (
                    legendre_four(gll_points[i])
                    / legendre_four(gll_points[j])
                    / (gll_points[i] - gll_points[j])
                )
    result[0, 0] = -5.0
    result[4, 4] = 5.0
    return result


def surface(
    drag_ref, wet_ref, elem_ref, node_ref, got, own_ref, beyond_ref, sides_ref,
    ext, drag, buoy, scale, tract, row_slot, col_slot, table_ref, store_fields,
):
    rows, cols = drag_ref.shape
    wide = cols + 128
    tall = rows + 8
    at_x, at_y = lax.axis_index("gx"), lax.axis_index("gy")
    last_x, last_y = lax.axis_size("gx") - 1, lax.axis_size("gy") - 1

    def wetness(x):
        return 1.0 - 0.6 * x

    sub = lax.broadcasted_iota(jnp.int32, (8, 128), 0)
    lane = lax.broadcasted_iota(jnp.int32, (8, 128), 1)
    up_half = sub < 4
    left_half = lane < 64

    def zero_rows(tile):
        tile = jnp.where(up_half & (at_x == last_x), 0.0, tile)
        return jnp.where(jnp.logical_not(up_half) & (at_x == 0), 0.0, tile)

    def zero_cols(tile):
        tile = jnp.where(left_half & (at_y == last_y), 0.0, tile)
        return jnp.where(jnp.logical_not(left_half) & (at_y == 0), 0.0, tile)

    def received(k, n, *at):
        if k < 6:
            return got[0][n][(k, *at)]
        tile = got[k - 5][n][at]
        return tile if k == 6 else tile.astype(jnp.float32)

    def place(k, r, c, tile):
        if k < 6:
            ext[0, k, r, c] = tile
        elif k == 6:
            drag[r, c] = tile
        else:
            buoy[r, c] = wetness(tile)

    tail = pl.ds(cols, 128)
    foot = pl.ds(rows, 8)
    ones = jnp.full((8, 128), 0.2, jnp.float32)
    row_scale = zero_rows(ones)
    col_scale = zero_cols(ones)

    def halo_rows(t, carry):
        at = pl.ds(pl.multiple_of(t * 128, 128), 128)
        for k in range(8):
            place(k, foot, at, zero_rows(received(k, 0, slice(None), at)))
        for r in range(0, rows, 8):
            scale[r : r + 8, at] = ones
        scale[foot, at] = row_scale
        return carry

    lax.fori_loop(0, cols // 128, halo_rows, 0)
    for k in range(8):
        for r in range(0, rows, 8):
            at = (slice(r, r + 8), slice(None))
            tile = jnp.where(left_half, received(k, 2, *at), received(k, 1, *at))
            place(k, pl.ds(r, 8), tail, zero_cols(tile))
        at = (slice(None), slice(None))
        tile = jnp.where(left_half, received(k, 4, *at), received(k, 3, *at))
        place(k, foot, tail, zero_cols(zero_rows(tile)))
    for r in range(0, rows, 8):
        scale[r : r + 8, tail] = col_scale
    scale[foot, tail] = zero_cols(row_scale)

    def own_cells(t, carry):
        at = pl.ds(pl.multiple_of(t * 128, 128), 128)
        drag[0:rows, at] = drag_ref[:, at]
        buoy[0:rows, at] = wetness(wet_ref[:, at].astype(jnp.float32))
        e = elem_ref[:, at]
        n = node_ref[:, at]
        surface_cols = 128 * (last_y + 1)
        er = e // surface_cols
        lx = er - 2 * at_x + 1
        ly = (e - er * surface_cols) - 128 * at_y + 1
        inside = (ly >= 1) & (ly <= 128)
        own_row = (lx == 1) | (lx == 2)
        half = jnp.where(own_row, 0, 1)
        line = 2 * n + jnp.where(lx >= 2, 1, 0)
        a = jnp.where(inside, line, 50)
        b = jnp.where(
            inside,
            half * 128 + ly - 1,
            jnp.where(ly == 0, 0, 128) + 64 * half + line,
        )
        row_slot[:, at] = a.astype(jnp.float32)
        col_slot[:, at] = b.astype(jnp.float32)
        return carry

    lax.fori_loop(0, cols // 128, own_cells, 0)

    lanes = lax.broadcasted_iota(jnp.int32, (tall, 128), 1)
    first_lane = lanes == 0
    last_lane = lanes == 127
    tiles = wide // 128

    def press(f0, f1, b):
        return b * (f0 + f1), upper_gravity * density_ratio * f0 + upper_gravity * f1

    def step(s, carry):
        now = s % 2
        later = 1 - now

        def tile_step(t, carry):
            at = pl.ds(pl.multiple_of(t * 128, 128), 128)
            t_hi = jnp.where(t == tiles - 1, 0, t + 1)
            t_lo = jnp.where(t == 0, tiles - 1, t - 1)
            at_hi = pl.ds(pl.multiple_of(t_hi * 128, 128), 128)
            at_lo = pl.ds(pl.multiple_of(t_lo * 128, 128), 128)
            f = [ext[now, k, :, at] for k in range(6)]
            b = buoy[:, at]
            one, two = press(f[0], f[1], b)
            sums = [None] * 6

            def add(k, value):
                sums[k] = value if sums[k] is None else sums[k] + value

            for ahead in (True, False):
                by = tall - 1 if ahead else 1
                def rolled(x):
                    return pltpu.roll(x, by, 0)
                sg = -1.0 if ahead else 1.0
                def mix(x, y):
                    return x - y if ahead else x + y
                add(0, rolled(mix(f[0], f[2])))
                add(1, rolled(mix(f[1], f[4])))
                add(2, rolled(mix(f[2], one)))
                add(3, rolled(f[3]))
                add(4, rolled(mix(f[4], two)))
                add(5, rolled(f[5]))
            for ahead in (True, False):
                by = 127 if ahead else 1
                edge = first_lane if ahead else last_lane
                other = at_hi if ahead else at_lo
                g = [jnp.where(edge, ext[now, k, :, other], f[k]) for k in range(6)]
                gb = jnp.where(edge, buoy[:, other], b)
                g_one, g_two = press(g[0], g[1], gb)
                def rolled(x):
                    return pltpu.roll(x, by, 1)
                def mix(x, y):
                    return x - y if ahead else x + y
                add(0, rolled(mix(g[0], g[3])))
                add(1, rolled(mix(g[1], g[5])))
                add(2, rolled(g[2]))
                add(3, rolled(mix(g[3], g_one)))
                add(4, rolled(g[4]))
                add(5, rolled(mix(g[5], g_two)))
            speed = jnp.sqrt(f[2] * f[2] + f[3] * f[3] + speed_floor)
            rub = 2.0 * drag[:, at] * speed
            k = scale[:, at]
            ext[later, 0, :, at] = k * (f[0] + sums[0])
            ext[later, 1, :, at] = k * (f[1] + sums[1])
            ext[later, 2, :, at] = k * (sums[2] + f[4] - rub * f[2])
            ext[later, 3, :, at] = k * (sums[3] + f[5] - rub * f[3])
            ext[later, 4, :, at] = k * (sums[4] + f[2])
            ext[later, 5, :, at] = k * (sums[5] + f[3])
            return carry

        return lax.fori_loop(0, tiles, tile_step, carry)

    lax.fori_loop(0, FLOW_STEPS, step, 0)
    store_fields.start()

    def pull(t, carry):
        at = pl.ds(pl.multiple_of(t * 128, 128), 128)
        f = [ext[0, k, 0:rows, at] for k in range(4)]
        rub = load_factor * drag[0:rows, at] * jnp.sqrt(f[2] * f[2] + f[3] * f[3] + speed_floor)
        tract[0, :, at] = rub * f[2]
        tract[1, :, at] = rub * f[3]
        tract[2, :, at] = -load_factor * (buoy[0:rows, at] * (f[0] + f[1]))
        return carry

    lax.fori_loop(0, cols // 128, pull, 0)

    table_ref[...] = jnp.zeros_like(table_ref)
    count = lax.broadcasted_iota(jnp.int32, (16, cols), 0).astype(jnp.float32).astype(jnp.bfloat16)

    def spread(r, carry):
        line = pl.ds(r, 1)

        def wide16(x):
            return jnp.broadcast_to(x, (16, cols)).astype(jnp.bfloat16)

        parts = []
        for k in range(3):
            value = tract[k, line, :]
            high = value.astype(jnp.bfloat16).astype(jnp.float32)
            parts.append(wide16(value))
            parts.append(wide16(value - high))
        a = wide16(row_slot[line, :])
        b = wide16(col_slot[line, :])
        zero = jnp.zeros((16, cols), jnp.bfloat16)
        one = jnp.ones((16, cols), jnp.bfloat16)
        hits = [a == count + jnp.bfloat16(16 * m) for m in range(4)]
        left = jnp.concatenate([jnp.where(h, p, zero) for p in parts for h in hits], axis=0)
        right = jnp.concatenate(
            [jnp.where(b == count + jnp.bfloat16(16 * m), one, zero) for m in range(16)], axis=0
        )
        got = lax.dot_general(
            left, right, (((1,), (1,)), ((), ())), preferred_element_type=jnp.float32
        )
        table_ref[...] += got
        return carry

    lax.fori_loop(0, rows, spread, 0)
    table = [table_ref[128 * k : 128 * k + 64] + table_ref[128 * k + 64 : 128 * k + 128] for k in range(3)]
    load_parts(table, own_ref, beyond_ref, sides_ref)


def line(matrix, s):
    even = [s[0] + s[4], s[1] + s[3]]
    odd = [s[0] - s[4], s[1] - s[3]]
    out = [None] * 5
    for a in range(2):
        half_sum = [0.5 * (matrix[a, p] - matrix[a, 4 - p]) for p in range(2)]
        half_diff = [0.5 * (matrix[a, p] + matrix[a, 4 - p]) for p in range(2)]
        x = float(half_sum[0]) * odd[0] + float(half_sum[1]) * odd[1]
        y = float(half_diff[0]) * even[0] + float(half_diff[1]) * even[1] + float(matrix[a, 2]) * s[2]
        out[a] = x + y
        out[4 - a] = x - y
    out[2] = float(matrix[2, 0]) * odd[0] + float(matrix[2, 1]) * odd[1]
    return out


def lane_row():
    lane = lax.broadcasted_iota(jnp.int32, (4, 128), 1)
    row = lax.broadcasted_iota(jnp.int32, (4, 128), 0)
    return lane, row


def internal_local(u_ref, lame_ref, shear_ref, stress, force):
    table = derivative_table()

    def slope_x(m, carry):
        for i in range(3):
            lines = line(table, [u_ref[i * 125 + a * 25 + m] for a in range(5)])
            for a in range(5):
                stress[i * 125 + a * 25 + m] = lines[a]
        return carry

    lax.fori_loop(0, 25, slope_x, 0)

    def plane(a, carry):
        weight = jnp.where(
            (a == 0) | (a == 4),
            np.float32(gll_weights[0]),
            jnp.where(a == 2, np.float32(gll_weights[2]), np.float32(gll_weights[1])),
        )
        lame = lame_ref[...] * -weight
        shear = shear_ref[...] * -weight

        def at(i, b, c):
            return i * 125 + a * 25 + b * 5 + c

        slope_y, slope_z = [], []
        for i in range(3):
            u = [[u_ref[at(i, b, c)] for c in range(5)] for b in range(5)]
            along_y = [line(table, [u[b][c] for b in range(5)]) for c in range(5)]
            slope_y.append([[along_y[c][b] for c in range(5)] for b in range(5)])
            slope_z.append([line(table, u[b]) for b in range(5)])
        pull_y = [[[None] * 5 for b in range(5)] for i in range(3)]
        pull_z = [[[None] * 5 for b in range(5)] for i in range(3)]
        for b in range(5):
            for c in range(5):
                w = np.float32(gll_weights[b] * gll_weights[c])
                g = [[stress[at(i, b, c)], slope_y[i][b][c], slope_z[i][b][c]] for i in range(3)]
                mu = shear * w
                twice = mu + mu
                spread = (lame * w) * (g[0][0] + g[1][1] + g[2][2])
                s00 = spread + twice * g[0][0]
                s11 = spread + twice * g[1][1]
                s22 = spread + twice * g[2][2]
                s01 = mu * (g[0][1] + g[1][0])
                s02 = mu * (g[0][2] + g[2][0])
                s12 = mu * (g[1][2] + g[2][1])
                stress[at(0, b, c)] = s00
                stress[at(1, b, c)] = s01
                stress[at(2, b, c)] = s02
                for i, (s_y, s_z) in enumerate(((s01, s02), (s11, s12), (s12, s22))):
                    pull_y[i][b][c] = s_y
                    pull_z[i][b][c] = s_z
        for i in range(3):
            along_y = [line(table.T, [pull_y[i][b][c] for b in range(5)]) for c in range(5)]
            for b in range(5):
                along_z = line(table.T, pull_z[i][b])
                for c in range(5):
                    force[at(i, b, c)] = along_y[c][b] + along_z[c]
        return carry

    lax.fori_loop(0, 5, plane, 0)
    lane, row = lane_row()
    low_x = row % 2 == 0
    low_z = row < 2

    def close_x(m, carry):
        for i in range(3):
            pulled = line(table.T, [stress[i * 125 + a * 25 + m] for a in range(5)])
            f = [force[i * 125 + a * 25 + m] + pulled[a] for a in range(5)]
            near = f[0] + jnp.where(low_x, 0.0, pltpu.roll(f[4], 1, 0))
            far = f[4] + jnp.where(low_x, pltpu.roll(f[0], 3, 0), 0.0)
            for a, value in enumerate((near, f[1], f[2], f[3], far)):
                force[i * 125 + a * 25 + m] = value
        return carry

    lax.fori_loop(0, 25, close_x, 0)

    def close_yz(ia, carry):
        base = ia * 25
        f = [[force[base + b * 5 + c] for c in range(5)] for b in range(5)]
        for c in range(5):
            near, far = f[0][c], f[4][c]
            f[0][c] = near + jnp.where(lane == 0, 0.0, pltpu.roll(far, 1, 1))
            f[4][c] = far + jnp.where(lane == 127, 0.0, pltpu.roll(near, 127, 1))
        for b in range(5):
            near, far = f[b][0], f[b][4]
            f[b][0] = near + jnp.where(low_z, 0.0, pltpu.roll(far, 2, 0))
            f[b][4] = far + jnp.where(low_z, pltpu.roll(near, 2, 0), 0.0)
        for b in range(5):
            for c in range(5):
                if b in (0, 4) or c in (0, 4):
                    force[base + b * 5 + c] = f[b][c]
        return carry

    lax.fori_loop(0, 15, close_yz, 0)


def pack_faces(force, face_x, face_y):
    lane, row = lane_row()
    low_x = row % 2 == 0

    def pack_x(m, carry):
        for i in range(3):
            face_x[i * 25 + m] = jnp.where(low_x, force[i * 125 + m], force[i * 125 + 100 + m])
        return carry

    lax.fori_loop(0, 25, pack_x, 0)
    ends = [jnp.zeros((4, 128), jnp.float32)] * 2
    for a in range(5):
        for i in range(3):
            for c in range(5):
                q = a * 15 + i * 5 + c
                n = i * 125 + a * 25 + c
                ends[0] = jnp.where(lane == q, pltpu.roll(force[n], q, 1), ends[0])
                ends[1] = jnp.where(lane == q, pltpu.roll(force[n + 20], q + 1, 1), ends[1])
    face_y[0] = ends[0]
    face_y[1] = ends[1]


def open_edges():
    at_x, at_y = lax.axis_index("gx"), lax.axis_index("gy")
    has = {-1: at_x > 0, 1: at_x < lax.axis_size("gx") - 1}
    has_y = {-1: at_y > 0, 1: at_y < lax.axis_size("gy") - 1}
    return has, has_y


def add_faces(force, got_x, got_y):
    has_x, has_y = open_edges()
    lane, row = lane_row()
    low_x = row % 2 == 0

    def add_x(m, carry):
        for i in range(3):
            low = jnp.where(low_x & has_x[-1], pltpu.roll(got_x[0][i * 25 + m], 3, 0), 0.0)
            high = jnp.where(low_x | jnp.logical_not(has_x[1]), 0.0, pltpu.roll(got_x[1][i * 25 + m], 1, 0))
            force[i * 125 + m] += low
            force[i * 125 + 100 + m] += high
        return carry

    lax.fori_loop(0, 25, add_x, 0)
    first, final = lane < 15, (lane >= 60) & (lane < 75)
    columns = []
    for side, end in ((-1, 1), (1, 0)):
        straight = got_y[0, side][end]
        low = pltpu.roll(pltpu.roll(got_y[-1, side][end], 68, 1), 3, 0)
        high = pltpu.roll(pltpu.roll(got_y[1, side][end], 60, 1), 1, 0)
        total = straight + jnp.where(first & low_x & has_x[-1], low, 0.0)
        total = total + jnp.where(final & jnp.logical_not(low_x) & has_x[1], high, 0.0)
        columns.append(jnp.where(has_y[side], total, 0.0))
    for a in range(5):
        for i in range(3):
            for c in range(5):
                q = a * 15 + i * 5 + c
                n = i * 125 + a * 25 + c
                force[n] += jnp.where(lane == 0, pltpu.roll(columns[0], (128 - q) % 128, 1), 0.0)
                force[n + 20] += jnp.where(lane == 127, pltpu.roll(columns[1], 127 - q, 1), 0.0)


def inverse_masses(density_ref, around, inverse):
    has_x, has_y = open_edges()
    lane, row = lane_row()
    low_x = row % 2 == 0
    low_z = row < 2

    def beside(mine, left, right):
        left = jnp.where(has_y[-1], left, 0.0)
        right = jnp.where(has_y[1], right, 0.0)
        before = jnp.where(lane == 0, pltpu.roll(left, 1, 1), pltpu.roll(mine, 1, 1))
        after = jnp.where(lane == 127, pltpu.roll(right, 127, 1), pltpu.roll(mine, 127, 1))
        return mine + before, mine, mine + after

    mine = beside(density_ref[...], around[0, -1][...], around[0, 1][...])
    low = beside(around[-1, 0][...], around[-1, -1][...], around[-1, 1][...])
    high = beside(around[1, 0][...], around[1, -1][...], around[1, 1][...])
    for b in range(3):
        lo = jnp.where(has_x[-1], low[b], 0.0)
        hi = jnp.where(has_x[1], high[b], 0.0)
        before = mine[b] + jnp.where(low_x, pltpu.roll(lo, 3, 0), pltpu.roll(mine[b], 1, 0))
        after = mine[b] + jnp.where(low_x, pltpu.roll(mine[b], 3, 0), pltpu.roll(hi, 1, 0))
        for a, value in enumerate((before, mine[b], after)):
            top = value + jnp.where(low_z, 0.0, pltpu.roll(value, 2, 0))
            bottom = value + jnp.where(low_z, pltpu.roll(value, 2, 0), 0.0)
            for c, total in enumerate((top, value, bottom)):
                inverse[a * 9 + b * 3 + c] = (solid_dt * solid_dt) / total


def kind(node):
    return 0 if node == 0 else 2 if node == 4 else 1


def advance_solid(force, load, inverse, now_ref, before_ref, out_ref):
    def component(i, carry):
        for a in range(5):
            for b in range(5):
                for c in range(5):
                    n = a * 25 + b * 5 + c
                    f = force[i * 125 + n]
                    if c == 0:
                        f = f + load[i * 25 + a * 5 + b]
                    w = np.float32(1.0 / (gll_weights[a] * gll_weights[b] * gll_weights[c]))
                    step = (inverse[kind(a) * 9 + kind(b) * 3 + kind(c)] * w) * f
                    at = i * 125 + n
                    out_ref[at] = (now_ref[at] + now_ref[at] - before_ref[at]) + step
        return carry

    lax.fori_loop(0, 3, component, 0)


def load_grid():
    row = lax.broadcasted_iota(jnp.int32, (56, 128), 0)
    lane = lax.broadcasted_iota(jnp.int32, (56, 128), 1)
    return row, lane


def rows_up(x, by):
    return jnp.concatenate([x[by:], jnp.zeros((by, 128), jnp.float32)], axis=0)


def rows_down(x, by):
    return jnp.concatenate([jnp.zeros((by, 128), jnp.float32), x[:-by]], axis=0)


def masks_x():
    row, lane = load_grid()
    even = row % 2 == 0
    odd = row % 2 == 1
    return (row < 10) & even, (row < 10) & odd, (row >= 40) & (row < 50) & even, (row >= 40) & (row < 50) & odd


def masks_y():
    row, lane = load_grid()
    place = row % 10
    return (place < 2) & (row < 50), (place >= 8) & (row < 50), lane == 0, lane == 127


def join_x(x):
    near_even, near_odd, far_even, far_odd = masks_x()
    return (
        x
        + jnp.where(near_odd, pltpu.roll(rows_up(x, 40), 1, 0), 0.0)
        + jnp.where(far_even, pltpu.roll(rows_down(x, 40), 55, 0), 0.0)
    )


def join_x_wide(own, halo):
    near_even, near_odd, far_even, far_odd = masks_x()
    own_new = join_x(own)
    own_new = own_new + jnp.where(near_even, rows_up(halo, 40), 0.0)
    own_new = own_new + jnp.where(far_odd, rows_down(halo, 40), 0.0)
    halo_new = halo + jnp.where(far_even, rows_down(own, 40), 0.0)
    halo_new = halo_new + jnp.where(near_odd, rows_up(own, 40), 0.0)
    return own_new, halo_new


def join_y(x, sides):
    near, far, first, final = masks_y()
    before, after = pltpu.roll(x, 1, 1), pltpu.roll(x, 127, 1)
    fill_before = 0.0 if sides is None else pltpu.roll(sides, 1, 1)
    fill_after = 0.0 if sides is None else pltpu.roll(sides, 127, 1)
    out = x + jnp.where(near, rows_up(jnp.where(first, fill_before, before), 8), 0.0)
    out = out + jnp.where(far, rows_down(jnp.where(final, fill_after, after), 8), 0.0)
    if sides is None:
        return out
    new = sides + jnp.where(far & final, rows_down(after, 8), 0.0)
    new = new + jnp.where(near & first, rows_up(before, 8), 0.0)
    return out, new


def columns_from(tile):
    row, lane = load_grid()
    turned = jnp.concatenate([tile, jnp.zeros((120, 128), jnp.float32)], axis=0).T
    out = []
    for k in range(3):
        halves = []
        for h in range(2):
            part = turned[64 * h : 64 * h + 56]
            left = pltpu.roll(part, 127 - 2 * k, 1)
            right = pltpu.roll(part, (128 - 2 * k - 1) % 128, 1)
            value = jnp.where(lane == 127, left, jnp.where(lane == 0, right, 0.0))
            halves.append(jnp.where(row < 50, value, 0.0))
        out.append(halves)
    return out


def columns_to(columns):
    lane = lax.broadcasted_iota(jnp.int32, (128, 128), 1)
    total = jnp.zeros((128, 128), jnp.float32)
    for k in range(3):
        pad = jnp.zeros((8, 128), jnp.float32)
        x = jnp.concatenate([columns[k][0], pad, columns[k][1], pad], axis=0)
        total = jnp.where(lane == 2 * k, pltpu.roll(x, 2 * k + 1, 1), total)
        total = jnp.where(lane == 2 * k + 1, pltpu.roll(x, 2 * k + 1, 1), total)
    return total.T[:8]


def load_parts(table, own_ref, beyond_ref, sides_ref):
    row, lane = load_grid()
    line_of = lax.broadcasted_iota(jnp.int32, (8, 128), 0)
    raw = jnp.zeros((8, 128), jnp.float32)
    for k in range(3):
        for side in range(2):
            last = jnp.broadcast_to(table[k][50:51, 128 * side : 128 * side + 128], (8, 128))
            raw = jnp.where(line_of == 2 * k + side, last, raw)
    columns = columns_from(raw)
    new_columns = []
    for k in range(3):
        own = jnp.where(row < 50, table[k][:56, :128], 0.0)
        halo = jnp.where(row < 50, table[k][:56, 128:], 0.0)
        own, halo = join_x_wide(own, halo)
        sides = join_x_wide(columns[k][0], columns[k][1])
        own, side_own = join_y(own, sides[0])
        halo, side_halo = join_y(halo, sides[1])
        own_ref[k] = own
        beyond_ref[k] = halo
        new_columns.append((side_own, side_halo))
    sides_ref[...] = columns_to(new_columns)


def load_total(own_ref, got_x, got_y, load):
    has_x, has_y = open_edges()
    row, lane = load_grid()
    even = row % 2 == 0
    tile_lane = lax.broadcasted_iota(jnp.int32, (8, 128), 1)
    tile_row = lax.broadcasted_iota(jnp.int32, (8, 128), 0)
    ends = []
    for side in (-1, 1):
        low = jnp.where(has_x[-1], pltpu.roll(got_y[-1, side][...], 127, 1), 0.0)
        high = jnp.where(has_x[1], pltpu.roll(got_y[1, side][...], 1, 1), 0.0)
        tile = jnp.where(tile_lane < 64, got_y[0, side][...], jnp.where(tile_lane % 2 == 0, low, high))
        ends.append(jnp.where(has_y[side], tile, 0.0))
    columns = columns_from(jnp.where(tile_row % 2 == 0, ends[1], ends[0]))
    for k in range(3):
        low = jnp.where(has_x[-1], pltpu.roll(got_x[0][k], 55, 0), 0.0)
        high = jnp.where(has_x[1], pltpu.roll(got_x[1][k], 1, 0), 0.0)
        rows = jnp.where(even, low, high) + join_y(columns[k][1], None)
        total = own_ref[k] + join_x(jnp.where(row < 50, rows, 0.0)) + join_y(columns[k][0], None)
        for n in range(25):
            load[k * 25 + n] = jnp.concatenate(
                [total[2 * n : 2 * n + 2], jnp.zeros((2, 128), jnp.float32)], axis=0
            )


AROUND = [(-1, 0), (1, 0), (0, -1), (0, 1), (-1, -1), (-1, 1), (1, -1), (1, 1)]
ASIDE = AROUND[2:]


def shape(*dims, kind=jnp.float32):
    return jax.ShapeDtypeStruct(dims, kind)


def halo_plan(rows, cols):
    edge_rows = {-1: pl.ds(0, 4), 1: pl.ds(rows - 4, 4)}
    edge_cols = {-1: pl.ds(0, 128), 1: pl.ds(cols - 128, 128)}
    place_rows = {-1: pl.ds(0, 4), 1: pl.ds(4, 4)}
    messages = []
    for source in range(3):
        every = (slice(None),) if source == 0 else ()
        for dx, dy in AROUND:
            row_in = edge_rows.get(dx, pl.ds(0, rows))
            row_out = place_rows.get(dx, pl.ds(0, rows))
            col_in = edge_cols.get(dy, pl.ds(0, cols))
            where = 0 if dy == 0 else (1 if dx == 0 else 3) + (0 if dy == 1 else 1)
            messages.append(
                (source, every + (row_in, col_in), 5 * source + where,
                 every + (row_out, pl.ds(0, cols if dy == 0 else 128)), (dx, dy))
            )
    return messages


def whole_body(*refs):
    (flow_in, drag_in, wet_in, elem_in, node_in, u_in, before_in, density_in, lame_in, shear_in) = refs[:10]
    fields_out, next_out, last_out = refs[10:13]
    (ext, drag, buoy, scale, tract, row_slot, col_slot, table) = refs[13:21]
    halos = refs[21:36]
    (drag_own, wet_own, elem_own, node_own) = refs[36:40]
    (u_zero, before, u_one, u_two, force, stress, load, inverse) = refs[40:48]
    (density, lame, shear, around) = refs[48:52]
    (face_x, face_y, got_face_x, got_face_y) = refs[52:56]
    (own, beyond, sides, got_beyond, got_sides) = refs[56:61]
    local_sem, sent, come = refs[61:]
    rows, cols = drag_own.shape
    at_x, at_y = lax.axis_index("gx"), lax.axis_index("gy")
    size_x, size_y = lax.axis_size("gx"), lax.axis_size("gy")

    def device(move):
        return ((at_x + move[0] + size_x) % size_x, (at_y + move[1] + size_y) % size_y)

    def opposite(move):
        return -move[0], -move[1]

    barrier = pltpu.get_barrier_semaphore()
    for move in AROUND:
        pl.semaphore_signal(barrier, inc=1, device_id=device(move), device_id_type=pl.DeviceIdType.MESH)
    reads = [
        pltpu.make_async_copy(source, target, local_sem.at[n])
        for n, (source, target) in enumerate(
            (
                (u_in, u_zero), (lame_in, lame), (shear_in, shear), (density_in, density),
                (flow_in, ext.at[0, :, 0:rows, 0:cols]), (drag_in, drag_own), (wet_in, wet_own),
                (elem_in, elem_own), (node_in, node_own), (before_in, before),
            )
        )
    ]
    for copy in reads:
        copy.start()
    store_fields = pltpu.make_async_copy(ext.at[0, :, 0:rows, 0:cols], fields_out, local_sem.at[10])
    store_last = pltpu.make_async_copy(u_one, last_out, local_sem.at[11])
    store_next = pltpu.make_async_copy(u_two, next_out, local_sem.at[12])
    pl.semaphore_wait(barrier, len(AROUND))
    number = [0]

    def send(source, target, move):
        n = number[0]
        number[0] += 1
        copy = pltpu.make_async_remote_copy(
            src_ref=source, dst_ref=target, send_sem=sent.at[n], recv_sem=come.at[n],
            device_id=device(move), device_id_type=pl.DeviceIdType.MESH,
        )
        copy.start()
        return copy

    operands = (flow_in, drag_in, wet_in)
    first = [
        send(operands[source].at[source_at], halos[target].at[target_at], move)
        for source, source_at, target, target_at, move in halo_plan(rows, cols)
    ]
    first += [send(density_in, around.at[AROUND.index(opposite(move))], move) for move in AROUND]

    def send_faces(step):
        copies = [send(face_x.at[step], got_face_x.at[step, 1], (-1, 0))]
        copies += [send(face_x.at[step], got_face_x.at[step, 0], (1, 0))]
        for move in ASIDE:
            copies.append(send(face_y.at[step], got_face_y.at[step, ASIDE.index(opposite(move))], move))
        return copies

    def faces_of(step):
        return (
            [got_face_x.at[step, n] for n in range(2)],
            {move: got_face_y.at[step, n] for n, move in enumerate(ASIDE)},
        )

    for copy in reads[:3]:
        copy.wait()
    internal_local(u_zero, lame, shear, stress, force)
    pack_faces(force, face_x.at[0], face_y.at[0])
    faces = send_faces(0)
    for copy in reads[3:] + first:
        copy.wait()
    inverse_masses(density, {move: around.at[n] for n, move in enumerate(AROUND)}, inverse)
    surface(
        drag_own, wet_own, elem_own, node_own, (halos[0:5], halos[5:10], halos[10:15]),
        own, beyond, sides, ext, drag, buoy, scale, tract, row_slot, col_slot, table, store_fields,
    )
    loads = [send(beyond, got_beyond.at[1], (-1, 0)), send(beyond, got_beyond.at[0], (1, 0))]
    for move in ASIDE:
        loads.append(send(sides, got_sides.at[ASIDE.index(opposite(move))], move))
    for copy in faces:
        copy.wait()
    add_faces(force, *faces_of(0))
    for copy in loads:
        copy.wait()
    load_total(
        own,
        [got_beyond.at[n] for n in range(2)],
        {move: got_sides.at[n] for n, move in enumerate(ASIDE)},
        load,
    )
    advance_solid(force, load, inverse, u_zero, before, u_one)
    store_last.start()
    internal_local(u_one, lame, shear, stress, force)
    pack_faces(force, face_x.at[1], face_y.at[1])
    faces = send_faces(1)
    for copy in faces:
        copy.wait()
    add_faces(force, *faces_of(1))
    advance_solid(force, load, inverse, u_one, u_zero, u_two)
    store_next.start()
    store_fields.wait()
    store_last.wait()
    store_next.wait()


def per_device(
    flow_state,
    drag_coefficient,
    wet_mask,
    target_elem,
    target_node,
    displacement,
    previous,
    density,
    lame_first,
    shear_modulus,
):
    rows, cols = drag_coefficient.shape
    tall, wide = rows + 8, cols + 128
    grid = displacement.shape
    nodes = (375, 4, 128)
    halo_shapes = []
    for lead, kind_of in (((6,), jnp.float32), ((), jnp.float32), ((), jnp.int32)):
        for dims in ((8, cols), (rows, 128), (rows, 128), (8, 128), (8, 128)):
            halo_shapes.append(pltpu.VMEM((*lead, *dims), kind_of))

    def floats(*dims):
        return pltpu.VMEM(dims, jnp.float32)

    def integers(*dims):
        return pltpu.VMEM(dims, jnp.int32)

    scratch = [
        floats(2, 6, tall, wide), floats(tall, wide), floats(tall, wide), floats(tall, wide),
        floats(3, rows, cols), floats(rows, cols), floats(rows, cols), floats(384, 256),
        *halo_shapes,
        floats(rows, cols), integers(rows, cols), integers(rows, cols), integers(rows, cols),
        *[floats(*nodes)] * 6, floats(75, 4, 128), floats(27, 4, 128),
        floats(4, 128), floats(4, 128), floats(4, 128), floats(8, 4, 128),
        floats(2, 75, 4, 128), floats(2, 2, 4, 128), floats(2, 2, 75, 4, 128), floats(2, 6, 2, 4, 128),
        floats(3, 56, 128), floats(3, 56, 128), floats(8, 128), floats(2, 3, 56, 128), floats(6, 8, 128),
        pltpu.SemaphoreType.DMA((13,)), pltpu.SemaphoreType.DMA((56,)), pltpu.SemaphoreType.DMA((56,)),
    ]
    anywhere = pl.BlockSpec(memory_space=pl.ANY)
    fields, u_two, u_one = pl.pallas_call(
        whole_body,
        out_shape=(shape(6, rows, cols), shape(*nodes), shape(*nodes)),
        in_specs=[anywhere] * 10,
        out_specs=(anywhere,) * 3,
        scratch_shapes=scratch,
        compiler_params=pltpu.CompilerParams(
            collective_id=1, has_side_effects=True, vmem_limit_bytes=56 * 2**20
        ),
    )(
        flow_state, drag_coefficient, wet_mask, target_elem, target_node,
        displacement.reshape(nodes), previous.reshape(nodes),
        *(x.reshape(4, 128) for x in (density, lame_first, shear_modulus)),
    )
    return (fields, u_two.reshape(grid), u_one.reshape(grid))


def solution(mesh):
    return jax.shard_map(
        per_device,
        mesh=mesh,
        in_specs=(
            P(None, "gx", "gy"),
            P("gx", "gy"),
            P("gx", "gy"),
            P("gx", "gy"),
            P("gx", "gy"),
            P(None, None, None, None, None, "gx", "gy"),
            P(None, None, None, None, None, "gx", "gy"),
            P(None, "gx", "gy"),
            P(None, "gx", "gy"),
            P(None, "gx", "gy"),
        ),
        out_specs=(
            P(None, "gx", "gy"),
            P(None, None, None, None, None, "gx", "gy"),
            P(None, None, None, None, None, "gx", "gy"),
        ),
        check_vma=False,
    )
```

```python
import jax
import jax.numpy as jnp
import numpy as np
from jax import lax
from jax.experimental import pallas as pl
from jax.experimental.pallas import tpu as pltpu
from jax.sharding import PartitionSpec as P

FLOW_STEPS = 4
SOLID_STEPS = 2
SLOT_ROWS = 51
GROUP = 8


gll_points = np.array([-1.0, -np.sqrt(3.0 / 7.0), 0.0, np.sqrt(3.0 / 7.0), 1.0])
gll_weights = np.array([0.1, 49.0 / 90.0, 32.0 / 45.0, 49.0 / 90.0, 0.1])
flow_dt = 0.4
diffusion = 0.2
coupling = 0.5
upper_gravity = 0.8
density_ratio = 0.7
speed_floor = 0.0001
load_factor = 4.0
solid_dt = 0.04


def legendre_four(x):
    return (35.0 * x**4 - 30.0 * x**2 + 3.0) / 8.0


def derivative_table():
    result = np.zeros((5, 5))
    for i in range(5):
        for j in range(5):
            if i != j:
                result[i, j] = (
                    legendre_four(gll_points[i])
                    / legendre_four(gll_points[j])
                    / (gll_points[i] - gll_points[j])
                )
    result[0, 0] = -5.0
    result[4, 4] = 5.0
    return result


def surface(
    drag_ref, wet_ref, elem_ref, node_ref, got, own_ref, beyond_ref, sides_ref,
    ext, drag, buoy, scale, tract, row_slot, col_slot, table_ref, store_fields,
):
    rows, cols = drag_ref.shape
    wide = cols + 128
    tall = rows + 8
    at_x, at_y = lax.axis_index("gx"), lax.axis_index("gy")
    last_x, last_y = lax.axis_size("gx") - 1, lax.axis_size("gy") - 1

    def wetness(x):
        return 1.0 - 0.6 * x

    sub = lax.broadcasted_iota(jnp.int32, (8, 128), 0)
    lane = lax.broadcasted_iota(jnp.int32, (8, 128), 1)
    up_half = sub < 4
    left_half = lane < 64

    def zero_rows(tile):
        tile = jnp.where(up_half & (at_x == last_x), 0.0, tile)
        return jnp.where(jnp.logical_not(up_half) & (at_x == 0), 0.0, tile)

    def zero_cols(tile):
        tile = jnp.where(left_half & (at_y == last_y), 0.0, tile)
        return jnp.where(jnp.logical_not(left_half) & (at_y == 0), 0.0, tile)

    def received(k, n, *at):
        if k < 6:
            return got[0][n][(k, *at)]
        tile = got[k - 5][n][at]
        return tile if k == 6 else tile.astype(jnp.float32)

    def place(k, r, c, tile):
        if k < 6:
            ext[0, k, r, c] = tile
        elif k == 6:
            drag[r, c] = tile
        else:
            buoy[r, c] = wetness(tile)

    tail = pl.ds(cols, 128)
    foot = pl.ds(rows, 8)
    ones = jnp.full((8, 128), 0.2, jnp.float32)
    row_scale = zero_rows(ones)
    col_scale = zero_cols(ones)

    def halo_rows(t, carry):
        at = pl.ds(pl.multiple_of(t * 128, 128), 128)
        for k in range(8):
            place(k, foot, at, zero_rows(received(k, 0, slice(None), at)))
        for r in range(0, rows, 8):
            scale[r : r + 8, at] = ones
        scale[foot, at] = row_scale
        return carry

    lax.fori_loop(0, cols // 128, halo_rows, 0)
    for k in range(8):
        for r in range(0, rows, 8):
            at = (slice(r, r + 8), slice(None))
            tile = jnp.where(left_half, received(k, 2, *at), received(k, 1, *at))
            place(k, pl.ds(r, 8), tail, zero_cols(tile))
        at = (slice(None), slice(None))
        tile = jnp.where(left_half, received(k, 4, *at), received(k, 3, *at))
        place(k, foot, tail, zero_cols(zero_rows(tile)))
    for r in range(0, rows, 8):
        scale[r : r + 8, tail] = col_scale
    scale[foot, tail] = zero_cols(row_scale)

    def own_cells(t, carry):
        at = pl.ds(pl.multiple_of(t * 128, 128), 128)
        drag[0:rows, at] = drag_ref[:, at]
        buoy[0:rows, at] = wetness(wet_ref[:, at].astype(jnp.float32))
        e = elem_ref[:, at]
        n = node_ref[:, at]
        surface_cols = 128 * (last_y + 1)
        er = e // surface_cols
        lx = er - 2 * at_x + 1
        ly = (e - er * surface_cols) - 128 * at_y + 1
        inside = (ly >= 1) & (ly <= 128)
        own_row = (lx == 1) | (lx == 2)
        half = jnp.where(own_row, 0, 1)
        line = 2 * n + jnp.where(lx >= 2, 1, 0)
        a = jnp.where(inside, line, 50)
        b = jnp.where(
            inside,
            half * 128 + ly - 1,
            jnp.where(ly == 0, 0, 128) + 64 * half + line,
        )
        row_slot[:, at] = a.astype(jnp.float32)
        col_slot[:, at] = b.astype(jnp.float32)
        return carry

    lax.fori_loop(0, cols // 128, own_cells, 0)

    lanes = lax.broadcasted_iota(jnp.int32, (tall, 128), 1)
    first_lane = lanes == 0
    last_lane = lanes == 127
    tiles = wide // 128

    def press(f0, f1, b):
        return b * (f0 + f1), upper_gravity * density_ratio * f0 + upper_gravity * f1

    def step(now, carry):
        later = 1 - now

        def tile_step(t, carry):
            at = pl.ds(pl.multiple_of(t * 128, 128), 128)
            t_hi = jnp.where(t == tiles - 1, 0, t + 1)
            t_lo = jnp.where(t == 0, tiles - 1, t - 1)
            at_hi = pl.ds(pl.multiple_of(t_hi * 128, 128), 128)
            at_lo = pl.ds(pl.multiple_of(t_lo * 128, 128), 128)
            f = [ext[now, k, :, at] for k in range(6)]
            b = buoy[:, at]
            one, two = press(f[0], f[1], b)
            sums = [None] * 6

            def add(k, value):
                sums[k] = value if sums[k] is None else sums[k] + value

            for ahead in (True, False):
                by = tall - 1 if ahead else 1
                def rolled(x):
                    return pltpu.roll(x, by, 0)
                sg = -1.0 if ahead else 1.0
                def mix(x, y):
                    return x - y if ahead else x + y
                add(0, rolled(mix(f[0], f[2])))
                add(1, rolled(mix(f[1], f[4])))
                add(2, rolled(mix(f[2], one)))
                add(3, rolled(f[3]))
                add(4, rolled(mix(f[4], two)))
                add(5, rolled(f[5]))
            for ahead in (True, False):
                by = 127 if ahead else 1
                edge = first_lane if ahead else last_lane
                other = at_hi if ahead else at_lo
                g = [jnp.where(edge, ext[now, k, :, other], f[k]) for k in range(6)]
                gb = jnp.where(edge, buoy[:, other], b)
                g_one, g_two = press(g[0], g[1], gb)
                def rolled(x):
                    return pltpu.roll(x, by, 1)
                def mix(x, y):
                    return x - y if ahead else x + y
                add(0, rolled(mix(g[0], g[3])))
                add(1, rolled(mix(g[1], g[5])))
                add(2, rolled(g[2]))
                add(3, rolled(mix(g[3], g_one)))
                add(4, rolled(g[4]))
                add(5, rolled(mix(g[5], g_two)))
            speed = jnp.sqrt(f[2] * f[2] + f[3] * f[3] + speed_floor)
            rub = 2.0 * drag[:, at] * speed
            k = scale[:, at]
            ext[later, 0, :, at] = k * (f[0] + sums[0])
            ext[later, 1, :, at] = k * (f[1] + sums[1])
            ext[later, 2, :, at] = k * (sums[2] + f[4] - rub * f[2])
            ext[later, 3, :, at] = k * (sums[3] + f[5] - rub * f[3])
            ext[later, 4, :, at] = k * (sums[4] + f[2])
            ext[later, 5, :, at] = k * (sums[5] + f[3])
            return carry

        return lax.fori_loop(0, tiles, tile_step, carry, unroll=True)

    lax.fori_loop(0, FLOW_STEPS // 2, lambda _, carry: step(1, step(0, carry)), 0)
    store_fields.start()

    def pull(t, carry):
        at = pl.ds(pl.multiple_of(t * 128, 128), 128)
        f = [ext[0, k, 0:rows, at] for k in range(4)]
        rub = load_factor * drag[0:rows, at] * jnp.sqrt(f[2] * f[2] + f[3] * f[3] + speed_floor)
        tract[0, :, at] = rub * f[2]
        tract[1, :, at] = rub * f[3]
        tract[2, :, at] = -load_factor * (buoy[0:rows, at] * (f[0] + f[1]))
        return carry

    lax.fori_loop(0, cols // 128, pull, 0)

    table_ref[...] = jnp.zeros_like(table_ref)
    narrow = jnp.bfloat16
    row16 = lax.broadcasted_iota(jnp.int32, (16, cols), 0)
    count = row16.astype(jnp.float32).astype(narrow)

    def spread(group, carry):
        lefts, rights = [], []
        for n in range(GROUP):
            line = pl.ds(group * GROUP + n, 1)

            def wide16(x):
                return jnp.broadcast_to(x, (16, cols)).astype(narrow)

            parts = []
            for k in range(3):
                value = tract[k, line, :]
                high = value.astype(narrow).astype(jnp.float32)
                parts.append(wide16(value))
                parts.append(wide16(value - high))
            a = wide16(row_slot[line, :])
            b = wide16(col_slot[line, :])
            zero = jnp.zeros((16, cols), narrow)
            one = jnp.ones((16, cols), narrow)
            pieces = []
            for top in range(0, table_ref.shape[0], 16):
                part, last = top // SLOT_ROWS, min((top + 15) // SLOT_ROWS, 5)
                skip = top - SLOT_ROWS * part
                if part == last:
                    pieces.append(jnp.where(a == count + narrow(skip), parts[part], zero))
                else:
                    split = SLOT_ROWS * last - top
                    target = row16 + jnp.where(row16 < split, skip, -split)
                    mixed = jnp.where(count < narrow(split), parts[part], parts[last])
                    pieces.append(jnp.where(a == target.astype(jnp.float32).astype(narrow), mixed, zero))
            lefts.append(jnp.concatenate(pieces, axis=0))
            rights.append(
                jnp.concatenate([jnp.where(b == count + narrow(16 * m), one, zero) for m in range(16)], axis=0)
            )
        table_ref[...] += lax.dot_general(
            jnp.concatenate(lefts, axis=1),
            jnp.concatenate(rights, axis=1),
            (((1,), (1,)), ((), ())),
            preferred_element_type=jnp.float32,
        )
        return carry

    lax.fori_loop(0, rows // GROUP, spread, 0)

    def part_rows(n):
        return table_ref[SLOT_ROWS * n : SLOT_ROWS * n + SLOT_ROWS]

    pad = jnp.zeros((64 - SLOT_ROWS, 256), jnp.float32)
    table = [
        jnp.concatenate([part_rows(2 * k) + part_rows(2 * k + 1), pad], axis=0) for k in range(3)
    ]
    load_parts(table, own_ref, beyond_ref, sides_ref)


def line(matrix, s):
    even = [s[0] + s[4], s[1] + s[3]]
    odd = [s[0] - s[4], s[1] - s[3]]
    out = [None] * 5
    for a in range(2):
        half_sum = [0.5 * (matrix[a, p] - matrix[a, 4 - p]) for p in range(2)]
        half_diff = [0.5 * (matrix[a, p] + matrix[a, 4 - p]) for p in range(2)]
        x = float(half_sum[0]) * odd[0] + float(half_sum[1]) * odd[1]
        y = float(half_diff[0]) * even[0] + float(half_diff[1]) * even[1] + float(matrix[a, 2]) * s[2]
        out[a] = x + y
        out[4 - a] = x - y
    out[2] = float(matrix[2, 0]) * odd[0] + float(matrix[2, 1]) * odd[1]
    return out


def lane_row():
    lane = lax.broadcasted_iota(jnp.int32, (4, 128), 1)
    row = lax.broadcasted_iota(jnp.int32, (4, 128), 0)
    return lane, row


def internal_local(u_ref, lame_ref, shear_ref, stress, force):
    table = derivative_table()

    def slope_x(m, carry):
        for i in range(3):
            lines = line(table, [u_ref[i * 125 + a * 25 + m] for a in range(5)])
            for a in range(5):
                stress[i * 125 + a * 25 + m] = lines[a]
        return carry

    lax.fori_loop(0, 25, slope_x, 0)

    def plane(a, carry):
        weight = jnp.where(
            (a == 0) | (a == 4),
            np.float32(gll_weights[0]),
            jnp.where(a == 2, np.float32(gll_weights[2]), np.float32(gll_weights[1])),
        )
        lame = lame_ref[...] * -weight
        shear = shear_ref[...] * -weight

        def at(i, b, c):
            return i * 125 + a * 25 + b * 5 + c

        slope_y, slope_z = [], []
        for i in range(3):
            u = [[u_ref[at(i, b, c)] for c in range(5)] for b in range(5)]
            along_y = [line(table, [u[b][c] for b in range(5)]) for c in range(5)]
            slope_y.append([[along_y[c][b] for c in range(5)] for b in range(5)])
            slope_z.append([line(table, u[b]) for b in range(5)])
        pull_y = [[[None] * 5 for b in range(5)] for i in range(3)]
        pull_z = [[[None] * 5 for b in range(5)] for i in range(3)]
        for b in range(5):
            for c in range(5):
                w = np.float32(gll_weights[b] * gll_weights[c])
                g = [[stress[at(i, b, c)], slope_y[i][b][c], slope_z[i][b][c]] for i in range(3)]
                mu = shear * w
                twice = mu + mu
                spread = (lame * w) * (g[0][0] + g[1][1] + g[2][2])
                s00 = spread + twice * g[0][0]
                s11 = spread + twice * g[1][1]
                s22 = spread + twice * g[2][2]
                s01 = mu * (g[0][1] + g[1][0])
                s02 = mu * (g[0][2] + g[2][0])
                s12 = mu * (g[1][2] + g[2][1])
                stress[at(0, b, c)] = s00
                stress[at(1, b, c)] = s01
                stress[at(2, b, c)] = s02
                for i, (s_y, s_z) in enumerate(((s01, s02), (s11, s12), (s12, s22))):
                    pull_y[i][b][c] = s_y
                    pull_z[i][b][c] = s_z
        for i in range(3):
            along_y = [line(table.T, [pull_y[i][b][c] for b in range(5)]) for c in range(5)]
            for b in range(5):
                along_z = line(table.T, pull_z[i][b])
                for c in range(5):
                    force[at(i, b, c)] = along_y[c][b] + along_z[c]
        return carry

    lax.fori_loop(0, 5, plane, 0)
    lane, row = lane_row()
    low_x = row % 2 == 0
    low_z = row < 2

    def close_x(m, carry):
        for i in range(3):
            pulled = line(table.T, [stress[i * 125 + a * 25 + m] for a in range(5)])
            f = [force[i * 125 + a * 25 + m] + pulled[a] for a in range(5)]
            near = f[0] + jnp.where(low_x, 0.0, pltpu.roll(f[4], 1, 0))
            far = f[4] + jnp.where(low_x, pltpu.roll(f[0], 3, 0), 0.0)
            for a, value in enumerate((near, f[1], f[2], f[3], far)):
                force[i * 125 + a * 25 + m] = value
        return carry

    lax.fori_loop(0, 25, close_x, 0)

    def close_yz(ia, carry):
        base = ia * 25
        f = [[force[base + b * 5 + c] for c in range(5)] for b in range(5)]
        for c in range(5):
            near, far = f[0][c], f[4][c]
            f[0][c] = near + jnp.where(lane == 0, 0.0, pltpu.roll(far, 1, 1))
            f[4][c] = far + jnp.where(lane == 127, 0.0, pltpu.roll(near, 127, 1))
        for b in range(5):
            near, far = f[b][0], f[b][4]
            f[b][0] = near + jnp.where(low_z, 0.0, pltpu.roll(far, 2, 0))
            f[b][4] = far + jnp.where(low_z, pltpu.roll(near, 2, 0), 0.0)
        for b in range(5):
            for c in range(5):
                if b in (0, 4) or c in (0, 4):
                    force[base + b * 5 + c] = f[b][c]
        return carry

    lax.fori_loop(0, 15, close_yz, 0)


def pack_faces(force, face_x, face_y):
    lane, row = lane_row()
    low_x = row % 2 == 0

    def pack_x(m, carry):
        for i in range(3):
            face_x[i * 25 + m] = jnp.where(low_x, force[i * 125 + m], force[i * 125 + 100 + m])
        return carry

    lax.fori_loop(0, 25, pack_x, 0)
    ends = [jnp.zeros((4, 128), jnp.float32)] * 2
    for a in range(5):
        for i in range(3):
            for c in range(5):
                q = a * 15 + i * 5 + c
                n = i * 125 + a * 25 + c
                ends[0] = jnp.where(lane == q, pltpu.roll(force[n], q, 1), ends[0])
                ends[1] = jnp.where(lane == q, pltpu.roll(force[n + 20], q + 1, 1), ends[1])
    face_y[0] = ends[0]
    face_y[1] = ends[1]


def open_edges():
    at_x, at_y = lax.axis_index("gx"), lax.axis_index("gy")
    has = {-1: at_x > 0, 1: at_x < lax.axis_size("gx") - 1}
    has_y = {-1: at_y > 0, 1: at_y < lax.axis_size("gy") - 1}
    return has, has_y


def add_faces(force, got_x, got_y):
    has_x, has_y = open_edges()
    lane, row = lane_row()
    low_x = row % 2 == 0

    def add_x(m, carry):
        for i in range(3):
            low = jnp.where(low_x & has_x[-1], pltpu.roll(got_x[0][i * 25 + m], 3, 0), 0.0)
            high = jnp.where(low_x | jnp.logical_not(has_x[1]), 0.0, pltpu.roll(got_x[1][i * 25 + m], 1, 0))
            force[i * 125 + m] += low
            force[i * 125 + 100 + m] += high
        return carry

    lax.fori_loop(0, 25, add_x, 0)
    first, final = lane < 15, (lane >= 60) & (lane < 75)
    columns = []
    for side, end in ((-1, 1), (1, 0)):
        straight = got_y[0, side][end]
        low = pltpu.roll(pltpu.roll(got_y[-1, side][end], 68, 1), 3, 0)
        high = pltpu.roll(pltpu.roll(got_y[1, side][end], 60, 1), 1, 0)
        total = straight + jnp.where(first & low_x & has_x[-1], low, 0.0)
        total = total + jnp.where(final & jnp.logical_not(low_x) & has_x[1], high, 0.0)
        columns.append(jnp.where(has_y[side], total, 0.0))
    for a in range(5):
        for i in range(3):
            for c in range(5):
                q = a * 15 + i * 5 + c
                n = i * 125 + a * 25 + c
                force[n] += jnp.where(lane == 0, pltpu.roll(columns[0], (128 - q) % 128, 1), 0.0)
                force[n + 20] += jnp.where(lane == 127, pltpu.roll(columns[1], 127 - q, 1), 0.0)


def inverse_masses(density_ref, around, inverse):
    has_x, has_y = open_edges()
    lane, row = lane_row()
    low_x = row % 2 == 0
    low_z = row < 2

    def beside(mine, left, right):
        left = jnp.where(has_y[-1], left, 0.0)
        right = jnp.where(has_y[1], right, 0.0)
        before = jnp.where(lane == 0, pltpu.roll(left, 1, 1), pltpu.roll(mine, 1, 1))
        after = jnp.where(lane == 127, pltpu.roll(right, 127, 1), pltpu.roll(mine, 127, 1))
        return mine + before, mine, mine + after

    mine = beside(density_ref[...], around[0, -1][...], around[0, 1][...])
    low = beside(around[-1, 0][...], around[-1, -1][...], around[-1, 1][...])
    high = beside(around[1, 0][...], around[1, -1][...], around[1, 1][...])
    for b in range(3):
        lo = jnp.where(has_x[-1], low[b], 0.0)
        hi = jnp.where(has_x[1], high[b], 0.0)
        before = mine[b] + jnp.where(low_x, pltpu.roll(lo, 3, 0), pltpu.roll(mine[b], 1, 0))
        after = mine[b] + jnp.where(low_x, pltpu.roll(mine[b], 3, 0), pltpu.roll(hi, 1, 0))
        for a, value in enumerate((before, mine[b], after)):
            top = value + jnp.where(low_z, 0.0, pltpu.roll(value, 2, 0))
            bottom = value + jnp.where(low_z, pltpu.roll(value, 2, 0), 0.0)
            for c, total in enumerate((top, value, bottom)):
                inverse[a * 9 + b * 3 + c] = (solid_dt * solid_dt) / total


def kind(node):
    return 0 if node == 0 else 2 if node == 4 else 1


def advance_solid(force, load, inverse, now_ref, before_ref, out_ref):
    def component(i, carry):
        for a in range(5):
            for b in range(5):
                for c in range(5):
                    n = a * 25 + b * 5 + c
                    f = force[i * 125 + n]
                    if c == 0:
                        f = f + load[i * 25 + a * 5 + b]
                    w = np.float32(1.0 / (gll_weights[a] * gll_weights[b] * gll_weights[c]))
                    step = (inverse[kind(a) * 9 + kind(b) * 3 + kind(c)] * w) * f
                    at = i * 125 + n
                    out_ref[at] = (now_ref[at] + now_ref[at] - before_ref[at]) + step
        return carry

    lax.fori_loop(0, 3, component, 0)


def load_grid():
    row = lax.broadcasted_iota(jnp.int32, (56, 128), 0)
    lane = lax.broadcasted_iota(jnp.int32, (56, 128), 1)
    return row, lane


def rows_up(x, by):
    return jnp.concatenate([x[by:], jnp.zeros((by, 128), jnp.float32)], axis=0)


def rows_down(x, by):
    return jnp.concatenate([jnp.zeros((by, 128), jnp.float32), x[:-by]], axis=0)


def masks_x():
    row, lane = load_grid()
    even = row % 2 == 0
    odd = row % 2 == 1
    return (row < 10) & even, (row < 10) & odd, (row >= 40) & (row < 50) & even, (row >= 40) & (row < 50) & odd


def masks_y():
    row, lane = load_grid()
    place = row % 10
    return (place < 2) & (row < 50), (place >= 8) & (row < 50), lane == 0, lane == 127


def join_x(x):
    near_even, near_odd, far_even, far_odd = masks_x()
    return (
        x
        + jnp.where(near_odd, pltpu.roll(rows_up(x, 40), 1, 0), 0.0)
        + jnp.where(far_even, pltpu.roll(rows_down(x, 40), 55, 0), 0.0)
    )


def join_x_wide(own, halo):
    near_even, near_odd, far_even, far_odd = masks_x()
    own_new = join_x(own)
    own_new = own_new + jnp.where(near_even, rows_up(halo, 40), 0.0)
    own_new = own_new + jnp.where(far_odd, rows_down(halo, 40), 0.0)
    halo_new = halo + jnp.where(far_even, rows_down(own, 40), 0.0)
    halo_new = halo_new + jnp.where(near_odd, rows_up(own, 40), 0.0)
    return own_new, halo_new


def join_y(x, sides):
    near, far, first, final = masks_y()
    before, after = pltpu.roll(x, 1, 1), pltpu.roll(x, 127, 1)
    fill_before = 0.0 if sides is None else pltpu.roll(sides, 1, 1)
    fill_after = 0.0 if sides is None else pltpu.roll(sides, 127, 1)
    out = x + jnp.where(near, rows_up(jnp.where(first, fill_before, before), 8), 0.0)
    out = out + jnp.where(far, rows_down(jnp.where(final, fill_after, after), 8), 0.0)
    if sides is None:
        return out
    new = sides + jnp.where(far & final, rows_down(after, 8), 0.0)
    new = new + jnp.where(near & first, rows_up(before, 8), 0.0)
    return out, new


def columns_from(tile):
    row, lane = load_grid()
    turned = jnp.concatenate([tile, jnp.zeros((120, 128), jnp.float32)], axis=0).T
    out = []
    for k in range(3):
        halves = []
        for h in range(2):
            part = turned[64 * h : 64 * h + 56]
            left = pltpu.roll(part, 127 - 2 * k, 1)
            right = pltpu.roll(part, (128 - 2 * k - 1) % 128, 1)
            value = jnp.where(lane == 127, left, jnp.where(lane == 0, right, 0.0))
            halves.append(jnp.where(row < 50, value, 0.0))
        out.append(halves)
    return out


def columns_to(columns):
    lane = lax.broadcasted_iota(jnp.int32, (128, 128), 1)
    total = jnp.zeros((128, 128), jnp.float32)
    for k in range(3):
        pad = jnp.zeros((8, 128), jnp.float32)
        x = jnp.concatenate([columns[k][0], pad, columns[k][1], pad], axis=0)
        total = jnp.where(lane == 2 * k, pltpu.roll(x, 2 * k + 1, 1), total)
        total = jnp.where(lane == 2 * k + 1, pltpu.roll(x, 2 * k + 1, 1), total)
    return total.T[:8]


def load_parts(table, own_ref, beyond_ref, sides_ref):
    row, lane = load_grid()
    line_of = lax.broadcasted_iota(jnp.int32, (8, 128), 0)
    raw = jnp.zeros((8, 128), jnp.float32)
    for k in range(3):
        for side in range(2):
            last = jnp.broadcast_to(table[k][50:51, 128 * side : 128 * side + 128], (8, 128))
            raw = jnp.where(line_of == 2 * k + side, last, raw)
    columns = columns_from(raw)
    new_columns = []
    for k in range(3):
        own = jnp.where(row < 50, table[k][:56, :128], 0.0)
        halo = jnp.where(row < 50, table[k][:56, 128:], 0.0)
        own, halo = join_x_wide(own, halo)
        sides = join_x_wide(columns[k][0], columns[k][1])
        own, side_own = join_y(own, sides[0])
        halo, side_halo = join_y(halo, sides[1])
        own_ref[k] = own
        beyond_ref[k] = halo
        new_columns.append((side_own, side_halo))
    sides_ref[...] = columns_to(new_columns)


def load_total(own_ref, got_x, got_y, load):
    has_x, has_y = open_edges()
    row, lane = load_grid()
    even = row % 2 == 0
    tile_lane = lax.broadcasted_iota(jnp.int32, (8, 128), 1)
    tile_row = lax.broadcasted_iota(jnp.int32, (8, 128), 0)
    ends = []
    for side in (-1, 1):
        low = jnp.where(has_x[-1], pltpu.roll(got_y[-1, side][...], 127, 1), 0.0)
        high = jnp.where(has_x[1], pltpu.roll(got_y[1, side][...], 1, 1), 0.0)
        tile = jnp.where(tile_lane < 64, got_y[0, side][...], jnp.where(tile_lane % 2 == 0, low, high))
        ends.append(jnp.where(has_y[side], tile, 0.0))
    columns = columns_from(jnp.where(tile_row % 2 == 0, ends[1], ends[0]))
    for k in range(3):
        low = jnp.where(has_x[-1], pltpu.roll(got_x[0][k], 55, 0), 0.0)
        high = jnp.where(has_x[1], pltpu.roll(got_x[1][k], 1, 0), 0.0)
        rows = jnp.where(even, low, high) + join_y(columns[k][1], None)
        total = own_ref[k] + join_x(jnp.where(row < 50, rows, 0.0)) + join_y(columns[k][0], None)
        for n in range(25):
            load[k * 25 + n] = jnp.concatenate(
                [total[2 * n : 2 * n + 2], jnp.zeros((2, 128), jnp.float32)], axis=0
            )


AROUND = [(-1, 0), (1, 0), (0, -1), (0, 1), (-1, -1), (-1, 1), (1, -1), (1, 1)]
ASIDE = AROUND[2:]


def shape(*dims, kind=jnp.float32):
    return jax.ShapeDtypeStruct(dims, kind)


def halo_plan(rows, cols):
    edge_rows = {-1: pl.ds(0, 4), 1: pl.ds(rows - 4, 4)}
    edge_cols = {-1: pl.ds(0, 128), 1: pl.ds(cols - 128, 128)}
    place_rows = {-1: pl.ds(0, 4), 1: pl.ds(4, 4)}
    messages = []
    for source in range(3):
        every = (slice(None),) if source == 0 else ()
        for dx, dy in AROUND:
            row_in = edge_rows.get(dx, pl.ds(0, rows))
            row_out = place_rows.get(dx, pl.ds(0, rows))
            col_in = edge_cols.get(dy, pl.ds(0, cols))
            where = 0 if dy == 0 else (1 if dx == 0 else 3) + (0 if dy == 1 else 1)
            messages.append(
                (source, every + (row_in, col_in), 5 * source + where,
                 every + (row_out, pl.ds(0, cols if dy == 0 else 128)), (dx, dy))
            )
    return messages


def whole_body(*refs):
    (flow_in, drag_in, wet_in, elem_in, node_in, u_in, before_in, density_in, lame_in, shear_in) = refs[:10]
    fields_out, next_out, last_out = refs[10:13]
    (ext, drag, buoy, scale, tract, row_slot, col_slot, table) = refs[13:21]
    halos = refs[21:36]
    (drag_own, wet_own, elem_own, node_own) = refs[36:40]
    (u_zero, before, u_one, u_two, force, stress, load, inverse) = refs[40:48]
    (density, lame, shear, around) = refs[48:52]
    (face_x, face_y, got_face_x, got_face_y) = refs[52:56]
    (own, beyond, sides, got_beyond, got_sides) = refs[56:61]
    local_sem, sent, come = refs[61:]
    rows, cols = drag_own.shape
    at_x, at_y = lax.axis_index("gx"), lax.axis_index("gy")
    size_x, size_y = lax.axis_size("gx"), lax.axis_size("gy")

    def device(move):
        return ((at_x + move[0] + size_x) % size_x, (at_y + move[1] + size_y) % size_y)

    def opposite(move):
        return -move[0], -move[1]

    barrier = pltpu.get_barrier_semaphore()
    for move in AROUND:
        pl.semaphore_signal(barrier, inc=1, device_id=device(move), device_id_type=pl.DeviceIdType.MESH)
    reads = [
        pltpu.make_async_copy(source, target, local_sem.at[n])
        for n, (source, target) in enumerate(
            (
                (u_in, u_zero), (lame_in, lame), (shear_in, shear), (density_in, density),
                (flow_in, ext.at[0, :, 0:rows, 0:cols]), (drag_in, drag_own), (wet_in, wet_own),
                (elem_in, elem_own), (node_in, node_own), (before_in, before),
            )
        )
    ]
    for copy in reads:
        copy.start()
    store_fields = pltpu.make_async_copy(ext.at[0, :, 0:rows, 0:cols], fields_out, local_sem.at[10])
    store_last = pltpu.make_async_copy(u_one, last_out, local_sem.at[11])
    store_next = pltpu.make_async_copy(u_two, next_out, local_sem.at[12])
    pl.semaphore_wait(barrier, len(AROUND))
    number = [0]

    def send(source, target, move):
        n = number[0]
        number[0] += 1
        copy = pltpu.make_async_remote_copy(
            src_ref=source, dst_ref=target, send_sem=sent.at[n], recv_sem=come.at[n],
            device_id=device(move), device_id_type=pl.DeviceIdType.MESH,
        )
        copy.start()
        return copy

    operands = (flow_in, drag_in, wet_in)
    first = [
        send(operands[source].at[source_at], halos[target].at[target_at], move)
        for source, source_at, target, target_at, move in halo_plan(rows, cols)
    ]
    first += [send(density_in, around.at[AROUND.index(opposite(move))], move) for move in AROUND]

    def send_faces(step):
        copies = [send(face_x.at[step], got_face_x.at[step, 1], (-1, 0))]
        copies += [send(face_x.at[step], got_face_x.at[step, 0], (1, 0))]
        for move in ASIDE:
            copies.append(send(face_y.at[step], got_face_y.at[step, ASIDE.index(opposite(move))], move))
        return copies

    def faces_of(step):
        return (
            [got_face_x.at[step, n] for n in range(2)],
            {move: got_face_y.at[step, n] for n, move in enumerate(ASIDE)},
        )

    for copy in reads[:3]:
        copy.wait()
    internal_local(u_zero, lame, shear, stress, force)
    pack_faces(force, face_x.at[0], face_y.at[0])
    faces = send_faces(0)
    for copy in reads[3:] + first:
        copy.wait()
    inverse_masses(density, {move: around.at[n] for n, move in enumerate(AROUND)}, inverse)
    surface(
        drag_own, wet_own, elem_own, node_own, (halos[0:5], halos[5:10], halos[10:15]),
        own, beyond, sides, ext, drag, buoy, scale, tract, row_slot, col_slot, table, store_fields,
    )
    loads = [send(beyond, got_beyond.at[1], (-1, 0)), send(beyond, got_beyond.at[0], (1, 0))]
    for move in ASIDE:
        loads.append(send(sides, got_sides.at[ASIDE.index(opposite(move))], move))
    for copy in faces:
        copy.wait()
    add_faces(force, *faces_of(0))
    for copy in loads:
        copy.wait()
    load_total(
        own,
        [got_beyond.at[n] for n in range(2)],
        {move: got_sides.at[n] for n, move in enumerate(ASIDE)},
        load,
    )
    advance_solid(force, load, inverse, u_zero, before, u_one)
    store_last.start()
    internal_local(u_one, lame, shear, stress, force)
    pack_faces(force, face_x.at[1], face_y.at[1])
    faces = send_faces(1)
    for copy in faces:
        copy.wait()
    add_faces(force, *faces_of(1))
    advance_solid(force, load, inverse, u_one, u_zero, u_two)
    store_next.start()
    store_fields.wait()
    store_last.wait()
    store_next.wait()


def store_body(*refs):
    sems = refs[6]
    copies = [pltpu.make_async_copy(refs[n], refs[3 + n], sems.at[n]) for n in range(3)]
    for copy in copies:
        copy.start()
    for copy in copies:
        copy.wait()


def per_device(
    flow_state,
    drag_coefficient,
    wet_mask,
    target_elem,
    target_node,
    displacement,
    previous,
    density,
    lame_first,
    shear_modulus,
):
    rows, cols = drag_coefficient.shape
    tall, wide = rows + 8, cols + 128
    grid = displacement.shape
    nodes = (375, 4, 128)
    halo_shapes = []
    for lead, kind_of in (((6,), jnp.float32), ((), jnp.float32), ((), jnp.int32)):
        for dims in ((8, cols), (rows, 128), (rows, 128), (8, 128), (8, 128)):
            halo_shapes.append(pltpu.VMEM((*lead, *dims), kind_of))

    def floats(*dims):
        return pltpu.VMEM(dims, jnp.float32)

    def integers(*dims):
        return pltpu.VMEM(dims, jnp.int32)

    scratch = [
        floats(2, 6, tall, wide), floats(tall, wide), floats(tall, wide), floats(tall, wide),
        floats(3, rows, cols), floats(rows, cols), floats(rows, cols), floats(320, 256),
        *halo_shapes,
        floats(rows, cols), integers(rows, cols), integers(rows, cols), integers(rows, cols),
        *[floats(*nodes)] * 6, floats(75, 4, 128), floats(27, 4, 128),
        floats(4, 128), floats(4, 128), floats(4, 128), floats(8, 4, 128),
        floats(2, 75, 4, 128), floats(2, 2, 4, 128), floats(2, 2, 75, 4, 128), floats(2, 6, 2, 4, 128),
        floats(3, 56, 128), floats(3, 56, 128), floats(8, 128), floats(2, 3, 56, 128), floats(6, 8, 128),
        pltpu.SemaphoreType.DMA((13,)), pltpu.SemaphoreType.DMA((56,)), pltpu.SemaphoreType.DMA((56,)),
    ]
    anywhere = pl.BlockSpec(memory_space=pl.ANY)
    results = pl.pallas_call(
        whole_body,
        out_shape=(shape(6, rows, cols), shape(*nodes), shape(*nodes)),
        in_specs=[anywhere] * 10,
        out_specs=(anywhere,) * 3,
        scratch_shapes=scratch,
        compiler_params=pltpu.CompilerParams(
            collective_id=1, has_side_effects=True, vmem_limit_bytes=56 * 2**20
        ),
    )(
        flow_state, drag_coefficient, wet_mask, target_elem, target_node,
        displacement.reshape(nodes), previous.reshape(nodes),
        *(x.reshape(4, 128) for x in (density, lame_first, shear_modulus)),
    )
    fields, u_two, u_one = pl.pallas_call(
        store_body,
        out_shape=tuple(shape(*x.shape) for x in results),
        in_specs=[anywhere] * 3,
        out_specs=(anywhere,) * 3,
        scratch_shapes=[pltpu.SemaphoreType.DMA((3,))],
    )(*results)
    return (fields, u_two.reshape(grid), u_one.reshape(grid))


def solution(mesh):
    return jax.shard_map(
        per_device,
        mesh=mesh,
        in_specs=(
            P(None, "gx", "gy"),
            P("gx", "gy"),
            P("gx", "gy"),
            P("gx", "gy"),
            P("gx", "gy"),
            P(None, None, None, None, None, "gx", "gy"),
            P(None, None, None, None, None, "gx", "gy"),
            P(None, "gx", "gy"),
            P(None, "gx", "gy"),
            P(None, "gx", "gy"),
        ),
        out_specs=(
            P(None, "gx", "gy"),
            P(None, None, None, None, None, "gx", "gy"),
            P(None, None, None, None, None, "gx", "gy"),
        ),
        check_vma=False,
    )
```

```python
import jax
import jax.numpy as jnp
import numpy as np
from jax import lax
from jax.experimental import pallas as pl
from jax.experimental.pallas import tpu as pltpu
from jax.sharding import PartitionSpec as P

FLOW_STEPS = 4
SOLID_STEPS = 2
SLOT_ROWS = 51
GROUP = 8


gll_points = np.array([-1.0, -np.sqrt(3.0 / 7.0), 0.0, np.sqrt(3.0 / 7.0), 1.0])
gll_weights = np.array([0.1, 49.0 / 90.0, 32.0 / 45.0, 49.0 / 90.0, 0.1])
flow_dt = 0.4
diffusion = 0.2
coupling = 0.5
upper_gravity = 0.8
density_ratio = 0.7
speed_floor = 0.0001
load_factor = 4.0
solid_dt = 0.04


def legendre_four(x):
    return (35.0 * x**4 - 30.0 * x**2 + 3.0) / 8.0


def derivative_table():
    result = np.zeros((5, 5))
    for i in range(5):
        for j in range(5):
            if i != j:
                result[i, j] = (
                    legendre_four(gll_points[i])
                    / legendre_four(gll_points[j])
                    / (gll_points[i] - gll_points[j])
                )
    result[0, 0] = -5.0
    result[4, 4] = 5.0
    return result


def surface(
    drag_ref, wet_ref, elem_ref, node_ref, arrive, got, own_ref, beyond_ref, sides_ref,
    ext, drag, buoy, scale, tract, row_slot, col_slot, table_ref, store_fields,
):
    rows, cols = drag_ref.shape
    wide = cols + 128
    tall = rows + 8
    at_x, at_y = lax.axis_index("gx"), lax.axis_index("gy")
    last_x, last_y = lax.axis_size("gx") - 1, lax.axis_size("gy") - 1

    def wetness(x):
        return 1.0 - 0.6 * x

    def own_cells(t, carry):
        at = pl.ds(pl.multiple_of(t * 128, 128), 128)
        drag[0:rows, at] = drag_ref[:, at]
        buoy[0:rows, at] = wetness(wet_ref[:, at].astype(jnp.float32))
        e = elem_ref[:, at]
        n = node_ref[:, at]
        surface_cols = 128 * (last_y + 1)
        er = e // surface_cols
        lx = er - 2 * at_x + 1
        ly = (e - er * surface_cols) - 128 * at_y + 1
        inside = (ly >= 1) & (ly <= 128)
        own_row = (lx == 1) | (lx == 2)
        half = jnp.where(own_row, 0, 1)
        line = 2 * n + jnp.where(lx >= 2, 1, 0)
        a = jnp.where(inside, line, 50)
        b = jnp.where(
            inside,
            half * 128 + ly - 1,
            jnp.where(ly == 0, 0, 128) + 64 * half + line,
        )
        row_slot[:, at] = a.astype(jnp.float32)
        col_slot[:, at] = b.astype(jnp.float32)
        return carry

    lax.fori_loop(0, cols // 128, own_cells, 0)
    arrive()

    sub = lax.broadcasted_iota(jnp.int32, (8, 128), 0)
    lane = lax.broadcasted_iota(jnp.int32, (8, 128), 1)
    up_half = sub < 4
    left_half = lane < 64

    def zero_rows(tile):
        tile = jnp.where(up_half & (at_x == last_x), 0.0, tile)
        return jnp.where(jnp.logical_not(up_half) & (at_x == 0), 0.0, tile)

    def zero_cols(tile):
        tile = jnp.where(left_half & (at_y == last_y), 0.0, tile)
        return jnp.where(jnp.logical_not(left_half) & (at_y == 0), 0.0, tile)

    def received(k, n, *at):
        if k < 6:
            return got[0][n][(k, *at)]
        tile = got[k - 5][n][at]
        return tile if k == 6 else tile.astype(jnp.float32)

    def place(k, r, c, tile):
        if k < 6:
            ext[0, k, r, c] = tile
        elif k == 6:
            drag[r, c] = tile
        else:
            buoy[r, c] = wetness(tile)

    tail = pl.ds(cols, 128)
    foot = pl.ds(rows, 8)
    ones = jnp.full((8, 128), 0.2, jnp.float32)
    row_scale = zero_rows(ones)
    col_scale = zero_cols(ones)

    def halo_rows(t, carry):
        at = pl.ds(pl.multiple_of(t * 128, 128), 128)
        for k in range(8):
            place(k, foot, at, zero_rows(received(k, 0, slice(None), at)))
        for r in range(0, rows, 8):
            scale[r : r + 8, at] = ones
        scale[foot, at] = row_scale
        return carry

    lax.fori_loop(0, cols // 128, halo_rows, 0)
    for k in range(8):
        for r in range(0, rows, 8):
            at = (slice(r, r + 8), slice(None))
            tile = jnp.where(left_half, received(k, 2, *at), received(k, 1, *at))
            place(k, pl.ds(r, 8), tail, zero_cols(tile))
        at = (slice(None), slice(None))
        tile = jnp.where(left_half, received(k, 4, *at), received(k, 3, *at))
        place(k, foot, tail, zero_cols(zero_rows(tile)))
    for r in range(0, rows, 8):
        scale[r : r + 8, tail] = col_scale
    scale[foot, tail] = zero_cols(row_scale)

    lanes = lax.broadcasted_iota(jnp.int32, (tall, 128), 1)
    first_lane = lanes == 0
    last_lane = lanes == 127
    tiles = wide // 128

    def press(f0, f1, b):
        return b * (f0 + f1), upper_gravity * density_ratio * f0 + upper_gravity * f1

    def step(now, carry):
        later = 1 - now

        def tile_step(t, carry):
            at = pl.ds(pl.multiple_of(t * 128, 128), 128)
            t_hi = jnp.where(t == tiles - 1, 0, t + 1)
            t_lo = jnp.where(t == 0, tiles - 1, t - 1)
            at_hi = pl.ds(pl.multiple_of(t_hi * 128, 128), 128)
            at_lo = pl.ds(pl.multiple_of(t_lo * 128, 128), 128)
            f = [ext[now, k, :, at] for k in range(6)]
            b = buoy[:, at]
            one, two = press(f[0], f[1], b)
            sums = [None] * 6

            def add(k, value):
                sums[k] = value if sums[k] is None else sums[k] + value

            for ahead in (True, False):
                by = tall - 1 if ahead else 1
                def rolled(x):
                    return pltpu.roll(x, by, 0)
                sg = -1.0 if ahead else 1.0
                def mix(x, y):
                    return x - y if ahead else x + y
                add(0, rolled(mix(f[0], f[2])))
                add(1, rolled(mix(f[1], f[4])))
                add(2, rolled(mix(f[2], one)))
                add(3, rolled(f[3]))
                add(4, rolled(mix(f[4], two)))
                add(5, rolled(f[5]))
            for ahead in (True, False):
                by = 127 if ahead else 1
                edge = first_lane if ahead else last_lane
                other = at_hi if ahead else at_lo
                g = [jnp.where(edge, ext[now, k, :, other], f[k]) for k in range(6)]
                gb = jnp.where(edge, buoy[:, other], b)
                g_one, g_two = press(g[0], g[1], gb)
                def rolled(x):
                    return pltpu.roll(x, by, 1)
                def mix(x, y):
                    return x - y if ahead else x + y
                add(0, rolled(mix(g[0], g[3])))
                add(1, rolled(mix(g[1], g[5])))
                add(2, rolled(g[2]))
                add(3, rolled(mix(g[3], g_one)))
                add(4, rolled(g[4]))
                add(5, rolled(mix(g[5], g_two)))
            speed = jnp.sqrt(f[2] * f[2] + f[3] * f[3] + speed_floor)
            rub = 2.0 * drag[:, at] * speed
            k = scale[:, at]
            ext[later, 0, :, at] = k * (f[0] + sums[0])
            ext[later, 1, :, at] = k * (f[1] + sums[1])
            ext[later, 2, :, at] = k * (sums[2] + f[4] - rub * f[2])
            ext[later, 3, :, at] = k * (sums[3] + f[5] - rub * f[3])
            ext[later, 4, :, at] = k * (sums[4] + f[2])
            ext[later, 5, :, at] = k * (sums[5] + f[3])
            return carry

        return lax.fori_loop(0, tiles, tile_step, carry, unroll=True)

    lax.fori_loop(0, FLOW_STEPS // 2, lambda _, carry: step(1, step(0, carry)), 0)
    store_fields.start()

    def pull(t, carry):
        at = pl.ds(pl.multiple_of(t * 128, 128), 128)
        f = [ext[0, k, 0:rows, at] for k in range(4)]
        rub = load_factor * drag[0:rows, at] * jnp.sqrt(f[2] * f[2] + f[3] * f[3] + speed_floor)
        tract[0, :, at] = rub * f[2]
        tract[1, :, at] = rub * f[3]
        tract[2, :, at] = -load_factor * (buoy[0:rows, at] * (f[0] + f[1]))
        return carry

    lax.fori_loop(0, cols // 128, pull, 0)

    table_ref[...] = jnp.zeros_like(table_ref)
    narrow = jnp.bfloat16
    row16 = lax.broadcasted_iota(jnp.int32, (16, cols), 0)
    count = row16.astype(jnp.float32).astype(narrow)

    def spread(group, carry):
        lefts, rights = [], []
        for n in range(GROUP):
            line = pl.ds(group * GROUP + n, 1)

            def wide16(x):
                return jnp.broadcast_to(x, (16, cols)).astype(narrow)

            parts = []
            for k in range(3):
                value = tract[k, line, :]
                high = value.astype(narrow).astype(jnp.float32)
                parts.append(wide16(value))
                parts.append(wide16(value - high))
            a = wide16(row_slot[line, :])
            b = wide16(col_slot[line, :])
            zero = jnp.zeros((16, cols), narrow)
            one = jnp.ones((16, cols), narrow)
            pieces = []
            for top in range(0, table_ref.shape[0], 16):
                part, last = top // SLOT_ROWS, min((top + 15) // SLOT_ROWS, 5)
                skip = top - SLOT_ROWS * part
                if part == last:
                    pieces.append(jnp.where(a == count + narrow(skip), parts[part], zero))
                else:
                    split = SLOT_ROWS * last - top
                    target = row16 + jnp.where(row16 < split, skip, -split)
                    mixed = jnp.where(count < narrow(split), parts[part], parts[last])
                    pieces.append(jnp.where(a == target.astype(jnp.float32).astype(narrow), mixed, zero))
            lefts.append(jnp.concatenate(pieces, axis=0))
            rights.append(
                jnp.concatenate([jnp.where(b == count + narrow(16 * m), one, zero) for m in range(16)], axis=0)
            )
        table_ref[...] += lax.dot_general(
            jnp.concatenate(lefts, axis=1),
            jnp.concatenate(rights, axis=1),
            (((1,), (1,)), ((), ())),
            preferred_element_type=jnp.float32,
        )
        return carry

    lax.fori_loop(0, rows // GROUP, spread, 0)

    def part_rows(n):
        return table_ref[SLOT_ROWS * n : SLOT_ROWS * n + SLOT_ROWS]

    pad = jnp.zeros((64 - SLOT_ROWS, 256), jnp.float32)
    table = [
        jnp.concatenate([part_rows(2 * k) + part_rows(2 * k + 1), pad], axis=0) for k in range(3)
    ]
    load_parts(table, own_ref, beyond_ref, sides_ref)


def line(matrix, s):
    even = [s[0] + s[4], s[1] + s[3]]
    odd = [s[0] - s[4], s[1] - s[3]]
    out = [None] * 5
    for a in range(2):
        half_sum = [0.5 * (matrix[a, p] - matrix[a, 4 - p]) for p in range(2)]
        half_diff = [0.5 * (matrix[a, p] + matrix[a, 4 - p]) for p in range(2)]
        x = float(half_sum[0]) * odd[0] + float(half_sum[1]) * odd[1]
        y = float(half_diff[0]) * even[0] + float(half_diff[1]) * even[1] + float(matrix[a, 2]) * s[2]
        out[a] = x + y
        out[4 - a] = x - y
    out[2] = float(matrix[2, 0]) * odd[0] + float(matrix[2, 1]) * odd[1]
    return out


def lane_row():
    lane = lax.broadcasted_iota(jnp.int32, (4, 128), 1)
    row = lax.broadcasted_iota(jnp.int32, (4, 128), 0)
    return lane, row


def internal_open(u_ref, lame_ref, shear_ref, stress, force):
    table = derivative_table()

    def slope_x(m, carry):
        for i in range(3):
            lines = line(table, [u_ref[i * 125 + a * 25 + m] for a in range(5)])
            for a in range(5):
                stress[i * 125 + a * 25 + m] = lines[a]
        return carry

    lax.fori_loop(0, 25, slope_x, 0)

    def plane(a, carry):
        weight = jnp.where(
            (a == 0) | (a == 4),
            np.float32(gll_weights[0]),
            jnp.where(a == 2, np.float32(gll_weights[2]), np.float32(gll_weights[1])),
        )
        lame = lame_ref[...] * -weight
        shear = shear_ref[...] * -weight

        def at(i, b, c):
            return i * 125 + a * 25 + b * 5 + c

        slope_y, slope_z = [], []
        for i in range(3):
            u = [[u_ref[at(i, b, c)] for c in range(5)] for b in range(5)]
            along_y = [line(table, [u[b][c] for b in range(5)]) for c in range(5)]
            slope_y.append([[along_y[c][b] for c in range(5)] for b in range(5)])
            slope_z.append([line(table, u[b]) for b in range(5)])
        pull_y = [[[None] * 5 for b in range(5)] for i in range(3)]
        pull_z = [[[None] * 5 for b in range(5)] for i in range(3)]
        for b in range(5):
            for c in range(5):
                w = np.float32(gll_weights[b] * gll_weights[c])
                g = [[stress[at(i, b, c)], slope_y[i][b][c], slope_z[i][b][c]] for i in range(3)]
                mu = shear * w
                twice = mu + mu
                spread = (lame * w) * (g[0][0] + g[1][1] + g[2][2])
                s00 = spread + twice * g[0][0]
                s11 = spread + twice * g[1][1]
                s22 = spread + twice * g[2][2]
                s01 = mu * (g[0][1] + g[1][0])
                s02 = mu * (g[0][2] + g[2][0])
                s12 = mu * (g[1][2] + g[2][1])
                stress[at(0, b, c)] = s00
                stress[at(1, b, c)] = s01
                stress[at(2, b, c)] = s02
                for i, (s_y, s_z) in enumerate(((s01, s02), (s11, s12), (s12, s22))):
                    pull_y[i][b][c] = s_y
                    pull_z[i][b][c] = s_z
        for i in range(3):
            along_y = [line(table.T, [pull_y[i][b][c] for b in range(5)]) for c in range(5)]
            for b in range(5):
                along_z = line(table.T, pull_z[i][b])
                for c in range(5):
                    force[at(i, b, c)] = along_y[c][b] + along_z[c]
        return carry

    lax.fori_loop(0, 5, plane, 0)


def internal_kick(kick, lame_ref, shear_ref, force):
    table = derivative_table()
    lame, shear = -lame_ref[...], -shear_ref[...]
    five = range(5)

    def grid(make):
        return [[make(a, b) for b in five] for a in five]

    def along_x(matrix, x):
        lines = [line(matrix, [x[a][b] for a in five]) for b in five]
        return grid(lambda a, b: lines[b][a])

    def along_y(matrix, x):
        lines = [line(matrix, x[a]) for a in five]
        return grid(lambda a, b: lines[a][b])

    def plus(x, y):
        return grid(lambda a, b: x[a][b] + y[a][b])

    def area(a, b):
        return np.float32(gll_weights[a] * gll_weights[b])

    d = [grid(lambda a, b: kick[i * 25 + a * 5 + b]) for i in range(3)]
    d_x = [along_x(table, x) for x in d]
    d_y = [along_y(table, x) for x in d]
    lame_w = grid(lambda a, b: lame * area(a, b))
    shear_w = grid(lambda a, b: shear * area(a, b))
    t_side = grid(lambda a, b: lame_w[a][b] * d[2][a][b])
    t_02 = grid(lambda a, b: shear_w[a][b] * d[0][a][b])
    t_12 = grid(lambda a, b: shear_w[a][b] * d[1][a][b])
    t_22 = grid(lambda a, b: t_side[a][b] + (shear_w[a][b] + shear_w[a][b]) * d[2][a][b])
    first = np.float32(gll_weights[0])
    l_0 = grid(lambda a, b: first * lame_w[a][b])
    m_0 = grid(lambda a, b: first * shear_w[a][b])
    e_22 = grid(lambda a, b: l_0[a][b] * (d_x[0][a][b] + d_y[1][a][b]))
    e_00 = grid(lambda a, b: e_22[a][b] + (m_0[a][b] + m_0[a][b]) * d_x[0][a][b])
    e_11 = grid(lambda a, b: e_22[a][b] + (m_0[a][b] + m_0[a][b]) * d_y[1][a][b])
    e_01 = grid(lambda a, b: m_0[a][b] * (d_y[0][a][b] + d_x[1][a][b]))
    e_02 = grid(lambda a, b: m_0[a][b] * d_x[2][a][b])
    e_12 = grid(lambda a, b: m_0[a][b] * d_y[2][a][b])
    turned = table.T
    pulled = (
        along_x(turned, t_side),
        along_y(turned, t_side),
        plus(along_x(turned, t_02), along_y(turned, t_12)),
    )
    flat = (
        plus(along_x(turned, e_00), along_y(turned, e_01)),
        plus(along_x(turned, e_01), along_y(turned, e_11)),
        plus(along_x(turned, e_02), along_y(turned, e_12)),
    )
    share = [float(table[c, 0] * gll_weights[c]) for c in five]
    upright = [float(sum(table[p, c] * share[p] for p in five)) for c in five]
    for i, (t, e) in enumerate(((t_02, e_02), (t_12, e_12), (t_22, e_22))):
        for a in five:
            for b in five:
                for c in five:
                    value = share[c] * pulled[i][a][b] + upright[c] * t[a][b]
                    value = value + float(table[0, c]) * e[a][b]
                    if c == 0:
                        value = value + flat[i][a][b]
                    force[i * 125 + a * 25 + b * 5 + c] += value


def internal_close(stress, force):
    table = derivative_table()
    lane, row = lane_row()
    low_x = row % 2 == 0
    low_z = row < 2

    def close_x(m, carry):
        for i in range(3):
            pulled = line(table.T, [stress[i * 125 + a * 25 + m] for a in range(5)])
            f = [force[i * 125 + a * 25 + m] + pulled[a] for a in range(5)]
            near = f[0] + jnp.where(low_x, 0.0, pltpu.roll(f[4], 1, 0))
            far = f[4] + jnp.where(low_x, pltpu.roll(f[0], 3, 0), 0.0)
            for a, value in enumerate((near, f[1], f[2], f[3], far)):
                force[i * 125 + a * 25 + m] = value
        return carry

    lax.fori_loop(0, 25, close_x, 0)

    def close_yz(ia, carry):
        base = ia * 25
        f = [[force[base + b * 5 + c] for c in range(5)] for b in range(5)]
        for c in range(5):
            near, far = f[0][c], f[4][c]
            f[0][c] = near + jnp.where(lane == 0, 0.0, pltpu.roll(far, 1, 1))
            f[4][c] = far + jnp.where(lane == 127, 0.0, pltpu.roll(near, 127, 1))
        for b in range(5):
            near, far = f[b][0], f[b][4]
            f[b][0] = near + jnp.where(low_z, 0.0, pltpu.roll(far, 2, 0))
            f[b][4] = far + jnp.where(low_z, pltpu.roll(near, 2, 0), 0.0)
        for b in range(5):
            for c in range(5):
                if b in (0, 4) or c in (0, 4):
                    force[base + b * 5 + c] = f[b][c]
        return carry

    lax.fori_loop(0, 15, close_yz, 0)


def pack_faces(force, face_x, face_y):
    lane, row = lane_row()
    low_x = row % 2 == 0

    def both(m, other):
        for i in range(3):
            near, far = force[i * 125 + m], force[i * 125 + 100 + m]
            near_other, far_other = force[i * 125 + other], force[i * 125 + 100 + other]
            face_x[0, i * 13 + m] = jnp.where(low_x, near, pltpu.roll(near_other, 1, 0))
            face_x[1, i * 13 + m] = jnp.where(low_x, pltpu.roll(far, 3, 0), far_other)

    def pack_x(m, carry):
        both(m, m + 13)
        return carry

    lax.fori_loop(0, 12, pack_x, 0)
    both(12, 12)
    ends = [jnp.zeros((4, 128), jnp.float32)] * 2
    for a in range(5):
        for i in range(3):
            for c in range(5):
                q = a * 15 + i * 5 + c
                n = i * 125 + a * 25 + c
                ends[0] = jnp.where(lane == q, pltpu.roll(force[n], q, 1), ends[0])
                ends[1] = jnp.where(lane == q, pltpu.roll(force[n + 20], q + 1, 1), ends[1])
    face_y[0] = ends[0]
    face_y[1] = ends[1]


def open_edges():
    at_x, at_y = lax.axis_index("gx"), lax.axis_index("gy")
    has = {-1: at_x > 0, 1: at_x < lax.axis_size("gx") - 1}
    has_y = {-1: at_y > 0, 1: at_y < lax.axis_size("gy") - 1}
    return has, has_y


def add_faces(force, got_x, got_y):
    has_x, has_y = open_edges()
    lane, row = lane_row()
    low_x = row % 2 == 0

    def one(m, other):
        for i in range(3):
            low, high = got_x[0][i * 13 + m], got_x[1][i * 13 + m]
            force[i * 125 + m] += jnp.where(low_x & has_x[-1], low, 0.0)
            force[i * 125 + 100 + m] += jnp.where(low_x | jnp.logical_not(has_x[1]), 0.0, pltpu.roll(high, 1, 0))
            if other is not None:
                low = jnp.where(low_x & has_x[-1], pltpu.roll(low, 3, 0), 0.0)
                high = jnp.where(low_x | jnp.logical_not(has_x[1]), 0.0, high)
                force[i * 125 + other] += low
                force[i * 125 + 100 + other] += high

    def add_x(m, carry):
        one(m, m + 13)
        return carry

    lax.fori_loop(0, 12, add_x, 0)
    one(12, None)
    first, final = lane < 15, (lane >= 60) & (lane < 75)
    columns = []
    for side, end in ((-1, 1), (1, 0)):
        straight = got_y[0, side][end]
        low = pltpu.roll(pltpu.roll(got_y[-1, side][end], 68, 1), 3, 0)
        high = pltpu.roll(pltpu.roll(got_y[1, side][end], 60, 1), 1, 0)
        total = straight + jnp.where(first & low_x & has_x[-1], low, 0.0)
        total = total + jnp.where(final & jnp.logical_not(low_x) & has_x[1], high, 0.0)
        columns.append(jnp.where(has_y[side], total, 0.0))
    for a in range(5):
        for i in range(3):
            for c in range(5):
                q = a * 15 + i * 5 + c
                n = i * 125 + a * 25 + c
                force[n] += jnp.where(lane == 0, pltpu.roll(columns[0], (128 - q) % 128, 1), 0.0)
                force[n + 20] += jnp.where(lane == 127, pltpu.roll(columns[1], 127 - q, 1), 0.0)


def inverse_masses(density_ref, around, inverse):
    has_x, has_y = open_edges()
    lane, row = lane_row()
    low_x = row % 2 == 0
    low_z = row < 2

    def beside(mine, left, right):
        left = jnp.where(has_y[-1], left, 0.0)
        right = jnp.where(has_y[1], right, 0.0)
        before = jnp.where(lane == 0, pltpu.roll(left, 1, 1), pltpu.roll(mine, 1, 1))
        after = jnp.where(lane == 127, pltpu.roll(right, 127, 1), pltpu.roll(mine, 127, 1))
        return mine + before, mine, mine + after

    mine = beside(density_ref[...], around[0, -1][...], around[0, 1][...])
    low = beside(around[-1, 0][...], around[-1, -1][...], around[-1, 1][...])
    high = beside(around[1, 0][...], around[1, -1][...], around[1, 1][...])
    for b in range(3):
        lo = jnp.where(has_x[-1], low[b], 0.0)
        hi = jnp.where(has_x[1], high[b], 0.0)
        before = mine[b] + jnp.where(low_x, pltpu.roll(lo, 3, 0), pltpu.roll(mine[b], 1, 0))
        after = mine[b] + jnp.where(low_x, pltpu.roll(mine[b], 3, 0), pltpu.roll(hi, 1, 0))
        for a, value in enumerate((before, mine[b], after)):
            top = value + jnp.where(low_z, 0.0, pltpu.roll(value, 2, 0))
            bottom = value + jnp.where(low_z, pltpu.roll(value, 2, 0), 0.0)
            for c, total in enumerate((top, value, bottom)):
                inverse[a * 9 + b * 3 + c] = (solid_dt * solid_dt) / total


def kind(node):
    return 0 if node == 0 else 2 if node == 4 else 1


def advance_solid(force, load, inverse, now_ref, before_ref, out_ref):
    def component(i, carry):
        for a in range(5):
            for b in range(5):
                for c in range(5):
                    n = a * 25 + b * 5 + c
                    f = force[i * 125 + n]
                    if c == 0 and load is not None:
                        f = f + load[i * 25 + a * 5 + b]
                    w = np.float32(1.0 / (gll_weights[a] * gll_weights[b] * gll_weights[c]))
                    step = (inverse[kind(a) * 9 + kind(b) * 3 + kind(c)] * w) * f
                    at = i * 125 + n
                    out_ref[at] = (now_ref[at] + now_ref[at] - before_ref[at]) + step
        return carry

    lax.fori_loop(0, 3, component, 0)


def kick_solid(load, inverse, out_ref, kick):
    def component(i, carry):
        for a in range(5):
            for b in range(5):
                n = i * 25 + a * 5 + b
                w = np.float32(1.0 / (gll_weights[a] * gll_weights[b] * gll_weights[0]))
                step = (inverse[kind(a) * 9 + kind(b) * 3] * w) * load[n]
                kick[n] = step
                out_ref[i * 125 + a * 25 + b * 5] += step
        return carry

    lax.fori_loop(0, 3, component, 0)


def load_grid():
    row = lax.broadcasted_iota(jnp.int32, (56, 128), 0)
    lane = lax.broadcasted_iota(jnp.int32, (56, 128), 1)
    return row, lane


def rows_up(x, by):
    return jnp.concatenate([x[by:], jnp.zeros((by, 128), jnp.float32)], axis=0)


def rows_down(x, by):
    return jnp.concatenate([jnp.zeros((by, 128), jnp.float32), x[:-by]], axis=0)


def masks_x():
    row, lane = load_grid()
    even = row % 2 == 0
    odd = row % 2 == 1
    return (row < 10) & even, (row < 10) & odd, (row >= 40) & (row < 50) & even, (row >= 40) & (row < 50) & odd


def masks_y():
    row, lane = load_grid()
    place = row % 10
    return (place < 2) & (row < 50), (place >= 8) & (row < 50), lane == 0, lane == 127


def join_x(x):
    near_even, near_odd, far_even, far_odd = masks_x()
    return (
        x
        + jnp.where(near_odd, pltpu.roll(rows_up(x, 40), 1, 0), 0.0)
        + jnp.where(far_even, pltpu.roll(rows_down(x, 40), 55, 0), 0.0)
    )


def join_x_wide(own, halo):
    near_even, near_odd, far_even, far_odd = masks_x()
    own_new = join_x(own)
    own_new = own_new + jnp.where(near_even, rows_up(halo, 40), 0.0)
    own_new = own_new + jnp.where(far_odd, rows_down(halo, 40), 0.0)
    halo_new = halo + jnp.where(far_even, rows_down(own, 40), 0.0)
    halo_new = halo_new + jnp.where(near_odd, rows_up(own, 40), 0.0)
    return own_new, halo_new


def join_y(x, sides):
    near, far, first, final = masks_y()
    before, after = pltpu.roll(x, 1, 1), pltpu.roll(x, 127, 1)
    fill_before = 0.0 if sides is None else pltpu.roll(sides, 1, 1)
    fill_after = 0.0 if sides is None else pltpu.roll(sides, 127, 1)
    out = x + jnp.where(near, rows_up(jnp.where(first, fill_before, before), 8), 0.0)
    out = out + jnp.where(far, rows_down(jnp.where(final, fill_after, after), 8), 0.0)
    if sides is None:
        return out
    new = sides + jnp.where(far & final, rows_down(after, 8), 0.0)
    new = new + jnp.where(near & first, rows_up(before, 8), 0.0)
    return out, new


def columns_from(tile):
    row, lane = load_grid()
    turned = jnp.concatenate([tile, jnp.zeros((120, 128), jnp.float32)], axis=0).T
    out = []
    for k in range(3):
        halves = []
        for h in range(2):
            part = turned[64 * h : 64 * h + 56]
            left = pltpu.roll(part, 127 - 2 * k, 1)
            right = pltpu.roll(part, (128 - 2 * k - 1) % 128, 1)
            value = jnp.where(lane == 127, left, jnp.where(lane == 0, right, 0.0))
            halves.append(jnp.where(row < 50, value, 0.0))
        out.append(halves)
    return out


def columns_to(columns):
    lane = lax.broadcasted_iota(jnp.int32, (128, 128), 1)
    total = jnp.zeros((128, 128), jnp.float32)
    for k in range(3):
        pad = jnp.zeros((8, 128), jnp.float32)
        x = jnp.concatenate([columns[k][0], pad, columns[k][1], pad], axis=0)
        total = jnp.where(lane == 2 * k, pltpu.roll(x, 2 * k + 1, 1), total)
        total = jnp.where(lane == 2 * k + 1, pltpu.roll(x, 2 * k + 1, 1), total)
    return total.T[:8]


def load_parts(table, own_ref, beyond_ref, sides_ref):
    row, lane = load_grid()
    line_of = lax.broadcasted_iota(jnp.int32, (8, 128), 0)
    raw = jnp.zeros((8, 128), jnp.float32)
    for k in range(3):
        for side in range(2):
            last = jnp.broadcast_to(table[k][50:51, 128 * side : 128 * side + 128], (8, 128))
            raw = jnp.where(line_of == 2 * k + side, last, raw)
    columns = columns_from(raw)
    new_columns = []
    for k in range(3):
        own = jnp.where(row < 50, table[k][:56, :128], 0.0)
        halo = jnp.where(row < 50, table[k][:56, 128:], 0.0)
        own, halo = join_x_wide(own, halo)
        sides = join_x_wide(columns[k][0], columns[k][1])
        own, side_own = join_y(own, sides[0])
        halo, side_halo = join_y(halo, sides[1])
        own_ref[k] = own
        beyond_ref[k] = halo
        new_columns.append((side_own, side_halo))
    sides_ref[...] = columns_to(new_columns)


def load_total(own_ref, got_x, got_y, load):
    has_x, has_y = open_edges()
    row, lane = load_grid()
    even = row % 2 == 0
    tile_lane = lax.broadcasted_iota(jnp.int32, (8, 128), 1)
    tile_row = lax.broadcasted_iota(jnp.int32, (8, 128), 0)
    ends = []
    for side in (-1, 1):
        low = jnp.where(has_x[-1], pltpu.roll(got_y[-1, side][...], 127, 1), 0.0)
        high = jnp.where(has_x[1], pltpu.roll(got_y[1, side][...], 1, 1), 0.0)
        tile = jnp.where(tile_lane < 64, got_y[0, side][...], jnp.where(tile_lane % 2 == 0, low, high))
        ends.append(jnp.where(has_y[side], tile, 0.0))
    columns = columns_from(jnp.where(tile_row % 2 == 0, ends[1], ends[0]))
    for k in range(3):
        low = jnp.where(has_x[-1], pltpu.roll(got_x[0][k], 55, 0), 0.0)
        high = jnp.where(has_x[1], pltpu.roll(got_x[1][k], 1, 0), 0.0)
        rows = jnp.where(even, low, high) + join_y(columns[k][1], None)
        total = own_ref[k] + join_x(jnp.where(row < 50, rows, 0.0)) + join_y(columns[k][0], None)
        for n in range(25):
            load[k * 25 + n] = jnp.concatenate(
                [total[2 * n : 2 * n + 2], jnp.zeros((2, 128), jnp.float32)], axis=0
            )


AROUND = [(-1, 0), (1, 0), (0, -1), (0, 1), (-1, -1), (-1, 1), (1, -1), (1, 1)]
ASIDE = AROUND[2:]


def shape(*dims, kind=jnp.float32):
    return jax.ShapeDtypeStruct(dims, kind)


def halo_plan(rows, cols):
    edge_rows = {-1: pl.ds(0, 4), 1: pl.ds(rows - 4, 4)}
    edge_cols = {-1: pl.ds(0, 128), 1: pl.ds(cols - 128, 128)}
    place_rows = {-1: pl.ds(0, 4), 1: pl.ds(4, 4)}
    messages = []
    for source in range(3):
        every = (slice(None),) if source == 0 else ()
        for dx, dy in AROUND:
            row_in = edge_rows.get(dx, pl.ds(0, rows))
            row_out = place_rows.get(dx, pl.ds(0, rows))
            col_in = edge_cols.get(dy, pl.ds(0, cols))
            where = 0 if dy == 0 else (1 if dx == 0 else 3) + (0 if dy == 1 else 1)
            messages.append(
                (source, every + (row_in, col_in), 5 * source + where,
                 every + (row_out, pl.ds(0, cols if dy == 0 else 128)), (dx, dy))
            )
    return messages


def whole_body(*refs):
    (flow_in, drag_in, wet_in, elem_in, node_in, u_in, before_in, density_in, lame_in, shear_in) = refs[:10]
    fields_out, next_out, last_out = refs[10:13]
    (ext, drag, buoy, scale, tract, row_slot, col_slot, table) = refs[13:21]
    halos = refs[21:36]
    (drag_own, wet_own, elem_own, node_own) = refs[36:40]
    (u_zero, before, u_one, u_two, force, stress, load, inverse) = refs[40:48]
    (density, lame, shear, around) = refs[48:52]
    (face_x, face_y, got_face_x, got_face_y) = refs[52:56]
    (own, beyond, sides, got_beyond, got_sides, kick) = refs[56:62]
    local_sem, sent, come = refs[62:]
    rows, cols = drag_own.shape
    at_x, at_y = lax.axis_index("gx"), lax.axis_index("gy")
    size_x, size_y = lax.axis_size("gx"), lax.axis_size("gy")

    def device(move):
        return ((at_x + move[0] + size_x) % size_x, (at_y + move[1] + size_y) % size_y)

    def opposite(move):
        return -move[0], -move[1]

    barrier = pltpu.get_barrier_semaphore()
    for move in AROUND:
        pl.semaphore_signal(barrier, inc=1, device_id=device(move), device_id_type=pl.DeviceIdType.MESH)
    reads = [
        pltpu.make_async_copy(source, target, local_sem.at[n])
        for n, (source, target) in enumerate(
            (
                (u_in, u_zero), (lame_in, lame), (shear_in, shear), (density_in, density),
                (flow_in, ext.at[0, :, 0:rows, 0:cols]), (drag_in, drag_own), (wet_in, wet_own),
                (elem_in, elem_own), (node_in, node_own), (before_in, before),
            )
        )
    ]
    for copy in reads:
        copy.start()
    store_fields = pltpu.make_async_copy(ext.at[0, :, 0:rows, 0:cols], fields_out, local_sem.at[10])
    store_last = pltpu.make_async_copy(u_one, last_out, local_sem.at[11])
    store_next = pltpu.make_async_copy(u_two, next_out, local_sem.at[12])
    pl.semaphore_wait(barrier, len(AROUND))
    number = [0]

    def send(source, target, move):
        n = number[0]
        number[0] += 1
        copy = pltpu.make_async_remote_copy(
            src_ref=source, dst_ref=target, send_sem=sent.at[n], recv_sem=come.at[n],
            device_id=device(move), device_id_type=pl.DeviceIdType.MESH,
        )
        copy.start()
        return copy

    operands = (flow_in, drag_in, wet_in)
    first = [
        send(operands[source].at[source_at], halos[target].at[target_at], move)
        for source, source_at, target, target_at, move in halo_plan(rows, cols)
    ]
    first += [send(density_in, around.at[AROUND.index(opposite(move))], move) for move in AROUND]

    def send_faces(step):
        copies = [send(face_x.at[step, 0], got_face_x.at[step, 1], (-1, 0))]
        copies += [send(face_x.at[step, 1], got_face_x.at[step, 0], (1, 0))]
        for move in ASIDE:
            copies.append(send(face_y.at[step], got_face_y.at[step, ASIDE.index(opposite(move))], move))
        return copies

    def faces_of(step):
        return (
            [got_face_x.at[step, n] for n in range(2)],
            {move: got_face_y.at[step, n] for n, move in enumerate(ASIDE)},
        )

    for copy in reads[:3]:
        copy.wait()
    internal_open(u_zero, lame, shear, stress, force)
    internal_close(stress, force)
    pack_faces(force, face_x.at[0], face_y.at[0])
    faces = send_faces(0)
    for copy in reads[3:]:
        copy.wait()

    def arrive():
        for copy in first:
            copy.wait()
        inverse_masses(density, {move: around.at[n] for n, move in enumerate(AROUND)}, inverse)

    surface(
        drag_own, wet_own, elem_own, node_own, arrive, (halos[0:5], halos[5:10], halos[10:15]),
        own, beyond, sides, ext, drag, buoy, scale, tract, row_slot, col_slot, table, store_fields,
    )
    loads = [send(beyond, got_beyond.at[1], (-1, 0)), send(beyond, got_beyond.at[0], (1, 0))]
    for move in ASIDE:
        loads.append(send(sides, got_sides.at[ASIDE.index(opposite(move))], move))
    for copy in faces:
        copy.wait()
    add_faces(force, *faces_of(0))
    advance_solid(force, None, inverse, u_zero, before, u_one)
    internal_open(u_one, lame, shear, stress, force)
    for copy in loads:
        copy.wait()
    load_total(
        own,
        [got_beyond.at[n] for n in range(2)],
        {move: got_sides.at[n] for n, move in enumerate(ASIDE)},
        load,
    )
    kick_solid(load, inverse, u_one, kick)
    store_last.start()
    internal_kick(kick, lame, shear, force)
    internal_close(stress, force)
    pack_faces(force, face_x.at[1], face_y.at[1])
    faces = send_faces(1)
    for copy in faces:
        copy.wait()
    add_faces(force, *faces_of(1))
    advance_solid(force, load, inverse, u_one, u_zero, u_two)
    store_next.start()
    store_fields.wait()
    store_last.wait()
    store_next.wait()


def store_body(*refs):
    taken, given = refs[9:]
    reads, writes = [], []
    for n in range(3):
        source, target, held = refs[n], refs[3 + n], refs[6 + n]
        step = source.shape[0] // 3
        for m in range(3):
            part = pl.ds(m * step, step)
            at = 3 * n + m
            reads.append(pltpu.make_async_copy(source.at[part], held.at[part], taken.at[at]))
            writes.append(pltpu.make_async_copy(held.at[part], target.at[part], given.at[at]))
    for copy in reads:
        copy.start()
    for read, write in zip(reads, writes):
        read.wait()
        write.start()
    for copy in writes:
        copy.wait()


def per_device(
    flow_state,
    drag_coefficient,
    wet_mask,
    target_elem,
    target_node,
    displacement,
    previous,
    density,
    lame_first,
    shear_modulus,
):
    rows, cols = drag_coefficient.shape
    tall, wide = rows + 8, cols + 128
    grid = displacement.shape
    nodes = (375, 4, 128)
    halo_shapes = []
    for lead, kind_of in (((6,), jnp.float32), ((), jnp.float32), ((), jnp.int32)):
        for dims in ((8, cols), (rows, 128), (rows, 128), (8, 128), (8, 128)):
            halo_shapes.append(pltpu.VMEM((*lead, *dims), kind_of))

    def floats(*dims):
        return pltpu.VMEM(dims, jnp.float32)

    def integers(*dims):
        return pltpu.VMEM(dims, jnp.int32)

    scratch = [
        floats(2, 6, tall, wide), floats(tall, wide), floats(tall, wide), floats(tall, wide),
        floats(3, rows, cols), floats(rows, cols), floats(rows, cols), floats(320, 256),
        *halo_shapes,
        floats(rows, cols), integers(rows, cols), integers(rows, cols), integers(rows, cols),
        *[floats(*nodes)] * 6, floats(75, 4, 128), floats(27, 4, 128),
        floats(4, 128), floats(4, 128), floats(4, 128), floats(8, 4, 128),
        floats(2, 2, 39, 4, 128), floats(2, 2, 4, 128), floats(2, 2, 39, 4, 128), floats(2, 6, 2, 4, 128),
        floats(3, 56, 128), floats(3, 56, 128), floats(8, 128), floats(2, 3, 56, 128), floats(6, 8, 128), floats(75, 4, 128),
        pltpu.SemaphoreType.DMA((13,)), pltpu.SemaphoreType.DMA((56,)), pltpu.SemaphoreType.DMA((56,)),
    ]
    anywhere = pl.BlockSpec(memory_space=pl.ANY)
    results = pl.pallas_call(
        whole_body,
        out_shape=(shape(6, rows, cols), shape(*nodes), shape(*nodes)),
        in_specs=[anywhere] * 10,
        out_specs=(anywhere,) * 3,
        scratch_shapes=scratch,
        compiler_params=pltpu.CompilerParams(
            collective_id=1, has_side_effects=True, vmem_limit_bytes=56 * 2**20
        ),
    )(
        flow_state, drag_coefficient, wet_mask, target_elem, target_node,
        displacement.reshape(nodes), previous.reshape(nodes),
        *(x.reshape(4, 128) for x in (density, lame_first, shear_modulus)),
    )
    fields, u_two, u_one = pl.pallas_call(
        store_body,
        out_shape=tuple(shape(*x.shape) for x in results),
        in_specs=[anywhere] * 3,
        out_specs=(anywhere,) * 3,
        scratch_shapes=[
            *[pltpu.VMEM(x.shape, jnp.float32) for x in results],
            pltpu.SemaphoreType.DMA((9,)), pltpu.SemaphoreType.DMA((9,)),
        ],
        compiler_params=pltpu.CompilerParams(vmem_limit_bytes=60 * 2**20),
    )(*results)
    return (fields, u_two.reshape(grid), u_one.reshape(grid))


def solution(mesh):
    return jax.shard_map(
        per_device,
        mesh=mesh,
        in_specs=(
            P(None, "gx", "gy"),
            P("gx", "gy"),
            P("gx", "gy"),
            P("gx", "gy"),
            P("gx", "gy"),
            P(None, None, None, None, None, "gx", "gy"),
            P(None, None, None, None, None, "gx", "gy"),
            P(None, "gx", "gy"),
            P(None, "gx", "gy"),
            P(None, "gx", "gy"),
        ),
        out_specs=(
            P(None, "gx", "gy"),
            P(None, None, None, None, None, "gx", "gy"),
            P(None, None, None, None, None, "gx", "gy"),
        ),
        check_vma=False,
    )
```

```python
import jax
import jax.numpy as jnp
import numpy as np
from jax import lax
from jax.experimental import pallas as pl
from jax.experimental.pallas import tpu as pltpu
from jax.sharding import PartitionSpec as P

FLOW_STEPS = 4
SOLID_STEPS = 2
SLOT_ROWS = 51
GROUP = 8


gll_points = np.array([-1.0, -np.sqrt(3.0 / 7.0), 0.0, np.sqrt(3.0 / 7.0), 1.0])
gll_weights = np.array([0.1, 49.0 / 90.0, 32.0 / 45.0, 49.0 / 90.0, 0.1])
flow_dt = 0.4
diffusion = 0.2
coupling = 0.5
upper_gravity = 0.8
density_ratio = 0.7
speed_floor = 0.0001
load_factor = 4.0
solid_dt = 0.04


def legendre_four(x):
    return (35.0 * x**4 - 30.0 * x**2 + 3.0) / 8.0


def derivative_table():
    result = np.zeros((5, 5))
    for i in range(5):
        for j in range(5):
            if i != j:
                result[i, j] = (
                    legendre_four(gll_points[i])
                    / legendre_four(gll_points[j])
                    / (gll_points[i] - gll_points[j])
                )
    result[0, 0] = -5.0
    result[4, 4] = 5.0
    return result


def surface(
    drag_ref, wet_ref, elem_ref, node_ref, arrive, got, own_ref, beyond_ref, sides_ref,
    ext, drag, buoy, scale, tract, row_slot, col_slot, table_ref, store_fields,
):
    rows, cols = drag_ref.shape
    wide = cols + 128
    tall = rows + 8
    at_x, at_y = lax.axis_index("gx"), lax.axis_index("gy")
    last_x, last_y = lax.axis_size("gx") - 1, lax.axis_size("gy") - 1

    def wetness(x):
        return 1.0 - 0.6 * x

    def own_cells(t, carry):
        at = pl.ds(pl.multiple_of(t * 128, 128), 128)
        drag[0:rows, at] = drag_ref[:, at]
        buoy[0:rows, at] = wetness(wet_ref[:, at].astype(jnp.float32))
        e = elem_ref[:, at]
        n = node_ref[:, at]
        surface_cols = 128 * (last_y + 1)
        er = lax.shift_right_logical(e, surface_cols.bit_length() - 1) if surface_cols & (surface_cols - 1) == 0 else e // surface_cols
        lx = er - 2 * at_x + 1
        ly = (e - er * surface_cols) - 128 * at_y + 1
        inside = (ly >= 1) & (ly <= 128)
        own_row = (lx == 1) | (lx == 2)
        half = jnp.where(own_row, 0, 1)
        line = 2 * n + jnp.where(lx >= 2, 1, 0)
        a = jnp.where(inside, line, 50)
        b = jnp.where(
            inside,
            half * 128 + ly - 1,
            jnp.where(ly == 0, 0, 128) + 64 * half + line,
        )
        row_slot[:, at] = a.astype(jnp.float32)
        col_slot[:, at] = b.astype(jnp.float32)
        return carry

    lax.fori_loop(0, cols // 128, own_cells, 0)
    arrive()

    sub = lax.broadcasted_iota(jnp.int32, (8, 128), 0)
    lane = lax.broadcasted_iota(jnp.int32, (8, 128), 1)
    up_half = sub < 4
    left_half = lane < 64

    def zero_rows(tile):
        tile = jnp.where(up_half & (at_x == last_x), 0.0, tile)
        return jnp.where(jnp.logical_not(up_half) & (at_x == 0), 0.0, tile)

    def zero_cols(tile):
        tile = jnp.where(left_half & (at_y == last_y), 0.0, tile)
        return jnp.where(jnp.logical_not(left_half) & (at_y == 0), 0.0, tile)

    def received(k, n, *at):
        if k < 6:
            return got[0][n][(k, *at)]
        tile = got[k - 5][n][at]
        return tile if k == 6 else tile.astype(jnp.float32)

    def place(k, r, c, tile):
        if k < 6:
            ext[0, k, r, c] = tile
        elif k == 6:
            drag[r, c] = tile
        else:
            buoy[r, c] = wetness(tile)

    tail = pl.ds(cols, 128)
    foot = pl.ds(rows, 8)
    ones = jnp.full((8, 128), 0.2, jnp.float32)
    row_scale = zero_rows(ones)
    col_scale = zero_cols(ones)

    def halo_rows(t, carry):
        at = pl.ds(pl.multiple_of(t * 128, 128), 128)
        for k in range(8):
            place(k, foot, at, zero_rows(received(k, 0, slice(None), at)))
        for r in range(0, rows, 8):
            scale[r : r + 8, at] = ones
        scale[foot, at] = row_scale
        return carry

    lax.fori_loop(0, cols // 128, halo_rows, 0)
    for k in range(8):
        for r in range(0, rows, 8):
            at = (slice(r, r + 8), slice(None))
            tile = jnp.where(left_half, received(k, 2, *at), received(k, 1, *at))
            place(k, pl.ds(r, 8), tail, zero_cols(tile))
        at = (slice(None), slice(None))
        tile = jnp.where(left_half, received(k, 4, *at), received(k, 3, *at))
        place(k, foot, tail, zero_cols(zero_rows(tile)))
    for r in range(0, rows, 8):
        scale[r : r + 8, tail] = col_scale
    scale[foot, tail] = zero_cols(row_scale)

    lanes = lax.broadcasted_iota(jnp.int32, (tall, 128), 1)
    first_lane = lanes == 0
    last_lane = lanes == 127
    tiles = wide // 128

    def press(f0, f1, b):
        return b * (f0 + f1), upper_gravity * density_ratio * f0 + upper_gravity * f1

    def step(now, carry):
        later = 1 - now

        def tile_step(t, carry):
            at = pl.ds(pl.multiple_of(t * 128, 128), 128)
            t_hi = jnp.where(t == tiles - 1, 0, t + 1)
            t_lo = jnp.where(t == 0, tiles - 1, t - 1)
            at_hi = pl.ds(pl.multiple_of(t_hi * 128, 128), 128)
            at_lo = pl.ds(pl.multiple_of(t_lo * 128, 128), 128)
            f = [ext[now, k, :, at] for k in range(6)]
            b = buoy[:, at]
            one, two = press(f[0], f[1], b)
            sums = [None] * 6

            def add(k, value):
                sums[k] = value if sums[k] is None else sums[k] + value

            for ahead in (True, False):
                by = tall - 1 if ahead else 1
                def rolled(x):
                    return pltpu.roll(x, by, 0)
                sg = -1.0 if ahead else 1.0
                def mix(x, y):
                    return x - y if ahead else x + y
                add(0, rolled(mix(f[0], f[2])))
                add(1, rolled(mix(f[1], f[4])))
                add(2, rolled(mix(f[2], one)))
                add(3, rolled(f[3]))
                add(4, rolled(mix(f[4], two)))
                add(5, rolled(f[5]))
            for ahead in (True, False):
                by = 127 if ahead else 1
                edge = first_lane if ahead else last_lane
                other = at_hi if ahead else at_lo
                g = [jnp.where(edge, ext[now, k, :, other], f[k]) for k in range(6)]
                gb = jnp.where(edge, buoy[:, other], b)
                g_one, g_two = press(g[0], g[1], gb)
                def rolled(x):
                    return pltpu.roll(x, by, 1)
                def mix(x, y):
                    return x - y if ahead else x + y
                add(0, rolled(mix(g[0], g[3])))
                add(1, rolled(mix(g[1], g[5])))
                add(2, rolled(g[2]))
                add(3, rolled(mix(g[3], g_one)))
                add(4, rolled(g[4]))
                add(5, rolled(mix(g[5], g_two)))
            speed = jnp.sqrt(f[2] * f[2] + f[3] * f[3] + speed_floor)
            rub = 2.0 * drag[:, at] * speed
            k = scale[:, at]
            ext[later, 0, :, at] = k * (f[0] + sums[0])
            ext[later, 1, :, at] = k * (f[1] + sums[1])
            ext[later, 2, :, at] = k * (sums[2] + f[4] - rub * f[2])
            ext[later, 3, :, at] = k * (sums[3] + f[5] - rub * f[3])
            ext[later, 4, :, at] = k * (sums[4] + f[2])
            ext[later, 5, :, at] = k * (sums[5] + f[3])
            return carry

        return lax.fori_loop(0, tiles, tile_step, carry, unroll=True)

    lax.fori_loop(0, FLOW_STEPS // 2, lambda _, carry: step(1, step(0, carry)), 0)
    store_fields.start()

    def pull(t, carry):
        at = pl.ds(pl.multiple_of(t * 128, 128), 128)
        f = [ext[0, k, 0:rows, at] for k in range(4)]
        rub = load_factor * drag[0:rows, at] * jnp.sqrt(f[2] * f[2] + f[3] * f[3] + speed_floor)
        tract[0, :, at] = rub * f[2]
        tract[1, :, at] = rub * f[3]
        tract[2, :, at] = -load_factor * (buoy[0:rows, at] * (f[0] + f[1]))
        return carry

    lax.fori_loop(0, cols // 128, pull, 0)

    table_ref[...] = jnp.zeros_like(table_ref)
    narrow = jnp.bfloat16
    row16 = lax.broadcasted_iota(jnp.int32, (16, cols), 0)
    count = row16.astype(jnp.float32).astype(narrow)

    def spread(group, carry):
        lefts, rights = [], []
        for n in range(GROUP):
            line = pl.ds(group * GROUP + n, 1)

            def wide16(x):
                return jnp.broadcast_to(x, (16, cols)).astype(narrow)

            parts = []
            for k in range(3):
                value = tract[k, line, :]
                high = value.astype(narrow).astype(jnp.float32)
                parts.append(wide16(value))
                parts.append(wide16(value - high))
            a = wide16(row_slot[line, :])
            b = wide16(col_slot[line, :])
            zero = jnp.zeros((16, cols), narrow)
            one = jnp.ones((16, cols), narrow)
            pieces = []
            for top in range(0, table_ref.shape[0], 16):
                part, last = top // SLOT_ROWS, min((top + 15) // SLOT_ROWS, 5)
                skip = top - SLOT_ROWS * part
                if part == last:
                    pieces.append(jnp.where(a == count + narrow(skip), parts[part], zero))
                else:
                    split = SLOT_ROWS * last - top
                    target = row16 + jnp.where(row16 < split, skip, -split)
                    mixed = jnp.where(count < narrow(split), parts[part], parts[last])
                    pieces.append(jnp.where(a == target.astype(jnp.float32).astype(narrow), mixed, zero))
            lefts.append(jnp.concatenate(pieces, axis=0))
            rights.append(
                jnp.concatenate([jnp.where(b == count + narrow(16 * m), one, zero) for m in range(16)], axis=0)
            )
        table_ref[...] += lax.dot_general(
            jnp.concatenate(lefts, axis=1),
            jnp.concatenate(rights, axis=1),
            (((1,), (1,)), ((), ())),
            preferred_element_type=jnp.float32,
        )
        return carry

    lax.fori_loop(0, rows // GROUP, spread, 0)

    def part_rows(n):
        return table_ref[SLOT_ROWS * n : SLOT_ROWS * n + SLOT_ROWS]

    pad = jnp.zeros((64 - SLOT_ROWS, 256), jnp.float32)
    table = [
        jnp.concatenate([part_rows(2 * k) + part_rows(2 * k + 1), pad], axis=0) for k in range(3)
    ]
    load_parts(table, own_ref, beyond_ref, sides_ref)


def line(matrix, s):
    even = [s[0] + s[4], s[1] + s[3]]
    odd = [s[0] - s[4], s[1] - s[3]]
    out = [None] * 5
    for a in range(2):
        half_sum = [0.5 * (matrix[a, p] - matrix[a, 4 - p]) for p in range(2)]
        half_diff = [0.5 * (matrix[a, p] + matrix[a, 4 - p]) for p in range(2)]
        x = float(half_sum[0]) * odd[0] + float(half_sum[1]) * odd[1]
        y = float(half_diff[0]) * even[0] + float(half_diff[1]) * even[1] + float(matrix[a, 2]) * s[2]
        out[a] = x + y
        out[4 - a] = x - y
    out[2] = float(matrix[2, 0]) * odd[0] + float(matrix[2, 1]) * odd[1]
    return out


def lane_row():
    lane = lax.broadcasted_iota(jnp.int32, (4, 128), 1)
    row = lax.broadcasted_iota(jnp.int32, (4, 128), 0)
    return lane, row


def internal_open(u_ref, lame_ref, shear_ref, stress, force):
    table = derivative_table()

    def slope_x(m, carry):
        for i in range(3):
            lines = line(table, [u_ref[i * 125 + a * 25 + m] for a in range(5)])
            for a in range(5):
                stress[i * 125 + a * 25 + m] = lines[a]
        return carry

    lax.fori_loop(0, 25, slope_x, 0)

    def plane(a, carry):
        weight = jnp.where(
            (a == 0) | (a == 4),
            np.float32(gll_weights[0]),
            jnp.where(a == 2, np.float32(gll_weights[2]), np.float32(gll_weights[1])),
        )
        lame = lame_ref[...] * -weight
        shear = shear_ref[...] * -weight

        def at(i, b, c):
            return i * 125 + a * 25 + b * 5 + c

        slope_y, slope_z = [], []
        for i in range(3):
            u = [[u_ref[at(i, b, c)] for c in range(5)] for b in range(5)]
            along_y = [line(table, [u[b][c] for b in range(5)]) for c in range(5)]
            slope_y.append([[along_y[c][b] for c in range(5)] for b in range(5)])
            slope_z.append([line(table, u[b]) for b in range(5)])
        pull_y = [[[None] * 5 for b in range(5)] for i in range(3)]
        pull_z = [[[None] * 5 for b in range(5)] for i in range(3)]
        for b in range(5):
            for c in range(5):
                w = np.float32(gll_weights[b] * gll_weights[c])
                g = [[stress[at(i, b, c)], slope_y[i][b][c], slope_z[i][b][c]] for i in range(3)]
                mu = shear * w
                twice = mu + mu
                spread = (lame * w) * (g[0][0] + g[1][1] + g[2][2])
                s00 = spread + twice * g[0][0]
                s11 = spread + twice * g[1][1]
                s22 = spread + twice * g[2][2]
                s01 = mu * (g[0][1] + g[1][0])
                s02 = mu * (g[0][2] + g[2][0])
                s12 = mu * (g[1][2] + g[2][1])
                stress[at(0, b, c)] = s00
                stress[at(1, b, c)] = s01
                stress[at(2, b, c)] = s02
                for i, (s_y, s_z) in enumerate(((s01, s02), (s11, s12), (s12, s22))):
                    pull_y[i][b][c] = s_y
                    pull_z[i][b][c] = s_z
        for i in range(3):
            along_y = [line(table.T, [pull_y[i][b][c] for b in range(5)]) for c in range(5)]
            for b in range(5):
                along_z = line(table.T, pull_z[i][b])
                for c in range(5):
                    force[at(i, b, c)] = along_y[c][b] + along_z[c]
        return carry

    lax.fori_loop(0, 5, plane, 0)


def internal_kick(kick, lame_ref, shear_ref, force):
    table = derivative_table()
    lame, shear = -lame_ref[...], -shear_ref[...]
    five = range(5)

    def grid(make):
        return [[make(a, b) for b in five] for a in five]

    def along_x(matrix, x):
        lines = [line(matrix, [x[a][b] for a in five]) for b in five]
        return grid(lambda a, b: lines[b][a])

    def along_y(matrix, x):
        lines = [line(matrix, x[a]) for a in five]
        return grid(lambda a, b: lines[a][b])

    def plus(x, y):
        return grid(lambda a, b: x[a][b] + y[a][b])

    def area(a, b):
        return np.float32(gll_weights[a] * gll_weights[b])

    d = [grid(lambda a, b: kick[i * 25 + a * 5 + b]) for i in range(3)]
    d_x = [along_x(table, x) for x in d]
    d_y = [along_y(table, x) for x in d]
    lame_w = grid(lambda a, b: lame * area(a, b))
    shear_w = grid(lambda a, b: shear * area(a, b))
    t_side = grid(lambda a, b: lame_w[a][b] * d[2][a][b])
    t_02 = grid(lambda a, b: shear_w[a][b] * d[0][a][b])
    t_12 = grid(lambda a, b: shear_w[a][b] * d[1][a][b])
    t_22 = grid(lambda a, b: t_side[a][b] + (shear_w[a][b] + shear_w[a][b]) * d[2][a][b])
    first = np.float32(gll_weights[0])
    l_0 = grid(lambda a, b: first * lame_w[a][b])
    m_0 = grid(lambda a, b: first * shear_w[a][b])
    e_22 = grid(lambda a, b: l_0[a][b] * (d_x[0][a][b] + d_y[1][a][b]))
    e_00 = grid(lambda a, b: e_22[a][b] + (m_0[a][b] + m_0[a][b]) * d_x[0][a][b])
    e_11 = grid(lambda a, b: e_22[a][b] + (m_0[a][b] + m_0[a][b]) * d_y[1][a][b])
    e_01 = grid(lambda a, b: m_0[a][b] * (d_y[0][a][b] + d_x[1][a][b]))
    e_02 = grid(lambda a, b: m_0[a][b] * d_x[2][a][b])
    e_12 = grid(lambda a, b: m_0[a][b] * d_y[2][a][b])
    turned = table.T
    pulled = (
        along_x(turned, t_side),
        along_y(turned, t_side),
        plus(along_x(turned, t_02), along_y(turned, t_12)),
    )
    flat = (
        plus(along_x(turned, e_00), along_y(turned, e_01)),
        plus(along_x(turned, e_01), along_y(turned, e_11)),
        plus(along_x(turned, e_02), along_y(turned, e_12)),
    )
    share = [float(table[c, 0] * gll_weights[c]) for c in five]
    upright = [float(sum(table[p, c] * share[p] for p in five)) for c in five]
    for i, (t, e) in enumerate(((t_02, e_02), (t_12, e_12), (t_22, e_22))):
        for a in five:
            for b in five:
                for c in five:
                    value = share[c] * pulled[i][a][b] + upright[c] * t[a][b]
                    value = value + float(table[0, c]) * e[a][b]
                    if c == 0:
                        value = value + flat[i][a][b]
                    force[i * 125 + a * 25 + b * 5 + c] += value


def internal_close(stress, force):
    table = derivative_table()
    lane, row = lane_row()
    low_x = row % 2 == 0
    low_z = row < 2

    def close_x(m, carry):
        for i in range(3):
            pulled = line(table.T, [stress[i * 125 + a * 25 + m] for a in range(5)])
            f = [force[i * 125 + a * 25 + m] + pulled[a] for a in range(5)]
            near = f[0] + jnp.where(low_x, 0.0, pltpu.roll(f[4], 1, 0))
            far = f[4] + jnp.where(low_x, pltpu.roll(f[0], 3, 0), 0.0)
            for a, value in enumerate((near, f[1], f[2], f[3], far)):
                force[i * 125 + a * 25 + m] = value
        return carry

    lax.fori_loop(0, 25, close_x, 0)

    def close_yz(ia, carry):
        base = ia * 25
        f = [[force[base + b * 5 + c] for c in range(5)] for b in range(5)]
        for c in range(5):
            near, far = f[0][c], f[4][c]
            f[0][c] = near + jnp.where(lane == 0, 0.0, pltpu.roll(far, 1, 1))
            f[4][c] = far + jnp.where(lane == 127, 0.0, pltpu.roll(near, 127, 1))
        for b in range(5):
            near, far = f[b][0], f[b][4]
            f[b][0] = near + jnp.where(low_z, 0.0, pltpu.roll(far, 2, 0))
            f[b][4] = far + jnp.where(low_z, pltpu.roll(near, 2, 0), 0.0)
        for b in range(5):
            for c in range(5):
                if b in (0, 4) or c in (0, 4):
                    force[base + b * 5 + c] = f[b][c]
        return carry

    lax.fori_loop(0, 15, close_yz, 0)


def pack_faces(force, face_x, face_y):
    lane, row = lane_row()
    low_x = row % 2 == 0

    def both(m, other):
        for i in range(3):
            near, far = force[i * 125 + m], force[i * 125 + 100 + m]
            near_other, far_other = force[i * 125 + other], force[i * 125 + 100 + other]
            face_x[0, i * 13 + m] = jnp.where(low_x, near, pltpu.roll(near_other, 1, 0))
            face_x[1, i * 13 + m] = jnp.where(low_x, pltpu.roll(far, 3, 0), far_other)

    def pack_x(m, carry):
        both(m, m + 13)
        return carry

    lax.fori_loop(0, 12, pack_x, 0)
    both(12, 12)
    ends = [jnp.zeros((4, 128), jnp.float32)] * 2
    for a in range(5):
        for i in range(3):
            for c in range(5):
                q = a * 15 + i * 5 + c
                n = i * 125 + a * 25 + c
                ends[0] = jnp.where(lane == q, pltpu.roll(force[n], q, 1), ends[0])
                ends[1] = jnp.where(lane == q, pltpu.roll(force[n + 20], q + 1, 1), ends[1])
    face_y[0] = ends[0]
    face_y[1] = ends[1]


def open_edges():
    at_x, at_y = lax.axis_index("gx"), lax.axis_index("gy")
    has = {-1: at_x > 0, 1: at_x < lax.axis_size("gx") - 1}
    has_y = {-1: at_y > 0, 1: at_y < lax.axis_size("gy") - 1}
    return has, has_y


def add_faces(target, got_x, got_y, factor):
    has_x, has_y = open_edges()
    lane, row = lane_row()
    low_x = row % 2 == 0
    from_low = low_x & has_x[-1]
    from_high = jnp.logical_not(low_x) & has_x[1]
    for m in range(13):
        for i in range(3):
            low, high = got_x[0][i * 13 + m], got_x[1][i * 13 + m]
            pairs = [(m, low, pltpu.roll(high, 1, 0))]
            if m < 12:
                pairs.append((m + 13, pltpu.roll(low, 3, 0), high))
            for at, near, far in pairs:
                b, c = at // 5, at % 5
                target[i * 125 + at] += factor(0, b, c, jnp.where(from_low, near, 0.0))
                target[i * 125 + 100 + at] += factor(4, b, c, jnp.where(from_high, far, 0.0))
    first, final = lane < 15, (lane >= 60) & (lane < 75)
    columns = []
    for side, end in ((-1, 1), (1, 0)):
        straight = got_y[0, side][end]
        low = pltpu.roll(pltpu.roll(got_y[-1, side][end], 68, 1), 3, 0)
        high = pltpu.roll(pltpu.roll(got_y[1, side][end], 60, 1), 1, 0)
        total = straight + jnp.where(first & low_x & has_x[-1], low, 0.0)
        total = total + jnp.where(final & jnp.logical_not(low_x) & has_x[1], high, 0.0)
        columns.append(jnp.where(has_y[side], total, 0.0))
    for a in range(5):
        for i in range(3):
            for c in range(5):
                q = a * 15 + i * 5 + c
                n = i * 125 + a * 25 + c
                near = jnp.where(lane == 0, pltpu.roll(columns[0], (128 - q) % 128, 1), 0.0)
                far = jnp.where(lane == 127, pltpu.roll(columns[1], 127 - q, 1), 0.0)
                target[n] += factor(a, 0, c, near)
                target[n + 20] += factor(a, 4, c, far)


def inverse_masses(density_ref, around, inverse):
    has_x, has_y = open_edges()
    lane, row = lane_row()
    low_x = row % 2 == 0
    low_z = row < 2

    def beside(mine, left, right):
        left = jnp.where(has_y[-1], left, 0.0)
        right = jnp.where(has_y[1], right, 0.0)
        before = jnp.where(lane == 0, pltpu.roll(left, 1, 1), pltpu.roll(mine, 1, 1))
        after = jnp.where(lane == 127, pltpu.roll(right, 127, 1), pltpu.roll(mine, 127, 1))
        return mine + before, mine, mine + after

    mine = beside(density_ref[...], around[0, -1][...], around[0, 1][...])
    low = beside(around[-1, 0][...], around[-1, -1][...], around[-1, 1][...])
    high = beside(around[1, 0][...], around[1, -1][...], around[1, 1][...])
    for b in range(3):
        lo = jnp.where(has_x[-1], low[b], 0.0)
        hi = jnp.where(has_x[1], high[b], 0.0)
        before = mine[b] + jnp.where(low_x, pltpu.roll(lo, 3, 0), pltpu.roll(mine[b], 1, 0))
        after = mine[b] + jnp.where(low_x, pltpu.roll(mine[b], 3, 0), pltpu.roll(hi, 1, 0))
        for a, value in enumerate((before, mine[b], after)):
            top = value + jnp.where(low_z, 0.0, pltpu.roll(value, 2, 0))
            bottom = value + jnp.where(low_z, pltpu.roll(value, 2, 0), 0.0)
            for c, total in enumerate((top, value, bottom)):
                inverse[a * 9 + b * 3 + c] = (solid_dt * solid_dt) / total


def kind(node):
    return 0 if node == 0 else 2 if node == 4 else 1


def moved_by(inverse, a, b, c, f):
    w = np.float32(1.0 / (gll_weights[a] * gll_weights[b] * gll_weights[c]))
    return (inverse[kind(a) * 9 + kind(b) * 3 + kind(c)] * w) * f


def advance_solid(force, load, inverse, now_ref, before_ref, out_ref):
    def component(i, carry):
        for a in range(5):
            for b in range(5):
                for c in range(5):
                    n = a * 25 + b * 5 + c
                    f = force[i * 125 + n]
                    if c == 0 and load is not None:
                        f = f + load[i * 25 + a * 5 + b]
                    step = moved_by(inverse, a, b, c, f)
                    at = i * 125 + n
                    out_ref[at] = (now_ref[at] + now_ref[at] - before_ref[at]) + step
        return carry

    lax.fori_loop(0, 3, component, 0)


def kick_solid(load, inverse, out_ref, kick):
    def component(i, carry):
        for a in range(5):
            for b in range(5):
                n = i * 25 + a * 5 + b
                step = moved_by(inverse, a, b, 0, load[n])
                kick[n] = step
                out_ref[i * 125 + a * 25 + b * 5] += step
        return carry

    lax.fori_loop(0, 3, component, 0)


def load_grid():
    row = lax.broadcasted_iota(jnp.int32, (56, 128), 0)
    lane = lax.broadcasted_iota(jnp.int32, (56, 128), 1)
    return row, lane


def rows_up(x, by):
    return jnp.concatenate([x[by:], jnp.zeros((by, 128), jnp.float32)], axis=0)


def rows_down(x, by):
    return jnp.concatenate([jnp.zeros((by, 128), jnp.float32), x[:-by]], axis=0)


def masks_x():
    row, lane = load_grid()
    even = row % 2 == 0
    odd = row % 2 == 1
    return (row < 10) & even, (row < 10) & odd, (row >= 40) & (row < 50) & even, (row >= 40) & (row < 50) & odd


def masks_y():
    row, lane = load_grid()
    place = row % 10
    return (place < 2) & (row < 50), (place >= 8) & (row < 50), lane == 0, lane == 127


def join_x(x):
    near_even, near_odd, far_even, far_odd = masks_x()
    return (
        x
        + jnp.where(near_odd, pltpu.roll(rows_up(x, 40), 1, 0), 0.0)
        + jnp.where(far_even, pltpu.roll(rows_down(x, 40), 55, 0), 0.0)
    )


def join_x_wide(own, halo):
    near_even, near_odd, far_even, far_odd = masks_x()
    own_new = join_x(own)
    own_new = own_new + jnp.where(near_even, rows_up(halo, 40), 0.0)
    own_new = own_new + jnp.where(far_odd, rows_down(halo, 40), 0.0)
    halo_new = halo + jnp.where(far_even, rows_down(own, 40), 0.0)
    halo_new = halo_new + jnp.where(near_odd, rows_up(own, 40), 0.0)
    return own_new, halo_new


def join_y(x, sides):
    near, far, first, final = masks_y()
    before, after = pltpu.roll(x, 1, 1), pltpu.roll(x, 127, 1)
    fill_before = 0.0 if sides is None else pltpu.roll(sides, 1, 1)
    fill_after = 0.0 if sides is None else pltpu.roll(sides, 127, 1)
    out = x + jnp.where(near, rows_up(jnp.where(first, fill_before, before), 8), 0.0)
    out = out + jnp.where(far, rows_down(jnp.where(final, fill_after, after), 8), 0.0)
    if sides is None:
        return out
    new = sides + jnp.where(far & final, rows_down(after, 8), 0.0)
    new = new + jnp.where(near & first, rows_up(before, 8), 0.0)
    return out, new


def columns_from(tile):
    row, lane = load_grid()
    turned = jnp.concatenate([tile, jnp.zeros((120, 128), jnp.float32)], axis=0).T
    out = []
    for k in range(3):
        halves = []
        for h in range(2):
            part = turned[64 * h : 64 * h + 56]
            left = pltpu.roll(part, 127 - 2 * k, 1)
            right = pltpu.roll(part, (128 - 2 * k - 1) % 128, 1)
            value = jnp.where(lane == 127, left, jnp.where(lane == 0, right, 0.0))
            halves.append(jnp.where(row < 50, value, 0.0))
        out.append(halves)
    return out


def columns_to(columns):
    lane = lax.broadcasted_iota(jnp.int32, (128, 128), 1)
    total = jnp.zeros((128, 128), jnp.float32)
    for k in range(3):
        pad = jnp.zeros((8, 128), jnp.float32)
        x = jnp.concatenate([columns[k][0], pad, columns[k][1], pad], axis=0)
        total = jnp.where(lane == 2 * k, pltpu.roll(x, 2 * k + 1, 1), total)
        total = jnp.where(lane == 2 * k + 1, pltpu.roll(x, 2 * k + 1, 1), total)
    return total.T[:8]


def load_parts(table, own_ref, beyond_ref, sides_ref):
    row, lane = load_grid()
    line_of = lax.broadcasted_iota(jnp.int32, (8, 128), 0)
    raw = jnp.zeros((8, 128), jnp.float32)
    for k in range(3):
        for side in range(2):
            last = jnp.broadcast_to(table[k][50:51, 128 * side : 128 * side + 128], (8, 128))
            raw = jnp.where(line_of == 2 * k + side, last, raw)
    columns = columns_from(raw)
    new_columns = []
    for k in range(3):
        own = jnp.where(row < 50, table[k][:56, :128], 0.0)
        halo = jnp.where(row < 50, table[k][:56, 128:], 0.0)
        own, halo = join_x_wide(own, halo)
        sides = join_x_wide(columns[k][0], columns[k][1])
        own, side_own = join_y(own, sides[0])
        halo, side_halo = join_y(halo, sides[1])
        own_ref[k] = own
        beyond_ref[k] = halo
        new_columns.append((side_own, side_halo))
    sides_ref[...] = columns_to(new_columns)


def load_total(own_ref, got_x, got_y, load):
    has_x, has_y = open_edges()
    row, lane = load_grid()
    even = row % 2 == 0
    tile_lane = lax.broadcasted_iota(jnp.int32, (8, 128), 1)
    tile_row = lax.broadcasted_iota(jnp.int32, (8, 128), 0)
    ends = []
    for side in (-1, 1):
        low = jnp.where(has_x[-1], pltpu.roll(got_y[-1, side][...], 127, 1), 0.0)
        high = jnp.where(has_x[1], pltpu.roll(got_y[1, side][...], 1, 1), 0.0)
        tile = jnp.where(tile_lane < 64, got_y[0, side][...], jnp.where(tile_lane % 2 == 0, low, high))
        ends.append(jnp.where(has_y[side], tile, 0.0))
    columns = columns_from(jnp.where(tile_row % 2 == 0, ends[1], ends[0]))
    for k in range(3):
        low = jnp.where(has_x[-1], pltpu.roll(got_x[0][k], 55, 0), 0.0)
        high = jnp.where(has_x[1], pltpu.roll(got_x[1][k], 1, 0), 0.0)
        rows = jnp.where(even, low, high) + join_y(columns[k][1], None)
        total = own_ref[k] + join_x(jnp.where(row < 50, rows, 0.0)) + join_y(columns[k][0], None)
        for n in range(25):
            load[k * 25 + n] = jnp.concatenate(
                [total[2 * n : 2 * n + 2], jnp.zeros((2, 128), jnp.float32)], axis=0
            )


AROUND = [(-1, 0), (1, 0), (0, -1), (0, 1), (-1, -1), (-1, 1), (1, -1), (1, 1)]
ASIDE = AROUND[2:]


def shape(*dims, kind=jnp.float32):
    return jax.ShapeDtypeStruct(dims, kind)


def halo_plan(rows, cols):
    edge_rows = {-1: pl.ds(0, 4), 1: pl.ds(rows - 4, 4)}
    edge_cols = {-1: pl.ds(0, 128), 1: pl.ds(cols - 128, 128)}
    place_rows = {-1: pl.ds(0, 4), 1: pl.ds(4, 4)}
    messages = []
    for source in range(3):
        every = (slice(None),) if source == 0 else ()
        for dx, dy in AROUND:
            row_in = edge_rows.get(dx, pl.ds(0, rows))
            row_out = place_rows.get(dx, pl.ds(0, rows))
            col_in = edge_cols.get(dy, pl.ds(0, cols))
            where = 0 if dy == 0 else (1 if dx == 0 else 3) + (0 if dy == 1 else 1)
            messages.append(
                (source, every + (row_in, col_in), 5 * source + where,
                 every + (row_out, pl.ds(0, cols if dy == 0 else 128)), (dx, dy))
            )
    return messages


def whole_body(*refs):
    (flow_in, drag_in, wet_in, elem_in, node_in, u_in, before_in, density_in, lame_in, shear_in) = refs[:10]
    fields_out, next_out, last_out = refs[10:13]
    (ext, drag, buoy, scale, tract, row_slot, col_slot, table) = refs[13:21]
    halos = refs[21:36]
    (drag_own, wet_own, elem_own, node_own) = refs[36:40]
    (u_zero, before, u_one, u_two, force, stress, load, inverse) = refs[40:48]
    (density, lame, shear, around) = refs[48:52]
    (face_x, face_y, got_face_x, got_face_y) = refs[52:56]
    (own, beyond, sides, got_beyond, got_sides, kick) = refs[56:62]
    local_sem, sent, come = refs[62:]
    rows, cols = drag_own.shape
    at_x, at_y = lax.axis_index("gx"), lax.axis_index("gy")
    size_x, size_y = lax.axis_size("gx"), lax.axis_size("gy")

    def device(move):
        return ((at_x + move[0] + size_x) % size_x, (at_y + move[1] + size_y) % size_y)

    def opposite(move):
        return -move[0], -move[1]

    def there(move):
        x, y = at_x + move[0], at_y + move[1]
        return (x >= 0) & (x < size_x) & (y >= 0) & (y < size_y)

    barrier = pltpu.get_barrier_semaphore()
    for move in AROUND:

        @pl.when(there(move))
        def _(move=move):
            pl.semaphore_signal(barrier, inc=1, device_id=device(move), device_id_type=pl.DeviceIdType.MESH)

    reads = [
        pltpu.make_async_copy(source, target, local_sem.at[n])
        for n, (source, target) in enumerate(
            (
                (u_in, u_zero), (lame_in, lame), (shear_in, shear), (density_in, density),
                (flow_in, ext.at[0, :, 0:rows, 0:cols]), (drag_in, drag_own), (wet_in, wet_own),
                (elem_in, elem_own), (node_in, node_own), (before_in, before),
            )
        )
    ]
    for copy in reads:
        copy.start()
    store_fields = pltpu.make_async_copy(ext.at[0, :, 0:rows, 0:cols], fields_out, local_sem.at[10])
    store_last = pltpu.make_async_copy(u_one, last_out, local_sem.at[11])
    store_next = pltpu.make_async_copy(u_two, next_out, local_sem.at[12])
    beside_x = 3 - jnp.where(at_x == 0, 1, 0) - jnp.where(at_x == size_x - 1, 1, 0)
    beside_y = 3 - jnp.where(at_y == 0, 1, 0) - jnp.where(at_y == size_y - 1, 1, 0)
    pl.semaphore_wait(barrier, beside_x * beside_y - 1)
    number = [0]

    def send(source, target, move):
        n = number[0]
        number[0] += 1
        copy = pltpu.make_async_remote_copy(
            src_ref=source, dst_ref=target, send_sem=sent.at[n], recv_sem=come.at[n],
            device_id=device(move), device_id_type=pl.DeviceIdType.MESH,
        )
        pl.when(there(move))(copy.start)
        return copy, move

    def finish(messages):
        for move in AROUND:
            mine = [copy for copy, way in messages if way == move]
            if mine:

                @pl.when(there(opposite(move)))
                def _(mine=mine):
                    for copy in mine:
                        copy.wait_recv()

                @pl.when(there(move))
                def _(mine=mine):
                    for copy in mine:
                        copy.wait_send()

    operands = (flow_in, drag_in, wet_in)
    first = [
        send(operands[source].at[source_at], halos[target].at[target_at], move)
        for source, source_at, target, target_at, move in halo_plan(rows, cols)
    ]
    first += [send(density_in, around.at[AROUND.index(opposite(move))], move) for move in AROUND]

    def send_faces(step):
        copies = [send(face_x.at[step, 0], got_face_x.at[step, 1], (-1, 0))]
        copies += [send(face_x.at[step, 1], got_face_x.at[step, 0], (1, 0))]
        for move in ASIDE:
            copies.append(send(face_y.at[step], got_face_y.at[step, ASIDE.index(opposite(move))], move))
        return copies

    def faces_of(step):
        return (
            [got_face_x.at[step, n] for n in range(2)],
            {move: got_face_y.at[step, n] for n, move in enumerate(ASIDE)},
        )

    for copy in reads[:3]:
        copy.wait()
    internal_open(u_zero, lame, shear, stress, force)
    internal_close(stress, force)
    pack_faces(force, face_x.at[0], face_y.at[0])
    faces = send_faces(0)
    for copy in reads[3:]:
        copy.wait()

    def arrive():
        finish(first)
        inverse_masses(density, {move: around.at[n] for n, move in enumerate(AROUND)}, inverse)

    surface(
        drag_own, wet_own, elem_own, node_own, arrive, (halos[0:5], halos[5:10], halos[10:15]),
        own, beyond, sides, ext, drag, buoy, scale, tract, row_slot, col_slot, table, store_fields,
    )
    loads = [send(beyond, got_beyond.at[1], (-1, 0)), send(beyond, got_beyond.at[0], (1, 0))]
    for move in ASIDE:
        loads.append(send(sides, got_sides.at[ASIDE.index(opposite(move))], move))
    finish(faces)
    add_faces(force, *faces_of(0), lambda a, b, c, f: f)
    advance_solid(force, None, inverse, u_zero, before, u_one)
    internal_open(u_one, lame, shear, stress, force)
    finish(loads)
    load_total(
        own,
        [got_beyond.at[n] for n in range(2)],
        {move: got_sides.at[n] for n, move in enumerate(ASIDE)},
        load,
    )
    kick_solid(load, inverse, u_one, kick)
    store_last.start()
    internal_kick(kick, lame, shear, force)
    internal_close(stress, force)
    pack_faces(force, face_x.at[1], face_y.at[1])
    faces = send_faces(1)
    advance_solid(force, load, inverse, u_one, u_zero, u_two)
    finish(faces)
    add_faces(u_two, *faces_of(1), lambda a, b, c, f: moved_by(inverse, a, b, c, f))
    store_next.start()
    store_fields.wait()
    store_last.wait()
    store_next.wait()


def store_body(*refs):
    taken, given = refs[9:]
    reads, writes = [], []
    for n in range(3):
        source, target, held = refs[n], refs[3 + n], refs[6 + n]
        step = source.shape[0] // 3
        for m in range(3):
            part = pl.ds(m * step, step)
            at = 3 * n + m
            reads.append(pltpu.make_async_copy(source.at[part], held.at[part], taken.at[at]))
            writes.append(pltpu.make_async_copy(held.at[part], target.at[part], given.at[at]))
    for copy in reads:
        copy.start()
    for read, write in zip(reads, writes):
        read.wait()
        write.start()
    for copy in writes:
        copy.wait()


def per_device(
    flow_state,
    drag_coefficient,
    wet_mask,
    target_elem,
    target_node,
    displacement,
    previous,
    density,
    lame_first,
    shear_modulus,
):
    rows, cols = drag_coefficient.shape
    tall, wide = rows + 8, cols + 128
    grid = displacement.shape
    nodes = (375, 4, 128)
    halo_shapes = []
    for lead, kind_of in (((6,), jnp.float32), ((), jnp.float32), ((), jnp.int32)):
        for dims in ((8, cols), (rows, 128), (rows, 128), (8, 128), (8, 128)):
            halo_shapes.append(pltpu.VMEM((*lead, *dims), kind_of))

    def floats(*dims):
        return pltpu.VMEM(dims, jnp.float32)

    def integers(*dims):
        return pltpu.VMEM(dims, jnp.int32)

    scratch = [
        floats(2, 6, tall, wide), floats(tall, wide), floats(tall, wide), floats(tall, wide),
        floats(3, rows, cols), floats(rows, cols), floats(rows, cols), floats(320, 256),
        *halo_shapes,
        floats(rows, cols), integers(rows, cols), integers(rows, cols), integers(rows, cols),
        *[floats(*nodes)] * 6, floats(75, 4, 128), floats(27, 4, 128),
        floats(4, 128), floats(4, 128), floats(4, 128), floats(8, 4, 128),
        floats(2, 2, 39, 4, 128), floats(2, 2, 4, 128), floats(2, 2, 39, 4, 128), floats(2, 6, 2, 4, 128),
        floats(3, 56, 128), floats(3, 56, 128), floats(8, 128), floats(2, 3, 56, 128), floats(6, 8, 128), floats(75, 4, 128),
        pltpu.SemaphoreType.DMA((13,)), pltpu.SemaphoreType.DMA((56,)), pltpu.SemaphoreType.DMA((56,)),
    ]
    anywhere = pl.BlockSpec(memory_space=pl.ANY)
    results = pl.pallas_call(
        whole_body,
        out_shape=(shape(6, rows, cols), shape(*nodes), shape(*nodes)),
        in_specs=[anywhere] * 10,
        out_specs=(anywhere,) * 3,
        scratch_shapes=scratch,
        compiler_params=pltpu.CompilerParams(
            collective_id=1, has_side_effects=True, vmem_limit_bytes=56 * 2**20
        ),
    )(
        flow_state, drag_coefficient, wet_mask, target_elem, target_node,
        displacement.reshape(nodes), previous.reshape(nodes),
        *(x.reshape(4, 128) for x in (density, lame_first, shear_modulus)),
    )
    fields, u_two, u_one = pl.pallas_call(
        store_body,
        out_shape=tuple(shape(*x.shape) for x in results),
        in_specs=[anywhere] * 3,
        out_specs=(anywhere,) * 3,
        scratch_shapes=[
            *[pltpu.VMEM(x.shape, jnp.float32) for x in results],
            pltpu.SemaphoreType.DMA((9,)), pltpu.SemaphoreType.DMA((9,)),
        ],
        compiler_params=pltpu.CompilerParams(vmem_limit_bytes=60 * 2**20),
    )(*results)
    return (fields, u_two.reshape(grid), u_one.reshape(grid))


def solution(mesh):
    return jax.shard_map(
        per_device,
        mesh=mesh,
        in_specs=(
            P(None, "gx", "gy"),
            P("gx", "gy"),
            P("gx", "gy"),
            P("gx", "gy"),
            P("gx", "gy"),
            P(None, None, None, None, None, "gx", "gy"),
            P(None, None, None, None, None, "gx", "gy"),
            P(None, "gx", "gy"),
            P(None, "gx", "gy"),
            P(None, "gx", "gy"),
        ),
        out_specs=(
            P(None, "gx", "gy"),
            P(None, None, None, None, None, "gx", "gy"),
            P(None, None, None, None, None, "gx", "gy"),
        ),
        check_vma=False,
    )
```

```python
import jax
import jax.numpy as jnp
import numpy as np
from jax import lax
from jax.experimental import pallas as pl
from jax.experimental.pallas import tpu as pltpu
from jax.sharding import PartitionSpec as P

FLOW_STEPS = 4
SOLID_STEPS = 2
SLOT_ROWS = 51
GROUP = 8


gll_points = np.array([-1.0, -np.sqrt(3.0 / 7.0), 0.0, np.sqrt(3.0 / 7.0), 1.0])
gll_weights = np.array([0.1, 49.0 / 90.0, 32.0 / 45.0, 49.0 / 90.0, 0.1])
flow_dt = 0.4
diffusion = 0.2
coupling = 0.5
upper_gravity = 0.8
density_ratio = 0.7
speed_floor = 0.0001
load_factor = 4.0
solid_dt = 0.04


def legendre_four(x):
    return (35.0 * x**4 - 30.0 * x**2 + 3.0) / 8.0


def derivative_table():
    result = np.zeros((5, 5))
    for i in range(5):
        for j in range(5):
            if i != j:
                result[i, j] = (
                    legendre_four(gll_points[i])
                    / legendre_four(gll_points[j])
                    / (gll_points[i] - gll_points[j])
                )
    result[0, 0] = -5.0
    result[4, 4] = 5.0
    return result


def surface(
    drag_ref, wet_ref, elem_ref, node_ref, arrive, got, own_ref, beyond_ref, sides_ref,
    ext, drag, buoy, scale, tract, row_slot, col_slot, table_ref, store_fields,
):
    rows, cols = drag_ref.shape
    wide = cols + 128
    tall = rows + 8
    at_x, at_y = lax.axis_index("gx"), lax.axis_index("gy")
    last_x, last_y = lax.axis_size("gx") - 1, lax.axis_size("gy") - 1

    def wetness(x):
        return 1.0 - 0.6 * x

    def own_cells(t, carry):
        at = pl.ds(pl.multiple_of(t * 128, 128), 128)
        drag[0:rows, at] = drag_ref[:, at]
        buoy[0:rows, at] = wetness(wet_ref[:, at].astype(jnp.float32))
        e = elem_ref[:, at]
        n = node_ref[:, at]
        surface_cols = 128 * (last_y + 1)
        er = lax.shift_right_logical(e, surface_cols.bit_length() - 1) if surface_cols & (surface_cols - 1) == 0 else e // surface_cols
        lx = er - 2 * at_x + 1
        ly = (e - er * surface_cols) - 128 * at_y + 1
        inside = (ly >= 1) & (ly <= 128)
        own_row = (lx == 1) | (lx == 2)
        half = jnp.where(own_row, 0, 1)
        line = 2 * n + jnp.where(lx >= 2, 1, 0)
        a = jnp.where(inside, line, 50)
        b = jnp.where(
            inside,
            half * 128 + ly - 1,
            jnp.where(ly == 0, 0, 128) + 64 * half + line,
        )
        row_slot[:, at] = a.astype(jnp.float32)
        col_slot[:, at] = b.astype(jnp.float32)
        return carry

    lax.fori_loop(0, cols // 128, own_cells, 0, unroll=True)
    arrive()

    sub = lax.broadcasted_iota(jnp.int32, (8, 128), 0)
    lane = lax.broadcasted_iota(jnp.int32, (8, 128), 1)
    up_half = sub < 4
    left_half = lane < 64

    def zero_rows(tile):
        tile = jnp.where(up_half & (at_x == last_x), 0.0, tile)
        return jnp.where(jnp.logical_not(up_half) & (at_x == 0), 0.0, tile)

    def zero_cols(tile):
        tile = jnp.where(left_half & (at_y == last_y), 0.0, tile)
        return jnp.where(jnp.logical_not(left_half) & (at_y == 0), 0.0, tile)

    def received(k, n, *at):
        if k < 6:
            return got[0][n][(k, *at)]
        tile = got[k - 5][n][at]
        return tile if k == 6 else tile.astype(jnp.float32)

    def place(k, r, c, tile):
        if k < 6:
            ext[0, k, r, c] = tile
        elif k == 6:
            drag[r, c] = tile
        else:
            buoy[r, c] = wetness(tile)

    tail = pl.ds(cols, 128)
    foot = pl.ds(rows, 8)
    ones = jnp.full((8, 128), 0.2, jnp.float32)
    row_scale = zero_rows(ones)
    col_scale = zero_cols(ones)

    def halo_rows(t, carry):
        at = pl.ds(pl.multiple_of(t * 128, 128), 128)
        for k in range(8):
            place(k, foot, at, zero_rows(received(k, 0, slice(None), at)))
        for r in range(0, rows, 8):
            scale[r : r + 8, at] = ones
        scale[foot, at] = row_scale
        return carry

    lax.fori_loop(0, cols // 128, halo_rows, 0, unroll=True)
    for k in range(8):
        for r in range(0, rows, 8):
            at = (slice(r, r + 8), slice(None))
            tile = jnp.where(left_half, received(k, 2, *at), received(k, 1, *at))
            place(k, pl.ds(r, 8), tail, zero_cols(tile))
        at = (slice(None), slice(None))
        tile = jnp.where(left_half, received(k, 4, *at), received(k, 3, *at))
        place(k, foot, tail, zero_cols(zero_rows(tile)))
    for r in range(0, rows, 8):
        scale[r : r + 8, tail] = col_scale
    scale[foot, tail] = zero_cols(row_scale)

    lanes = lax.broadcasted_iota(jnp.int32, (tall, 128), 1)
    first_lane = lanes == 0
    last_lane = lanes == 127
    tiles = wide // 128

    def press(f0, f1, b):
        return b * (f0 + f1), upper_gravity * density_ratio * f0 + upper_gravity * f1

    def step(now, carry, final=False):
        later = 1 - now
        height = rows if final else tall
        cells = slice(0, height)

        def tile_step(t, carry):
            at = pl.ds(pl.multiple_of(t * 128, 128), 128)
            t_hi = jnp.where(t == tiles - 1, 0, t + 1)
            t_lo = jnp.where(t == 0, tiles - 1, t - 1)
            at_hi = pl.ds(pl.multiple_of(t_hi * 128, 128), 128)
            at_lo = pl.ds(pl.multiple_of(t_lo * 128, 128), 128)
            f = [ext[now, k, :, at] for k in range(6)]
            b = buoy[:, at]
            one, two = press(f[0], f[1], b)
            sums = [None] * 6

            def add(k, value):
                sums[k] = value if sums[k] is None else sums[k] + value

            for ahead in (True, False):
                by = tall - 1 if ahead else 1
                def rolled(x):
                    return pltpu.roll(x, by, 0)[cells]
                def mix(x, y):
                    return x - y if ahead else x + y
                add(0, rolled(mix(f[0], f[2])))
                add(1, rolled(mix(f[1], f[4])))
                add(2, rolled(mix(f[2], one)))
                add(3, rolled(f[3]))
                add(4, rolled(mix(f[4], two)))
                add(5, rolled(f[5]))
            f = [x[cells] for x in f]
            b = b[cells]
            for ahead in (True, False):
                by = 127 if ahead else 1
                edge = (first_lane if ahead else last_lane)[cells]
                other = at_hi if ahead else at_lo
                g = [jnp.where(edge, ext[now, k, cells, other], f[k]) for k in range(6)]
                gb = jnp.where(edge, buoy[cells, other], b)
                g_one, g_two = press(g[0], g[1], gb)
                def rolled(x):
                    return pltpu.roll(x, by, 1)
                def mix(x, y):
                    return x - y if ahead else x + y
                add(0, rolled(mix(g[0], g[3])))
                add(1, rolled(mix(g[1], g[5])))
                add(2, rolled(g[2]))
                add(3, rolled(mix(g[3], g_one)))
                add(4, rolled(g[4]))
                add(5, rolled(mix(g[5], g_two)))
            speed = jnp.sqrt(f[2] * f[2] + f[3] * f[3] + speed_floor)
            rub = 2.0 * drag[cells, at] * speed
            k = scale[cells, at]
            new = (
                k * (f[0] + sums[0]),
                k * (f[1] + sums[1]),
                k * (sums[2] + f[4] - rub * f[2]),
                k * (sums[3] + f[5] - rub * f[3]),
                k * (sums[4] + f[2]),
                k * (sums[5] + f[3]),
            )
            for n, value in enumerate(new):
                ext[later, n, cells, at] = value
            if final:
                speed = jnp.sqrt(new[2] * new[2] + new[3] * new[3] + speed_floor)
                rub = load_factor * drag[cells, at] * speed
                tract[0, :, at] = rub * new[2]
                tract[1, :, at] = rub * new[3]
                tract[2, :, at] = -load_factor * (b * (new[0] + new[1]))
            return carry

        return lax.fori_loop(0, tiles - 1 if final else tiles, tile_step, carry, unroll=True)

    lax.fori_loop(0, FLOW_STEPS // 2 - 1, lambda _, carry: step(1, step(0, carry)), 0)
    step(1, step(0, 0), final=True)
    store_fields.start()

    table_ref[...] = jnp.zeros_like(table_ref)
    narrow = jnp.bfloat16
    row16 = lax.broadcasted_iota(jnp.int32, (16, cols), 0)
    count = row16.astype(jnp.float32).astype(narrow)

    def spread(group, carry):
        lefts, rights = [], []
        for n in range(GROUP):
            line = pl.ds(group * GROUP + n, 1)

            def wide16(x):
                return jnp.broadcast_to(x, (16, cols)).astype(narrow)

            parts = []
            for k in range(3):
                value = tract[k, line, :]
                high = value.astype(narrow).astype(jnp.float32)
                parts.append(wide16(value))
                parts.append(wide16(value - high))
            a = wide16(row_slot[line, :])
            b = wide16(col_slot[line, :])
            zero = jnp.zeros((16, cols), narrow)
            one = jnp.ones((16, cols), narrow)
            pieces = []
            for top in range(0, table_ref.shape[0], 16):
                part, last = top // SLOT_ROWS, min((top + 15) // SLOT_ROWS, 5)
                skip = top - SLOT_ROWS * part
                if part == last:
                    pieces.append(jnp.where(a == count + narrow(skip), parts[part], zero))
                else:
                    split = SLOT_ROWS * last - top
                    target = row16 + jnp.where(row16 < split, skip, -split)
                    mixed = jnp.where(count < narrow(split), parts[part], parts[last])
                    pieces.append(jnp.where(a == target.astype(jnp.float32).astype(narrow), mixed, zero))
            lefts.append(jnp.concatenate(pieces, axis=0))
            rights.append(
                jnp.concatenate([jnp.where(b == count + narrow(16 * m), one, zero) for m in range(16)], axis=0)
            )
        table_ref[...] += lax.dot_general(
            jnp.concatenate(lefts, axis=1),
            jnp.concatenate(rights, axis=1),
            (((1,), (1,)), ((), ())),
            preferred_element_type=jnp.float32,
        )
        return carry

    lax.fori_loop(0, rows // GROUP, spread, 0)

    def part_rows(n):
        return table_ref[SLOT_ROWS * n : SLOT_ROWS * n + SLOT_ROWS]

    pad = jnp.zeros((64 - SLOT_ROWS, 256), jnp.float32)
    table = [
        jnp.concatenate([part_rows(2 * k) + part_rows(2 * k + 1), pad], axis=0) for k in range(3)
    ]
    load_parts(table, own_ref, beyond_ref, sides_ref)


def line(matrix, s):
    even = [s[0] + s[4], s[1] + s[3]]
    odd = [s[0] - s[4], s[1] - s[3]]
    out = [None] * 5
    for a in range(2):
        half_sum = [0.5 * (matrix[a, p] - matrix[a, 4 - p]) for p in range(2)]
        half_diff = [0.5 * (matrix[a, p] + matrix[a, 4 - p]) for p in range(2)]
        x = float(half_sum[0]) * odd[0] + float(half_sum[1]) * odd[1]
        y = float(half_diff[0]) * even[0] + float(half_diff[1]) * even[1] + float(matrix[a, 2]) * s[2]
        out[a] = x + y
        out[4 - a] = x - y
    out[2] = float(matrix[2, 0]) * odd[0] + float(matrix[2, 1]) * odd[1]
    return out


def lane_row():
    lane = lax.broadcasted_iota(jnp.int32, (4, 128), 1)
    row = lax.broadcasted_iota(jnp.int32, (4, 128), 0)
    return lane, row


def internal_open(u_ref, lame_ref, shear_ref, stress, force):
    table = derivative_table()

    def slope_x(m, carry):
        for i in range(3):
            lines = line(table, [u_ref[i * 125 + a * 25 + m] for a in range(5)])
            for a in range(5):
                stress[i * 125 + a * 25 + m] = lines[a]
        return carry

    lax.fori_loop(0, 25, slope_x, 0, unroll=True)

    def plane(a, carry):
        weight = jnp.where(
            (a == 0) | (a == 4),
            np.float32(gll_weights[0]),
            jnp.where(a == 2, np.float32(gll_weights[2]), np.float32(gll_weights[1])),
        )
        lame = lame_ref[...] * -weight
        shear = shear_ref[...] * -weight

        def at(i, b, c):
            return i * 125 + a * 25 + b * 5 + c

        slope_y, slope_z = [], []
        for i in range(3):
            u = [[u_ref[at(i, b, c)] for c in range(5)] for b in range(5)]
            along_y = [line(table, [u[b][c] for b in range(5)]) for c in range(5)]
            slope_y.append([[along_y[c][b] for c in range(5)] for b in range(5)])
            slope_z.append([line(table, u[b]) for b in range(5)])
        pull_y = [[[None] * 5 for b in range(5)] for i in range(3)]
        pull_z = [[[None] * 5 for b in range(5)] for i in range(3)]
        for b in range(5):
            for c in range(5):
                w = np.float32(gll_weights[b] * gll_weights[c])
                g = [[stress[at(i, b, c)], slope_y[i][b][c], slope_z[i][b][c]] for i in range(3)]
                mu = shear * w
                twice = mu + mu
                spread = (lame * w) * (g[0][0] + g[1][1] + g[2][2])
                s00 = spread + twice * g[0][0]
                s11 = spread + twice * g[1][1]
                s22 = spread + twice * g[2][2]
                s01 = mu * (g[0][1] + g[1][0])
                s02 = mu * (g[0][2] + g[2][0])
                s12 = mu * (g[1][2] + g[2][1])
                stress[at(0, b, c)] = s00
                stress[at(1, b, c)] = s01
                stress[at(2, b, c)] = s02
                for i, (s_y, s_z) in enumerate(((s01, s02), (s11, s12), (s12, s22))):
                    pull_y[i][b][c] = s_y
                    pull_z[i][b][c] = s_z
        for i in range(3):
            along_y = [line(table.T, [pull_y[i][b][c] for b in range(5)]) for c in range(5)]
            for b in range(5):
                along_z = line(table.T, pull_z[i][b])
                for c in range(5):
                    force[at(i, b, c)] = along_y[c][b] + along_z[c]
        return carry

    lax.fori_loop(0, 5, plane, 0)


def internal_kick(kick, lame_ref, shear_ref, force):
    table = derivative_table()
    lame, shear = -lame_ref[...], -shear_ref[...]
    five = range(5)

    def grid(make):
        return [[make(a, b) for b in five] for a in five]

    def along_x(matrix, x):
        lines = [line(matrix, [x[a][b] for a in five]) for b in five]
        return grid(lambda a, b: lines[b][a])

    def along_y(matrix, x):
        lines = [line(matrix, x[a]) for a in five]
        return grid(lambda a, b: lines[a][b])

    def plus(x, y):
        return grid(lambda a, b: x[a][b] + y[a][b])

    def area(a, b):
        return np.float32(gll_weights[a] * gll_weights[b])

    d = [grid(lambda a, b: kick[i * 25 + a * 5 + b]) for i in range(3)]
    d_x = [along_x(table, x) for x in d]
    d_y = [along_y(table, x) for x in d]
    lame_w = grid(lambda a, b: lame * area(a, b))
    shear_w = grid(lambda a, b: shear * area(a, b))
    t_side = grid(lambda a, b: lame_w[a][b] * d[2][a][b])
    t_02 = grid(lambda a, b: shear_w[a][b] * d[0][a][b])
    t_12 = grid(lambda a, b: shear_w[a][b] * d[1][a][b])
    t_22 = grid(lambda a, b: t_side[a][b] + (shear_w[a][b] + shear_w[a][b]) * d[2][a][b])
    first = np.float32(gll_weights[0])
    l_0 = grid(lambda a, b: first * lame_w[a][b])
    m_0 = grid(lambda a, b: first * shear_w[a][b])
    e_22 = grid(lambda a, b: l_0[a][b] * (d_x[0][a][b] + d_y[1][a][b]))
    e_00 = grid(lambda a, b: e_22[a][b] + (m_0[a][b] + m_0[a][b]) * d_x[0][a][b])
    e_11 = grid(lambda a, b: e_22[a][b] + (m_0[a][b] + m_0[a][b]) * d_y[1][a][b])
    e_01 = grid(lambda a, b: m_0[a][b] * (d_y[0][a][b] + d_x[1][a][b]))
    e_02 = grid(lambda a, b: m_0[a][b] * d_x[2][a][b])
    e_12 = grid(lambda a, b: m_0[a][b] * d_y[2][a][b])
    turned = table.T
    pulled = (
        along_x(turned, t_side),
        along_y(turned, t_side),
        plus(along_x(turned, t_02), along_y(turned, t_12)),
    )
    flat = (
        plus(along_x(turned, e_00), along_y(turned, e_01)),
        plus(along_x(turned, e_01), along_y(turned, e_11)),
        plus(along_x(turned, e_02), along_y(turned, e_12)),
    )
    share = [float(table[c, 0] * gll_weights[c]) for c in five]
    upright = [float(sum(table[p, c] * share[p] for p in five)) for c in five]
    for i, (t, e) in enumerate(((t_02, e_02), (t_12, e_12), (t_22, e_22))):
        for a in five:
            for b in five:
                for c in five:
                    value = share[c] * pulled[i][a][b] + upright[c] * t[a][b]
                    value = value + float(table[0, c]) * e[a][b]
                    if c == 0:
                        value = value + flat[i][a][b]
                    force[i * 125 + a * 25 + b * 5 + c] += value


def internal_close(stress, force):
    table = derivative_table()
    lane, row = lane_row()
    low_x = row % 2 == 0
    low_z = row < 2

    def close_x(m, carry):
        for i in range(3):
            pulled = line(table.T, [stress[i * 125 + a * 25 + m] for a in range(5)])
            f = [force[i * 125 + a * 25 + m] + pulled[a] for a in range(5)]
            near = f[0] + jnp.where(low_x, 0.0, pltpu.roll(f[4], 1, 0))
            far = f[4] + jnp.where(low_x, pltpu.roll(f[0], 3, 0), 0.0)
            for a, value in enumerate((near, f[1], f[2], f[3], far)):
                force[i * 125 + a * 25 + m] = value
        return carry

    lax.fori_loop(0, 25, close_x, 0, unroll=True)

    def close_yz(ia, carry):
        base = ia * 25
        f = [[force[base + b * 5 + c] for c in range(5)] for b in range(5)]
        for c in range(5):
            near, far = f[0][c], f[4][c]
            f[0][c] = near + jnp.where(lane == 0, 0.0, pltpu.roll(far, 1, 1))
            f[4][c] = far + jnp.where(lane == 127, 0.0, pltpu.roll(near, 127, 1))
        for b in range(5):
            near, far = f[b][0], f[b][4]
            f[b][0] = near + jnp.where(low_z, 0.0, pltpu.roll(far, 2, 0))
            f[b][4] = far + jnp.where(low_z, pltpu.roll(near, 2, 0), 0.0)
        for b in range(5):
            for c in range(5):
                if b in (0, 4) or c in (0, 4):
                    force[base + b * 5 + c] = f[b][c]
        return carry

    lax.fori_loop(0, 15, close_yz, 0, unroll=True)


def pack_faces(force, face_x, face_y):
    lane, row = lane_row()
    low_x = row % 2 == 0

    def both(m, other):
        for i in range(3):
            near, far = force[i * 125 + m], force[i * 125 + 100 + m]
            near_other, far_other = force[i * 125 + other], force[i * 125 + 100 + other]
            face_x[0, i * 13 + m] = jnp.where(low_x, near, pltpu.roll(near_other, 1, 0))
            face_x[1, i * 13 + m] = jnp.where(low_x, pltpu.roll(far, 3, 0), far_other)

    def pack_x(m, carry):
        both(m, m + 13)
        return carry

    lax.fori_loop(0, 12, pack_x, 0, unroll=True)
    both(12, 12)
    ends = [jnp.zeros((4, 128), jnp.float32)] * 2
    for a in range(5):
        for i in range(3):
            for c in range(5):
                q = a * 15 + i * 5 + c
                n = i * 125 + a * 25 + c
                ends[0] = jnp.where(lane == q, pltpu.roll(force[n], q, 1), ends[0])
                ends[1] = jnp.where(lane == q, pltpu.roll(force[n + 20], q + 1, 1), ends[1])
    face_y[0] = ends[0]
    face_y[1] = ends[1]


def open_edges():
    at_x, at_y = lax.axis_index("gx"), lax.axis_index("gy")
    has = {-1: at_x > 0, 1: at_x < lax.axis_size("gx") - 1}
    has_y = {-1: at_y > 0, 1: at_y < lax.axis_size("gy") - 1}
    return has, has_y


def add_faces(target, got_x, got_y, factor):
    has_x, has_y = open_edges()
    lane, row = lane_row()
    low_x = row % 2 == 0
    from_low = low_x & has_x[-1]
    from_high = jnp.logical_not(low_x) & has_x[1]
    for m in range(13):
        for i in range(3):
            low, high = got_x[0][i * 13 + m], got_x[1][i * 13 + m]
            pairs = [(m, low, pltpu.roll(high, 1, 0))]
            if m < 12:
                pairs.append((m + 13, pltpu.roll(low, 3, 0), high))
            for at, near, far in pairs:
                b, c = at // 5, at % 5
                target[i * 125 + at] += factor(0, b, c, jnp.where(from_low, near, 0.0))
                target[i * 125 + 100 + at] += factor(4, b, c, jnp.where(from_high, far, 0.0))
    first, final = lane < 15, (lane >= 60) & (lane < 75)
    columns = []
    for side, end in ((-1, 1), (1, 0)):
        straight = got_y[0, side][end]
        low = pltpu.roll(pltpu.roll(got_y[-1, side][end], 68, 1), 3, 0)
        high = pltpu.roll(pltpu.roll(got_y[1, side][end], 60, 1), 1, 0)
        total = straight + jnp.where(first & low_x & has_x[-1], low, 0.0)
        total = total + jnp.where(final & jnp.logical_not(low_x) & has_x[1], high, 0.0)
        columns.append(jnp.where(has_y[side], total, 0.0))
    for a in range(5):
        for i in range(3):
            for c in range(5):
                q = a * 15 + i * 5 + c
                n = i * 125 + a * 25 + c
                near = jnp.where(lane == 0, pltpu.roll(columns[0], (128 - q) % 128, 1), 0.0)
                far = jnp.where(lane == 127, pltpu.roll(columns[1], 127 - q, 1), 0.0)
                target[n] += factor(a, 0, c, near)
                target[n + 20] += factor(a, 4, c, far)


def inverse_masses(density_ref, around, inverse):
    has_x, has_y = open_edges()
    lane, row = lane_row()
    low_x = row % 2 == 0
    low_z = row < 2

    def beside(mine, left, right):
        left = jnp.where(has_y[-1], left, 0.0)
        right = jnp.where(has_y[1], right, 0.0)
        before = jnp.where(lane == 0, pltpu.roll(left, 1, 1), pltpu.roll(mine, 1, 1))
        after = jnp.where(lane == 127, pltpu.roll(right, 127, 1), pltpu.roll(mine, 127, 1))
        return mine + before, mine, mine + after

    mine = beside(density_ref[...], around[0, -1][...], around[0, 1][...])
    low = beside(around[-1, 0][...], around[-1, -1][...], around[-1, 1][...])
    high = beside(around[1, 0][...], around[1, -1][...], around[1, 1][...])
    for b in range(3):
        lo = jnp.where(has_x[-1], low[b], 0.0)
        hi = jnp.where(has_x[1], high[b], 0.0)
        before = mine[b] + jnp.where(low_x, pltpu.roll(lo, 3, 0), pltpu.roll(mine[b], 1, 0))
        after = mine[b] + jnp.where(low_x, pltpu.roll(mine[b], 3, 0), pltpu.roll(hi, 1, 0))
        for a, value in enumerate((before, mine[b], after)):
            top = value + jnp.where(low_z, 0.0, pltpu.roll(value, 2, 0))
            bottom = value + jnp.where(low_z, pltpu.roll(value, 2, 0), 0.0)
            for c, total in enumerate((top, value, bottom)):
                inverse[a * 9 + b * 3 + c] = (solid_dt * solid_dt) / total


def kind(node):
    return 0 if node == 0 else 2 if node == 4 else 1


def moved_by(inverse, a, b, c, f):
    w = np.float32(1.0 / (gll_weights[a] * gll_weights[b] * gll_weights[c]))
    return (inverse[kind(a) * 9 + kind(b) * 3 + kind(c)] * w) * f


def advance_solid(force, load, inverse, now_ref, before_ref, out_ref):
    def component(i, carry):
        for a in range(5):
            for b in range(5):
                for c in range(5):
                    n = a * 25 + b * 5 + c
                    f = force[i * 125 + n]
                    if c == 0 and load is not None:
                        f = f + load[i * 25 + a * 5 + b]
                    step = moved_by(inverse, a, b, c, f)
                    at = i * 125 + n
                    out_ref[at] = (now_ref[at] + now_ref[at] - before_ref[at]) + step
        return carry

    lax.fori_loop(0, 3, component, 0)


def kick_solid(load, inverse, out_ref, kick):
    def component(i, carry):
        for a in range(5):
            for b in range(5):
                n = i * 25 + a * 5 + b
                step = moved_by(inverse, a, b, 0, load[n])
                kick[n] = step
                out_ref[i * 125 + a * 25 + b * 5] += step
        return carry

    lax.fori_loop(0, 3, component, 0)


def load_grid():
    row = lax.broadcasted_iota(jnp.int32, (56, 128), 0)
    lane = lax.broadcasted_iota(jnp.int32, (56, 128), 1)
    return row, lane


def rows_up(x, by):
    return jnp.concatenate([x[by:], jnp.zeros((by, 128), jnp.float32)], axis=0)


def rows_down(x, by):
    return jnp.concatenate([jnp.zeros((by, 128), jnp.float32), x[:-by]], axis=0)


def masks_x():
    row, lane = load_grid()
    even = row % 2 == 0
    odd = row % 2 == 1
    return (row < 10) & even, (row < 10) & odd, (row >= 40) & (row < 50) & even, (row >= 40) & (row < 50) & odd


def masks_y():
    row, lane = load_grid()
    place = row % 10
    return (place < 2) & (row < 50), (place >= 8) & (row < 50), lane == 0, lane == 127


def join_x(x):
    near_even, near_odd, far_even, far_odd = masks_x()
    return (
        x
        + jnp.where(near_odd, pltpu.roll(rows_up(x, 40), 1, 0), 0.0)
        + jnp.where(far_even, pltpu.roll(rows_down(x, 40), 55, 0), 0.0)
    )


def join_x_wide(own, halo):
    near_even, near_odd, far_even, far_odd = masks_x()
    own_new = join_x(own)
    own_new = own_new + jnp.where(near_even, rows_up(halo, 40), 0.0)
    own_new = own_new + jnp.where(far_odd, rows_down(halo, 40), 0.0)
    halo_new = halo + jnp.where(far_even, rows_down(own, 40), 0.0)
    halo_new = halo_new + jnp.where(near_odd, rows_up(own, 40), 0.0)
    return own_new, halo_new


def join_y(x, sides):
    near, far, first, final = masks_y()
    before, after = pltpu.roll(x, 1, 1), pltpu.roll(x, 127, 1)
    fill_before = 0.0 if sides is None else pltpu.roll(sides, 1, 1)
    fill_after = 0.0 if sides is None else pltpu.roll(sides, 127, 1)
    out = x + jnp.where(near, rows_up(jnp.where(first, fill_before, before), 8), 0.0)
    out = out + jnp.where(far, rows_down(jnp.where(final, fill_after, after), 8), 0.0)
    if sides is None:
        return out
    new = sides + jnp.where(far & final, rows_down(after, 8), 0.0)
    new = new + jnp.where(near & first, rows_up(before, 8), 0.0)
    return out, new


def columns_from(tile):
    row, lane = load_grid()
    turned = jnp.concatenate([tile, jnp.zeros((120, 128), jnp.float32)], axis=0).T
    out = []
    for k in range(3):
        halves = []
        for h in range(2):
            part = turned[64 * h : 64 * h + 56]
            left = pltpu.roll(part, 127 - 2 * k, 1)
            right = pltpu.roll(part, (128 - 2 * k - 1) % 128, 1)
            value = jnp.where(lane == 127, left, jnp.where(lane == 0, right, 0.0))
            halves.append(jnp.where(row < 50, value, 0.0))
        out.append(halves)
    return out


def columns_to(columns):
    lane = lax.broadcasted_iota(jnp.int32, (128, 128), 1)
    total = jnp.zeros((128, 128), jnp.float32)
    for k in range(3):
        pad = jnp.zeros((8, 128), jnp.float32)
        x = jnp.concatenate([columns[k][0], pad, columns[k][1], pad], axis=0)
        total = jnp.where(lane == 2 * k, pltpu.roll(x, 2 * k + 1, 1), total)
        total = jnp.where(lane == 2 * k + 1, pltpu.roll(x, 2 * k + 1, 1), total)
    return total.T[:8]


def load_parts(table, own_ref, beyond_ref, sides_ref):
    row, lane = load_grid()
    line_of = lax.broadcasted_iota(jnp.int32, (8, 128), 0)
    raw = jnp.zeros((8, 128), jnp.float32)
    for k in range(3):
        for side in range(2):
            last = jnp.broadcast_to(table[k][50:51, 128 * side : 128 * side + 128], (8, 128))
            raw = jnp.where(line_of == 2 * k + side, last, raw)
    columns = columns_from(raw)
    new_columns = []
    for k in range(3):
        own = jnp.where(row < 50, table[k][:56, :128], 0.0)
        halo = jnp.where(row < 50, table[k][:56, 128:], 0.0)
        own, halo = join_x_wide(own, halo)
        sides = join_x_wide(columns[k][0], columns[k][1])
        own, side_own = join_y(own, sides[0])
        halo, side_halo = join_y(halo, sides[1])
        own_ref[k] = own
        beyond_ref[k] = halo
        new_columns.append((side_own, side_halo))
    sides_ref[...] = columns_to(new_columns)


def load_total(own_ref, got_x, got_y, load):
    has_x, has_y = open_edges()
    row, lane = load_grid()
    even = row % 2 == 0
    tile_lane = lax.broadcasted_iota(jnp.int32, (8, 128), 1)
    tile_row = lax.broadcasted_iota(jnp.int32, (8, 128), 0)
    ends = []
    for side in (-1, 1):
        low = jnp.where(has_x[-1], pltpu.roll(got_y[-1, side][...], 127, 1), 0.0)
        high = jnp.where(has_x[1], pltpu.roll(got_y[1, side][...], 1, 1), 0.0)
        tile = jnp.where(tile_lane < 64, got_y[0, side][...], jnp.where(tile_lane % 2 == 0, low, high))
        ends.append(jnp.where(has_y[side], tile, 0.0))
    columns = columns_from(jnp.where(tile_row % 2 == 0, ends[1], ends[0]))
    for k in range(3):
        low = jnp.where(has_x[-1], pltpu.roll(got_x[0][k], 55, 0), 0.0)
        high = jnp.where(has_x[1], pltpu.roll(got_x[1][k], 1, 0), 0.0)
        rows = jnp.where(even, low, high) + join_y(columns[k][1], None)
        total = own_ref[k] + join_x(jnp.where(row < 50, rows, 0.0)) + join_y(columns[k][0], None)
        for n in range(25):
            load[k * 25 + n] = jnp.concatenate(
                [total[2 * n : 2 * n + 2], jnp.zeros((2, 128), jnp.float32)], axis=0
            )


AROUND = [(-1, 0), (1, 0), (0, -1), (0, 1), (-1, -1), (-1, 1), (1, -1), (1, 1)]
ASIDE = AROUND[2:]


def shape(*dims, kind=jnp.float32):
    return jax.ShapeDtypeStruct(dims, kind)


def halo_plan(rows, cols):
    edge_rows = {-1: pl.ds(0, 4), 1: pl.ds(rows - 4, 4)}
    edge_cols = {-1: pl.ds(0, 128), 1: pl.ds(cols - 128, 128)}
    place_rows = {-1: pl.ds(0, 4), 1: pl.ds(4, 4)}
    messages = []
    for source in range(3):
        every = (slice(None),) if source == 0 else ()
        for dx, dy in AROUND:
            row_in = edge_rows.get(dx, pl.ds(0, rows))
            row_out = place_rows.get(dx, pl.ds(0, rows))
            col_in = edge_cols.get(dy, pl.ds(0, cols))
            where = 0 if dy == 0 else (1 if dx == 0 else 3) + (0 if dy == 1 else 1)
            messages.append(
                (source, every + (row_in, col_in), 5 * source + where,
                 every + (row_out, pl.ds(0, cols if dy == 0 else 128)), (dx, dy))
            )
    return messages


def whole_body(*refs):
    (flow_in, drag_in, wet_in, elem_in, node_in, u_in, before_in, density_in, lame_in, shear_in) = refs[:10]
    fields_out, next_out, last_out = refs[10:13]
    (ext, drag, buoy, scale, tract, row_slot, col_slot, table) = refs[13:21]
    halos = refs[21:36]
    (drag_own, wet_own, elem_own, node_own) = refs[36:40]
    (u_zero, before, u_one, u_two, force, stress, load, inverse) = refs[40:48]
    (density, lame, shear, around) = refs[48:52]
    (face_x, face_y, got_face_x, got_face_y) = refs[52:56]
    (own, beyond, sides, got_beyond, got_sides, kick) = refs[56:62]
    local_sem, sent, come = refs[62:]
    rows, cols = drag_own.shape
    at_x, at_y = lax.axis_index("gx"), lax.axis_index("gy")
    size_x, size_y = lax.axis_size("gx"), lax.axis_size("gy")

    def device(move):
        return ((at_x + move[0] + size_x) % size_x, (at_y + move[1] + size_y) % size_y)

    def opposite(move):
        return -move[0], -move[1]

    def there(move):
        x, y = at_x + move[0], at_y + move[1]
        return (x >= 0) & (x < size_x) & (y >= 0) & (y < size_y)

    barrier = pltpu.get_barrier_semaphore()
    for move in AROUND:

        @pl.when(there(move))
        def _(move=move):
            pl.semaphore_signal(barrier, inc=1, device_id=device(move), device_id_type=pl.DeviceIdType.MESH)

    reads = [
        pltpu.make_async_copy(source, target, local_sem.at[n])
        for n, (source, target) in enumerate(
            (
                (u_in, u_zero), (lame_in, lame), (shear_in, shear), (density_in, density),
                (flow_in, ext.at[0, :, 0:rows, 0:cols]), (drag_in, drag_own), (wet_in, wet_own),
                (elem_in, elem_own), (node_in, node_own), (before_in, before),
            )
        )
    ]
    for copy in reads:
        copy.start()
    store_fields = pltpu.make_async_copy(ext.at[0, :, 0:rows, 0:cols], fields_out, local_sem.at[10])
    store_last = pltpu.make_async_copy(u_one, last_out, local_sem.at[11])
    store_next = pltpu.make_async_copy(u_two, next_out, local_sem.at[12])
    beside_x = 3 - jnp.where(at_x == 0, 1, 0) - jnp.where(at_x == size_x - 1, 1, 0)
    beside_y = 3 - jnp.where(at_y == 0, 1, 0) - jnp.where(at_y == size_y - 1, 1, 0)
    pl.semaphore_wait(barrier, beside_x * beside_y - 1)
    number = [0]

    def send(source, target, move):
        n = number[0]
        number[0] += 1
        copy = pltpu.make_async_remote_copy(
            src_ref=source, dst_ref=target, send_sem=sent.at[n], recv_sem=come.at[n],
            device_id=device(move), device_id_type=pl.DeviceIdType.MESH,
        )
        return copy, move

    def each(messages, toward, act):
        for move in AROUND:
            mine = [copy for copy, way in messages if way == move]
            if mine:

                @pl.when(there(move if toward else opposite(move)))
                def _(mine=mine):
                    for copy in mine:
                        act(copy)

    def launch(messages):
        each(messages, True, lambda copy: copy.start())

    def finish(messages):
        each(messages, False, lambda copy: copy.wait_recv())

    def drain(messages):
        each(messages, True, lambda copy: copy.wait_send())

    operands = (flow_in, drag_in, wet_in)
    first = [
        send(operands[source].at[source_at], halos[target].at[target_at], move)
        for source, source_at, target, target_at, move in halo_plan(rows, cols)
    ]
    first += [send(density_in, around.at[AROUND.index(opposite(move))], move) for move in AROUND]
    launch(first)

    def send_faces(step):
        copies = [send(face_x.at[step, 0], got_face_x.at[step, 1], (-1, 0))]
        copies += [send(face_x.at[step, 1], got_face_x.at[step, 0], (1, 0))]
        for move in ASIDE:
            copies.append(send(face_y.at[step], got_face_y.at[step, ASIDE.index(opposite(move))], move))
        launch(copies)
        return copies

    def faces_of(step):
        return (
            [got_face_x.at[step, n] for n in range(2)],
            {move: got_face_y.at[step, n] for n, move in enumerate(ASIDE)},
        )

    for copy in reads[:3]:
        copy.wait()
    internal_open(u_zero, lame, shear, stress, force)
    internal_close(stress, force)
    pack_faces(force, face_x.at[0], face_y.at[0])
    faces = send_faces(0)
    for copy in reads[3:]:
        copy.wait()

    def arrive():
        finish(first)
        inverse_masses(density, {move: around.at[n] for n, move in enumerate(AROUND)}, inverse)

    surface(
        drag_own, wet_own, elem_own, node_own, arrive, (halos[0:5], halos[5:10], halos[10:15]),
        own, beyond, sides, ext, drag, buoy, scale, tract, row_slot, col_slot, table, store_fields,
    )
    loads = [send(beyond, got_beyond.at[1], (-1, 0)), send(beyond, got_beyond.at[0], (1, 0))]
    for move in ASIDE:
        loads.append(send(sides, got_sides.at[ASIDE.index(opposite(move))], move))
    launch(loads)
    finish(faces)
    add_faces(force, *faces_of(0), lambda a, b, c, f: f)
    advance_solid(force, None, inverse, u_zero, before, u_one)
    internal_open(u_one, lame, shear, stress, force)
    finish(loads)
    load_total(
        own,
        [got_beyond.at[n] for n in range(2)],
        {move: got_sides.at[n] for n, move in enumerate(ASIDE)},
        load,
    )
    kick_solid(load, inverse, u_one, kick)
    store_last.start()
    internal_kick(kick, lame, shear, force)
    internal_close(stress, force)
    pack_faces(force, face_x.at[1], face_y.at[1])
    last_faces = send_faces(1)
    advance_solid(force, load, inverse, u_one, u_zero, u_two)
    finish(last_faces)
    add_faces(u_two, *faces_of(1), lambda a, b, c, f: moved_by(inverse, a, b, c, f))
    store_next.start()
    drain(first + faces + loads + last_faces)
    store_fields.wait()
    store_last.wait()
    store_next.wait()


def store_body(*refs):
    taken, given = refs[9:]
    reads, writes = [], []
    for n in range(3):
        source, target, held = refs[n], refs[3 + n], refs[6 + n]
        step = source.shape[0] // 3
        for m in range(3):
            part = pl.ds(m * step, step)
            at = 3 * n + m
            reads.append(pltpu.make_async_copy(source.at[part], held.at[part], taken.at[at]))
            writes.append(pltpu.make_async_copy(held.at[part], target.at[part], given.at[at]))
    for copy in reads:
        copy.start()
    for read, write in zip(reads, writes):
        read.wait()
        write.start()
    for copy in writes:
        copy.wait()


def per_device(
    flow_state,
    drag_coefficient,
    wet_mask,
    target_elem,
    target_node,
    displacement,
    previous,
    density,
    lame_first,
    shear_modulus,
):
    rows, cols = drag_coefficient.shape
    tall, wide = rows + 8, cols + 128
    grid = displacement.shape
    nodes = (375, 4, 128)
    halo_shapes = []
    for lead, kind_of in (((6,), jnp.float32), ((), jnp.float32), ((), jnp.int32)):
        for dims in ((8, cols), (rows, 128), (rows, 128), (8, 128), (8, 128)):
            halo_shapes.append(pltpu.VMEM((*lead, *dims), kind_of))

    def floats(*dims):
        return pltpu.VMEM(dims, jnp.float32)

    def integers(*dims):
        return pltpu.VMEM(dims, jnp.int32)

    scratch = [
        floats(2, 6, tall, wide), floats(tall, wide), floats(tall, wide), floats(tall, wide),
        floats(3, rows, cols), floats(rows, cols), floats(rows, cols), floats(320, 256),
        *halo_shapes,
        floats(rows, cols), integers(rows, cols), integers(rows, cols), integers(rows, cols),
        *[floats(*nodes)] * 6, floats(75, 4, 128), floats(27, 4, 128),
        floats(4, 128), floats(4, 128), floats(4, 128), floats(8, 4, 128),
        floats(2, 2, 39, 4, 128), floats(2, 2, 4, 128), floats(2, 2, 39, 4, 128), floats(2, 6, 2, 4, 128),
        floats(3, 56, 128), floats(3, 56, 128), floats(8, 128), floats(2, 3, 56, 128), floats(6, 8, 128), floats(75, 4, 128),
        pltpu.SemaphoreType.DMA((13,)), pltpu.SemaphoreType.DMA((56,)), pltpu.SemaphoreType.DMA((56,)),
    ]
    anywhere = pl.BlockSpec(memory_space=pl.ANY)
    results = pl.pallas_call(
        whole_body,
        out_shape=(shape(6, rows, cols), shape(*nodes), shape(*nodes)),
        in_specs=[anywhere] * 10,
        out_specs=(anywhere,) * 3,
        scratch_shapes=scratch,
        compiler_params=pltpu.CompilerParams(
            collective_id=1, has_side_effects=True, vmem_limit_bytes=56 * 2**20
        ),
    )(
        flow_state, drag_coefficient, wet_mask, target_elem, target_node,
        displacement.reshape(nodes), previous.reshape(nodes),
        *(x.reshape(4, 128) for x in (density, lame_first, shear_modulus)),
    )
    fields, u_two, u_one = pl.pallas_call(
        store_body,
        out_shape=tuple(shape(*x.shape) for x in results),
        in_specs=[anywhere] * 3,
        out_specs=(anywhere,) * 3,
        scratch_shapes=[
            *[pltpu.VMEM(x.shape, jnp.float32) for x in results],
            pltpu.SemaphoreType.DMA((9,)), pltpu.SemaphoreType.DMA((9,)),
        ],
        compiler_params=pltpu.CompilerParams(vmem_limit_bytes=60 * 2**20),
    )(*results)
    return (fields, u_two.reshape(grid), u_one.reshape(grid))


def solution(mesh):
    return jax.shard_map(
        per_device,
        mesh=mesh,
        in_specs=(
            P(None, "gx", "gy"),
            P("gx", "gy"),
            P("gx", "gy"),
            P("gx", "gy"),
            P("gx", "gy"),
            P(None, None, None, None, None, "gx", "gy"),
            P(None, None, None, None, None, "gx", "gy"),
            P(None, "gx", "gy"),
            P(None, "gx", "gy"),
            P(None, "gx", "gy"),
        ),
        out_specs=(
            P(None, "gx", "gy"),
            P(None, None, None, None, None, "gx", "gy"),
            P(None, None, None, None, None, "gx", "gy"),
        ),
        check_vma=False,
    )
```

```python
import jax
import jax.numpy as jnp
import numpy as np
from jax import lax
from jax.experimental import pallas as pl
from jax.experimental.pallas import tpu as pltpu
from jax.sharding import PartitionSpec as P

FLOW_STEPS = 4
SOLID_STEPS = 2
SLOT_ROWS = 51
GROUP = 8


gll_points = np.array([-1.0, -np.sqrt(3.0 / 7.0), 0.0, np.sqrt(3.0 / 7.0), 1.0])
gll_weights = np.array([0.1, 49.0 / 90.0, 32.0 / 45.0, 49.0 / 90.0, 0.1])
flow_dt = 0.4
diffusion = 0.2
coupling = 0.5
upper_gravity = 0.8
density_ratio = 0.7
speed_floor = 0.0001
load_factor = 4.0
solid_dt = 0.04


def legendre_four(x):
    return (35.0 * x**4 - 30.0 * x**2 + 3.0) / 8.0


def derivative_table():
    result = np.zeros((5, 5))
    for i in range(5):
        for j in range(5):
            if i != j:
                result[i, j] = (
                    legendre_four(gll_points[i])
                    / legendre_four(gll_points[j])
                    / (gll_points[i] - gll_points[j])
                )
    result[0, 0] = -5.0
    result[4, 4] = 5.0
    return result


def surface(
    drag_ref, wet_ref, elem_ref, node_ref, arrive, got, own_ref, beyond_ref, sides_ref,
    ext, drag, buoy, scale, tract, row_slot, col_slot, table_ref, store_fields,
):
    rows, cols = drag_ref.shape
    wide = cols + 128
    tall = rows + 8
    at_x, at_y = lax.axis_index("gx"), lax.axis_index("gy")
    last_x, last_y = lax.axis_size("gx") - 1, lax.axis_size("gy") - 1

    def wetness(x):
        return 1.0 - 0.6 * x

    def own_cells(t, carry):
        at = pl.ds(pl.multiple_of(t * 128, 128), 128)
        drag[0:rows, at] = drag_ref[:, at]
        buoy[0:rows, at] = wetness(wet_ref[:, at].astype(jnp.float32))
        e = elem_ref[:, at]
        n = node_ref[:, at]
        surface_cols = 128 * (last_y + 1)
        er = lax.shift_right_logical(e, surface_cols.bit_length() - 1) if surface_cols & (surface_cols - 1) == 0 else e // surface_cols
        lx = er - 2 * at_x + 1
        ly = (e - er * surface_cols) - 128 * at_y + 1
        inside = (ly >= 1) & (ly <= 128)
        own_row = (lx == 1) | (lx == 2)
        half = jnp.where(own_row, 0, 1)
        line = 2 * n + jnp.where(lx >= 2, 1, 0)
        a = jnp.where(inside, line, 50)
        b = jnp.where(
            inside,
            half * 128 + ly - 1,
            jnp.where(ly == 0, 0, 128) + 64 * half + line,
        )
        row_slot[:, at] = a.astype(jnp.float32)
        col_slot[:, at] = b.astype(jnp.float32)
        return carry

    lax.fori_loop(0, cols // 128, own_cells, 0, unroll=True)
    arrive()

    sub = lax.broadcasted_iota(jnp.int32, (8, 128), 0)
    lane = lax.broadcasted_iota(jnp.int32, (8, 128), 1)
    up_half = sub < 4
    left_half = lane < 64

    def zero_rows(tile):
        tile = jnp.where(up_half & (at_x == last_x), 0.0, tile)
        return jnp.where(jnp.logical_not(up_half) & (at_x == 0), 0.0, tile)

    def zero_cols(tile):
        tile = jnp.where(left_half & (at_y == last_y), 0.0, tile)
        return jnp.where(jnp.logical_not(left_half) & (at_y == 0), 0.0, tile)

    def received(k, n, *at):
        if k < 6:
            return got[0][n][(k, *at)]
        tile = got[k - 5][n][at]
        return tile if k == 6 else tile.astype(jnp.float32)

    def place(k, r, c, tile):
        if k < 6:
            ext[0, k, r, c] = tile
        elif k == 6:
            drag[r, c] = tile
        else:
            buoy[r, c] = wetness(tile)

    tail = pl.ds(cols, 128)
    foot = pl.ds(rows, 8)
    ones = jnp.full((8, 128), 0.2, jnp.float32)
    row_scale = zero_rows(ones)
    col_scale = zero_cols(ones)

    def halo_rows(t, carry):
        at = pl.ds(pl.multiple_of(t * 128, 128), 128)
        for k in range(8):
            place(k, foot, at, zero_rows(received(k, 0, slice(None), at)))
        for r in range(0, rows, 8):
            scale[r : r + 8, at] = ones
        scale[foot, at] = row_scale
        return carry

    lax.fori_loop(0, cols // 128, halo_rows, 0, unroll=True)
    for k in range(8):
        for r in range(0, rows, 8):
            at = (slice(r, r + 8), slice(None))
            tile = jnp.where(left_half, received(k, 2, *at), received(k, 1, *at))
            place(k, pl.ds(r, 8), tail, zero_cols(tile))
        at = (slice(None), slice(None))
        tile = jnp.where(left_half, received(k, 4, *at), received(k, 3, *at))
        place(k, foot, tail, zero_cols(zero_rows(tile)))
    for r in range(0, rows, 8):
        scale[r : r + 8, tail] = col_scale
    scale[foot, tail] = zero_cols(row_scale)

    lanes = lax.broadcasted_iota(jnp.int32, (tall, 128), 1)
    first_lane = lanes == 0
    last_lane = lanes == 127
    tiles = wide // 128

    def press(f0, f1, b):
        return b * (f0 + f1), upper_gravity * density_ratio * f0 + upper_gravity * f1

    def step(now, carry, final=False):
        later = 1 - now
        height = rows if final else tall
        cells = slice(0, height)

        def tile_step(t, carry):
            at = pl.ds(pl.multiple_of(t * 128, 128), 128)
            t_hi = jnp.where(t == tiles - 1, 0, t + 1)
            t_lo = jnp.where(t == 0, tiles - 1, t - 1)
            at_hi = pl.ds(pl.multiple_of(t_hi * 128, 128), 128)
            at_lo = pl.ds(pl.multiple_of(t_lo * 128, 128), 128)
            f = [ext[now, k, :, at] for k in range(6)]
            b = buoy[:, at]
            one, two = press(f[0], f[1], b)
            sums = [None] * 6

            def add(k, value):
                sums[k] = value if sums[k] is None else sums[k] + value

            for ahead in (True, False):
                by = tall - 1 if ahead else 1
                def rolled(x):
                    return pltpu.roll(x, by, 0)[cells]
                def mix(x, y):
                    return x - y if ahead else x + y
                add(0, rolled(mix(f[0], f[2])))
                add(1, rolled(mix(f[1], f[4])))
                add(2, rolled(mix(f[2], one)))
                add(3, rolled(f[3]))
                add(4, rolled(mix(f[4], two)))
                add(5, rolled(f[5]))
            f = [x[cells] for x in f]
            b = b[cells]
            for ahead in (True, False):
                by = 127 if ahead else 1
                edge = (first_lane if ahead else last_lane)[cells]
                other = at_hi if ahead else at_lo
                g = [jnp.where(edge, ext[now, k, cells, other], f[k]) for k in range(6)]
                gb = jnp.where(edge, buoy[cells, other], b)
                g_one, g_two = press(g[0], g[1], gb)
                def rolled(x):
                    return pltpu.roll(x, by, 1)
                def mix(x, y):
                    return x - y if ahead else x + y
                add(0, rolled(mix(g[0], g[3])))
                add(1, rolled(mix(g[1], g[5])))
                add(2, rolled(g[2]))
                add(3, rolled(mix(g[3], g_one)))
                add(4, rolled(g[4]))
                add(5, rolled(mix(g[5], g_two)))
            speed = jnp.sqrt(f[2] * f[2] + f[3] * f[3] + speed_floor)
            rub = 2.0 * drag[cells, at] * speed
            k = scale[cells, at]
            new = (
                k * (f[0] + sums[0]),
                k * (f[1] + sums[1]),
                k * (sums[2] + f[4] - rub * f[2]),
                k * (sums[3] + f[5] - rub * f[3]),
                k * (sums[4] + f[2]),
                k * (sums[5] + f[3]),
            )
            for n, value in enumerate(new):
                ext[later, n, cells, at] = value
            if final:
                speed = jnp.sqrt(new[2] * new[2] + new[3] * new[3] + speed_floor)
                rub = load_factor * drag[cells, at] * speed
                tract[0, :, at] = rub * new[2]
                tract[1, :, at] = rub * new[3]
                tract[2, :, at] = -load_factor * (b * (new[0] + new[1]))
            return carry

        return lax.fori_loop(0, tiles - 1 if final else tiles, tile_step, carry, unroll=True)

    lax.fori_loop(0, FLOW_STEPS // 2 - 1, lambda _, carry: step(1, step(0, carry)), 0)
    step(1, step(0, 0), final=True)
    store_fields.start()

    table_ref[...] = jnp.zeros_like(table_ref)
    narrow = jnp.bfloat16
    row16 = lax.broadcasted_iota(jnp.int32, (16, cols), 0)
    count = row16.astype(jnp.float32).astype(narrow)

    def spread(group, carry):
        lefts, rights = [], []
        for n in range(GROUP):
            line = pl.ds(group * GROUP + n, 1)

            def wide16(x):
                return jnp.broadcast_to(x, (16, cols)).astype(narrow)

            parts = []
            for k in range(3):
                value = tract[k, line, :]
                high = value.astype(narrow).astype(jnp.float32)
                parts.append(wide16(value))
                parts.append(wide16(value - high))
            a = wide16(row_slot[line, :])
            b = wide16(col_slot[line, :])
            zero = jnp.zeros((16, cols), narrow)
            one = jnp.ones((16, cols), narrow)
            pieces = []
            for top in range(0, table_ref.shape[0], 16):
                part, last = top // SLOT_ROWS, min((top + 15) // SLOT_ROWS, 5)
                skip = top - SLOT_ROWS * part
                if part == last:
                    pieces.append(jnp.where(a == count + narrow(skip), parts[part], zero))
                else:
                    split = SLOT_ROWS * last - top
                    target = row16 + jnp.where(row16 < split, skip, -split)
                    mixed = jnp.where(count < narrow(split), parts[part], parts[last])
                    pieces.append(jnp.where(a == target.astype(jnp.float32).astype(narrow), mixed, zero))
            lefts.append(jnp.concatenate(pieces, axis=0))
            rights.append(
                jnp.concatenate([jnp.where(b == count + narrow(16 * m), one, zero) for m in range(16)], axis=0)
            )
        table_ref[...] += lax.dot_general(
            jnp.concatenate(lefts, axis=1),
            jnp.concatenate(rights, axis=1),
            (((1,), (1,)), ((), ())),
            preferred_element_type=jnp.float32,
        )
        return carry

    lax.fori_loop(0, rows // GROUP, spread, 0)

    def part_rows(n):
        return table_ref[SLOT_ROWS * n : SLOT_ROWS * n + SLOT_ROWS]

    pad = jnp.zeros((64 - SLOT_ROWS, 256), jnp.float32)
    table = [
        jnp.concatenate([part_rows(2 * k) + part_rows(2 * k + 1), pad], axis=0) for k in range(3)
    ]
    load_parts(table, own_ref, beyond_ref, sides_ref)


def line(matrix, s):
    even = [s[0] + s[4], s[1] + s[3]]
    odd = [s[0] - s[4], s[1] - s[3]]
    out = [None] * 5
    for a in range(2):
        half_sum = [0.5 * (matrix[a, p] - matrix[a, 4 - p]) for p in range(2)]
        half_diff = [0.5 * (matrix[a, p] + matrix[a, 4 - p]) for p in range(2)]
        x = float(half_sum[0]) * odd[0] + float(half_sum[1]) * odd[1]
        y = float(half_diff[0]) * even[0] + float(half_diff[1]) * even[1] + float(matrix[a, 2]) * s[2]
        out[a] = x + y
        out[4 - a] = x - y
    out[2] = float(matrix[2, 0]) * odd[0] + float(matrix[2, 1]) * odd[1]
    return out


def lane_row():
    lane = lax.broadcasted_iota(jnp.int32, (4, 128), 1)
    row = lax.broadcasted_iota(jnp.int32, (4, 128), 0)
    return lane, row


def internal_open(u_ref, lame_ref, shear_ref, stress, force):
    table = derivative_table()

    def slope_x(m, carry):
        for i in range(3):
            lines = line(table, [u_ref[i * 125 + a * 25 + m] for a in range(5)])
            for a in range(5):
                stress[i * 125 + a * 25 + m] = lines[a]
        return carry

    lax.fori_loop(0, 25, slope_x, 0, unroll=True)

    def plane(a, carry):
        weight = jnp.where(
            (a == 0) | (a == 4),
            np.float32(gll_weights[0]),
            jnp.where(a == 2, np.float32(gll_weights[2]), np.float32(gll_weights[1])),
        )
        lame = lame_ref[...] * -weight
        shear = shear_ref[...] * -weight

        def at(i, b, c):
            return i * 125 + a * 25 + b * 5 + c

        slope_y, slope_z = [], []
        for i in range(3):
            u = [[u_ref[at(i, b, c)] for c in range(5)] for b in range(5)]
            along_y = [line(table, [u[b][c] for b in range(5)]) for c in range(5)]
            slope_y.append([[along_y[c][b] for c in range(5)] for b in range(5)])
            slope_z.append([line(table, u[b]) for b in range(5)])
        pull_y = [[[None] * 5 for b in range(5)] for i in range(3)]
        pull_z = [[[None] * 5 for b in range(5)] for i in range(3)]
        for b in range(5):
            for c in range(5):
                w = np.float32(gll_weights[b] * gll_weights[c])
                g = [[stress[at(i, b, c)], slope_y[i][b][c], slope_z[i][b][c]] for i in range(3)]
                mu = shear * w
                twice = mu + mu
                spread = (lame * w) * (g[0][0] + g[1][1] + g[2][2])
                s00 = spread + twice * g[0][0]
                s11 = spread + twice * g[1][1]
                s22 = spread + twice * g[2][2]
                s01 = mu * (g[0][1] + g[1][0])
                s02 = mu * (g[0][2] + g[2][0])
                s12 = mu * (g[1][2] + g[2][1])
                stress[at(0, b, c)] = s00
                stress[at(1, b, c)] = s01
                stress[at(2, b, c)] = s02
                for i, (s_y, s_z) in enumerate(((s01, s02), (s11, s12), (s12, s22))):
                    pull_y[i][b][c] = s_y
                    pull_z[i][b][c] = s_z
        for i in range(3):
            along_y = [line(table.T, [pull_y[i][b][c] for b in range(5)]) for c in range(5)]
            for b in range(5):
                along_z = line(table.T, pull_z[i][b])
                for c in range(5):
                    force[at(i, b, c)] = along_y[c][b] + along_z[c]
        return carry

    lax.fori_loop(0, 5, plane, 0)


def internal_kick(kick, lame_ref, shear_ref, force):
    table = derivative_table()
    lame, shear = -lame_ref[...], -shear_ref[...]
    five = range(5)

    def grid(make):
        return [[make(a, b) for b in five] for a in five]

    def along_x(matrix, x):
        lines = [line(matrix, [x[a][b] for a in five]) for b in five]
        return grid(lambda a, b: lines[b][a])

    def along_y(matrix, x):
        lines = [line(matrix, x[a]) for a in five]
        return grid(lambda a, b: lines[a][b])

    def plus(x, y):
        return grid(lambda a, b: x[a][b] + y[a][b])

    def area(a, b):
        return np.float32(gll_weights[a] * gll_weights[b])

    d = [grid(lambda a, b: kick[i * 25 + a * 5 + b]) for i in range(3)]
    d_x = [along_x(table, x) for x in d]
    d_y = [along_y(table, x) for x in d]
    lame_w = grid(lambda a, b: lame * area(a, b))
    shear_w = grid(lambda a, b: shear * area(a, b))
    t_side = grid(lambda a, b: lame_w[a][b] * d[2][a][b])
    t_02 = grid(lambda a, b: shear_w[a][b] * d[0][a][b])
    t_12 = grid(lambda a, b: shear_w[a][b] * d[1][a][b])
    t_22 = grid(lambda a, b: t_side[a][b] + (shear_w[a][b] + shear_w[a][b]) * d[2][a][b])
    first = np.float32(gll_weights[0])
    l_0 = grid(lambda a, b: first * lame_w[a][b])
    m_0 = grid(lambda a, b: first * shear_w[a][b])
    e_22 = grid(lambda a, b: l_0[a][b] * (d_x[0][a][b] + d_y[1][a][b]))
    e_00 = grid(lambda a, b: e_22[a][b] + (m_0[a][b] + m_0[a][b]) * d_x[0][a][b])
    e_11 = grid(lambda a, b: e_22[a][b] + (m_0[a][b] + m_0[a][b]) * d_y[1][a][b])
    e_01 = grid(lambda a, b: m_0[a][b] * (d_y[0][a][b] + d_x[1][a][b]))
    e_02 = grid(lambda a, b: m_0[a][b] * d_x[2][a][b])
    e_12 = grid(lambda a, b: m_0[a][b] * d_y[2][a][b])
    turned = table.T
    pulled = (
        along_x(turned, t_side),
        along_y(turned, t_side),
        plus(along_x(turned, t_02), along_y(turned, t_12)),
    )
    flat = (
        plus(along_x(turned, e_00), along_y(turned, e_01)),
        plus(along_x(turned, e_01), along_y(turned, e_11)),
        plus(along_x(turned, e_02), along_y(turned, e_12)),
    )
    share = [float(table[c, 0] * gll_weights[c]) for c in five]
    upright = [float(sum(table[p, c] * share[p] for p in five)) for c in five]
    for i, (t, e) in enumerate(((t_02, e_02), (t_12, e_12), (t_22, e_22))):
        for a in five:
            for b in five:
                for c in five:
                    value = share[c] * pulled[i][a][b] + upright[c] * t[a][b]
                    value = value + float(table[0, c]) * e[a][b]
                    if c == 0:
                        value = value + flat[i][a][b]
                    force[i * 125 + a * 25 + b * 5 + c] += value


def internal_close(stress, force):
    table = derivative_table()
    lane, row = lane_row()
    low_x = row % 2 == 0
    low_z = row < 2

    def close_x(m, carry):
        for i in range(3):
            pulled = line(table.T, [stress[i * 125 + a * 25 + m] for a in range(5)])
            f = [force[i * 125 + a * 25 + m] + pulled[a] for a in range(5)]
            near = f[0] + jnp.where(low_x, 0.0, pltpu.roll(f[4], 1, 0))
            far = f[4] + jnp.where(low_x, pltpu.roll(f[0], 3, 0), 0.0)
            for a, value in enumerate((near, f[1], f[2], f[3], far)):
                force[i * 125 + a * 25 + m] = value
        return carry

    lax.fori_loop(0, 25, close_x, 0, unroll=True)

    def close_yz(ia, carry):
        base = ia * 25
        f = [[force[base + b * 5 + c] for c in range(5)] for b in range(5)]
        for c in range(5):
            near, far = f[0][c], f[4][c]
            f[0][c] = near + jnp.where(lane == 0, 0.0, pltpu.roll(far, 1, 1))
            f[4][c] = far + jnp.where(lane == 127, 0.0, pltpu.roll(near, 127, 1))
        for b in range(5):
            near, far = f[b][0], f[b][4]
            f[b][0] = near + jnp.where(low_z, 0.0, pltpu.roll(far, 2, 0))
            f[b][4] = far + jnp.where(low_z, pltpu.roll(near, 2, 0), 0.0)
        for b in range(5):
            for c in range(5):
                if b in (0, 4) or c in (0, 4):
                    force[base + b * 5 + c] = f[b][c]
        return carry

    lax.fori_loop(0, 15, close_yz, 0, unroll=True)


def pack_faces_y(force, face_y):
    lane, row = lane_row()
    ends = [jnp.zeros((4, 128), jnp.float32)] * 2
    for a in range(5):
        for i in range(3):
            for c in range(5):
                q = a * 15 + i * 5 + c
                n = i * 125 + a * 25 + c
                ends[0] = jnp.where(lane == q, pltpu.roll(force[n], q, 1), ends[0])
                ends[1] = jnp.where(lane == q, pltpu.roll(force[n + 20], q + 1, 1), ends[1])
    face_y[0] = ends[0]
    face_y[1] = ends[1]


def pack_faces_x(force, face_x):
    lane, row = lane_row()
    low_x = row % 2 == 0

    def both(m, other):
        for i in range(3):
            near, far = force[i * 125 + m], force[i * 125 + 100 + m]
            near_other, far_other = force[i * 125 + other], force[i * 125 + 100 + other]
            face_x[0, i * 13 + m] = jnp.where(low_x, near, pltpu.roll(near_other, 1, 0))
            face_x[1, i * 13 + m] = jnp.where(low_x, pltpu.roll(far, 3, 0), far_other)

    def pack_x(m, carry):
        both(m, m + 13)
        return carry

    lax.fori_loop(0, 12, pack_x, 0, unroll=True)
    both(12, 12)


def open_edges():
    at_x, at_y = lax.axis_index("gx"), lax.axis_index("gy")
    has = {-1: at_x > 0, 1: at_x < lax.axis_size("gx") - 1}
    has_y = {-1: at_y > 0, 1: at_y < lax.axis_size("gy") - 1}
    return has, has_y


def add_faces(target, got_x, got_y, factor, arrive):
    has_x, has_y = open_edges()
    lane, row = lane_row()
    low_x = row % 2 == 0
    from_low = low_x & has_x[-1]
    from_high = jnp.logical_not(low_x) & has_x[1]
    arrive(AROUND[:2])
    for m in range(13):
        for i in range(3):
            low, high = got_x[0][i * 13 + m], got_x[1][i * 13 + m]
            pairs = [(m, low, pltpu.roll(high, 1, 0))]
            if m < 12:
                pairs.append((m + 13, pltpu.roll(low, 3, 0), high))
            for at, near, far in pairs:
                b, c = at // 5, at % 5
                target[i * 125 + at] += factor(0, b, c, jnp.where(from_low, near, 0.0))
                target[i * 125 + 100 + at] += factor(4, b, c, jnp.where(from_high, far, 0.0))

    def add_columns(columns, ends):
        for a in ends:
            for i in range(3):
                for c in range(5):
                    q = a * 15 + i * 5 + c
                    n = i * 125 + a * 25 + c
                    near = jnp.where(lane == 0, pltpu.roll(columns[0], (128 - q) % 128, 1), 0.0)
                    far = jnp.where(lane == 127, pltpu.roll(columns[1], 127 - q, 1), 0.0)
                    target[n] += factor(a, 0, c, near)
                    target[n + 20] += factor(a, 4, c, far)

    sides = ((-1, 1), (1, 0))
    arrive(AROUND[2:4])
    add_columns([jnp.where(has_y[side], got_y[0, side][end], 0.0) for side, end in sides], range(5))
    arrive(AROUND[4:])
    first, final = lane < 15, (lane >= 60) & (lane < 75)
    columns = []
    for side, end in sides:
        low = pltpu.roll(pltpu.roll(got_y[-1, side][end], 68, 1), 3, 0)
        high = pltpu.roll(pltpu.roll(got_y[1, side][end], 60, 1), 1, 0)
        total = jnp.where(first & low_x & has_x[-1], low, 0.0)
        total = total + jnp.where(final & jnp.logical_not(low_x) & has_x[1], high, 0.0)
        columns.append(jnp.where(has_y[side], total, 0.0))
    add_columns(columns, (0, 4))


def inverse_masses(density_ref, around, inverse):
    has_x, has_y = open_edges()
    lane, row = lane_row()
    low_x = row % 2 == 0
    low_z = row < 2

    def beside(mine, left, right):
        left = jnp.where(has_y[-1], left, 0.0)
        right = jnp.where(has_y[1], right, 0.0)
        before = jnp.where(lane == 0, pltpu.roll(left, 1, 1), pltpu.roll(mine, 1, 1))
        after = jnp.where(lane == 127, pltpu.roll(right, 127, 1), pltpu.roll(mine, 127, 1))
        return mine + before, mine, mine + after

    mine = beside(density_ref[...], around[0, -1][...], around[0, 1][...])
    low = beside(around[-1, 0][...], around[-1, -1][...], around[-1, 1][...])
    high = beside(around[1, 0][...], around[1, -1][...], around[1, 1][...])
    for b in range(3):
        lo = jnp.where(has_x[-1], low[b], 0.0)
        hi = jnp.where(has_x[1], high[b], 0.0)
        before = mine[b] + jnp.where(low_x, pltpu.roll(lo, 3, 0), pltpu.roll(mine[b], 1, 0))
        after = mine[b] + jnp.where(low_x, pltpu.roll(mine[b], 3, 0), pltpu.roll(hi, 1, 0))
        for a, value in enumerate((before, mine[b], after)):
            top = value + jnp.where(low_z, 0.0, pltpu.roll(value, 2, 0))
            bottom = value + jnp.where(low_z, pltpu.roll(value, 2, 0), 0.0)
            for c, total in enumerate((top, value, bottom)):
                inverse[a * 9 + b * 3 + c] = (solid_dt * solid_dt) / total


def kind(node):
    return 0 if node == 0 else 2 if node == 4 else 1


def moved_by(inverse, a, b, c, f):
    w = np.float32(1.0 / (gll_weights[a] * gll_weights[b] * gll_weights[c]))
    return (inverse[kind(a) * 9 + kind(b) * 3 + kind(c)] * w) * f


def advance_solid(force, load, inverse, now_ref, before_ref, out_ref):
    def component(i, carry):
        for a in range(5):
            for b in range(5):
                for c in range(5):
                    n = a * 25 + b * 5 + c
                    f = force[i * 125 + n]
                    if c == 0 and load is not None:
                        f = f + load[i * 25 + a * 5 + b]
                    step = moved_by(inverse, a, b, c, f)
                    at = i * 125 + n
                    out_ref[at] = (now_ref[at] + now_ref[at] - before_ref[at]) + step
        return carry

    lax.fori_loop(0, 3, component, 0)


def kick_solid(load, inverse, out_ref, kick):
    def component(i, carry):
        for a in range(5):
            for b in range(5):
                n = i * 25 + a * 5 + b
                step = moved_by(inverse, a, b, 0, load[n])
                kick[n] = step
                out_ref[i * 125 + a * 25 + b * 5] += step
        return carry

    lax.fori_loop(0, 3, component, 0)


def load_grid():
    row = lax.broadcasted_iota(jnp.int32, (56, 128), 0)
    lane = lax.broadcasted_iota(jnp.int32, (56, 128), 1)
    return row, lane


def rows_up(x, by):
    return jnp.concatenate([x[by:], jnp.zeros((by, 128), jnp.float32)], axis=0)


def rows_down(x, by):
    return jnp.concatenate([jnp.zeros((by, 128), jnp.float32), x[:-by]], axis=0)


def masks_x():
    row, lane = load_grid()
    even = row % 2 == 0
    odd = row % 2 == 1
    return (row < 10) & even, (row < 10) & odd, (row >= 40) & (row < 50) & even, (row >= 40) & (row < 50) & odd


def masks_y():
    row, lane = load_grid()
    place = row % 10
    return (place < 2) & (row < 50), (place >= 8) & (row < 50), lane == 0, lane == 127


def join_x(x):
    near_even, near_odd, far_even, far_odd = masks_x()
    return (
        x
        + jnp.where(near_odd, pltpu.roll(rows_up(x, 40), 1, 0), 0.0)
        + jnp.where(far_even, pltpu.roll(rows_down(x, 40), 55, 0), 0.0)
    )


def join_x_wide(own, halo):
    near_even, near_odd, far_even, far_odd = masks_x()
    own_new = join_x(own)
    own_new = own_new + jnp.where(near_even, rows_up(halo, 40), 0.0)
    own_new = own_new + jnp.where(far_odd, rows_down(halo, 40), 0.0)
    halo_new = halo + jnp.where(far_even, rows_down(own, 40), 0.0)
    halo_new = halo_new + jnp.where(near_odd, rows_up(own, 40), 0.0)
    return own_new, halo_new


def join_y(x, sides):
    near, far, first, final = masks_y()
    before, after = pltpu.roll(x, 1, 1), pltpu.roll(x, 127, 1)
    fill_before = 0.0 if sides is None else pltpu.roll(sides, 1, 1)
    fill_after = 0.0 if sides is None else pltpu.roll(sides, 127, 1)
    out = x + jnp.where(near, rows_up(jnp.where(first, fill_before, before), 8), 0.0)
    out = out + jnp.where(far, rows_down(jnp.where(final, fill_after, after), 8), 0.0)
    if sides is None:
        return out
    new = sides + jnp.where(far & final, rows_down(after, 8), 0.0)
    new = new + jnp.where(near & first, rows_up(before, 8), 0.0)
    return out, new


def columns_from(tile):
    row, lane = load_grid()
    turned = jnp.concatenate([tile, jnp.zeros((120, 128), jnp.float32)], axis=0).T
    out = []
    for k in range(3):
        halves = []
        for h in range(2):
            part = turned[64 * h : 64 * h + 56]
            left = pltpu.roll(part, 127 - 2 * k, 1)
            right = pltpu.roll(part, (128 - 2 * k - 1) % 128, 1)
            value = jnp.where(lane == 127, left, jnp.where(lane == 0, right, 0.0))
            halves.append(jnp.where(row < 50, value, 0.0))
        out.append(halves)
    return out


def columns_to(columns):
    lane = lax.broadcasted_iota(jnp.int32, (128, 128), 1)
    total = jnp.zeros((128, 128), jnp.float32)
    for k in range(3):
        pad = jnp.zeros((8, 128), jnp.float32)
        x = jnp.concatenate([columns[k][0], pad, columns[k][1], pad], axis=0)
        total = jnp.where(lane == 2 * k, pltpu.roll(x, 2 * k + 1, 1), total)
        total = jnp.where(lane == 2 * k + 1, pltpu.roll(x, 2 * k + 1, 1), total)
    return total.T[:8]


def load_parts(table, own_ref, beyond_ref, sides_ref):
    row, lane = load_grid()
    line_of = lax.broadcasted_iota(jnp.int32, (8, 128), 0)
    raw = jnp.zeros((8, 128), jnp.float32)
    for k in range(3):
        for side in range(2):
            last = jnp.broadcast_to(table[k][50:51, 128 * side : 128 * side + 128], (8, 128))
            raw = jnp.where(line_of == 2 * k + side, last, raw)
    columns = columns_from(raw)
    new_columns = []
    for k in range(3):
        own = jnp.where(row < 50, table[k][:56, :128], 0.0)
        halo = jnp.where(row < 50, table[k][:56, 128:], 0.0)
        own, halo = join_x_wide(own, halo)
        sides = join_x_wide(columns[k][0], columns[k][1])
        own, side_own = join_y(own, sides[0])
        halo, side_halo = join_y(halo, sides[1])
        own_ref[k] = own
        beyond_ref[k] = halo
        new_columns.append((side_own, side_halo))
    sides_ref[...] = columns_to(new_columns)


def load_total(own_ref, got_x, got_y, load):
    has_x, has_y = open_edges()
    row, lane = load_grid()
    even = row % 2 == 0
    tile_lane = lax.broadcasted_iota(jnp.int32, (8, 128), 1)
    tile_row = lax.broadcasted_iota(jnp.int32, (8, 128), 0)
    ends = []
    for side in (-1, 1):
        low = jnp.where(has_x[-1], pltpu.roll(got_y[-1, side][...], 127, 1), 0.0)
        high = jnp.where(has_x[1], pltpu.roll(got_y[1, side][...], 1, 1), 0.0)
        tile = jnp.where(tile_lane < 64, got_y[0, side][...], jnp.where(tile_lane % 2 == 0, low, high))
        ends.append(jnp.where(has_y[side], tile, 0.0))
    columns = columns_from(jnp.where(tile_row % 2 == 0, ends[1], ends[0]))
    for k in range(3):
        low = jnp.where(has_x[-1], pltpu.roll(got_x[0][k], 55, 0), 0.0)
        high = jnp.where(has_x[1], pltpu.roll(got_x[1][k], 1, 0), 0.0)
        rows = jnp.where(even, low, high) + join_y(columns[k][1], None)
        total = own_ref[k] + join_x(jnp.where(row < 50, rows, 0.0)) + join_y(columns[k][0], None)
        for n in range(25):
            load[k * 25 + n] = jnp.concatenate(
                [total[2 * n : 2 * n + 2], jnp.zeros((2, 128), jnp.float32)], axis=0
            )


AROUND = [(-1, 0), (1, 0), (0, -1), (0, 1), (-1, -1), (-1, 1), (1, -1), (1, 1)]
ASIDE = AROUND[2:]


def shape(*dims, kind=jnp.float32):
    return jax.ShapeDtypeStruct(dims, kind)


def halo_plan(rows, cols):
    edge_rows = {-1: pl.ds(0, 4), 1: pl.ds(rows - 4, 4)}
    edge_cols = {-1: pl.ds(0, 128), 1: pl.ds(cols - 128, 128)}
    place_rows = {-1: pl.ds(0, 4), 1: pl.ds(4, 4)}
    messages = []
    for source in range(3):
        every = (slice(None),) if source == 0 else ()
        for dx, dy in AROUND:
            row_in = edge_rows.get(dx, pl.ds(0, rows))
            row_out = place_rows.get(dx, pl.ds(0, rows))
            col_in = edge_cols.get(dy, pl.ds(0, cols))
            where = 0 if dy == 0 else (1 if dx == 0 else 3) + (0 if dy == 1 else 1)
            messages.append(
                (source, every + (row_in, col_in), 5 * source + where,
                 every + (row_out, pl.ds(0, cols if dy == 0 else 128)), (dx, dy))
            )
    return messages


def whole_body(*refs):
    (flow_in, drag_in, wet_in, elem_in, node_in, u_in, before_in, density_in, lame_in, shear_in) = refs[:10]
    fields_out, next_out, last_out = refs[10:13]
    (ext, drag, buoy, scale, tract, row_slot, col_slot, table) = refs[13:21]
    halos = refs[21:36]
    (drag_own, wet_own, elem_own, node_own) = refs[36:40]
    (u_zero, before, u_one, u_two, force, stress, load, inverse) = refs[40:48]
    (density, lame, shear, around) = refs[48:52]
    (face_x, face_y, got_face_x, got_face_y) = refs[52:56]
    (own, beyond, sides, got_beyond, got_sides, kick) = refs[56:62]
    local_sem, sent, come = refs[62:]
    rows, cols = drag_own.shape
    at_x, at_y = lax.axis_index("gx"), lax.axis_index("gy")
    size_x, size_y = lax.axis_size("gx"), lax.axis_size("gy")

    def device(move):
        return ((at_x + move[0] + size_x) % size_x, (at_y + move[1] + size_y) % size_y)

    def opposite(move):
        return -move[0], -move[1]

    def there(move):
        x, y = at_x + move[0], at_y + move[1]
        return (x >= 0) & (x < size_x) & (y >= 0) & (y < size_y)

    barrier = pltpu.get_barrier_semaphore()
    for move in AROUND:

        @pl.when(there(move))
        def _(move=move):
            pl.semaphore_signal(barrier, inc=1, device_id=device(move), device_id_type=pl.DeviceIdType.MESH)

    reads = [
        pltpu.make_async_copy(source, target, local_sem.at[n])
        for n, (source, target) in enumerate(
            (
                (u_in, u_zero), (lame_in, lame), (shear_in, shear), (density_in, density),
                (flow_in, ext.at[0, :, 0:rows, 0:cols]), (drag_in, drag_own), (wet_in, wet_own),
                (elem_in, elem_own), (node_in, node_own), (before_in, before),
            )
        )
    ]
    for copy in reads:
        copy.start()
    store_fields = pltpu.make_async_copy(ext.at[0, :, 0:rows, 0:cols], fields_out, local_sem.at[10])
    store_last = pltpu.make_async_copy(u_one, last_out, local_sem.at[11])
    store_next = pltpu.make_async_copy(u_two, next_out, local_sem.at[12])
    beside_x = 3 - jnp.where(at_x == 0, 1, 0) - jnp.where(at_x == size_x - 1, 1, 0)
    beside_y = 3 - jnp.where(at_y == 0, 1, 0) - jnp.where(at_y == size_y - 1, 1, 0)
    pl.semaphore_wait(barrier, beside_x * beside_y - 1)
    number = [0]

    def send(source, target, move):
        n = number[0]
        number[0] += 1
        copy = pltpu.make_async_remote_copy(
            src_ref=source, dst_ref=target, send_sem=sent.at[n], recv_sem=come.at[n],
            device_id=device(move), device_id_type=pl.DeviceIdType.MESH,
        )
        return copy, move

    def each(messages, toward, act):
        for move in AROUND:
            mine = [copy for copy, way in messages if way == move]
            if mine:

                @pl.when(there(move if toward else opposite(move)))
                def _(mine=mine):
                    for copy in mine:
                        act(copy)

    def launch(messages):
        each(messages, True, lambda copy: copy.start())

    def finish(messages, moves=AROUND):
        some = [message for message in messages if message[1] in moves]
        each(some, False, lambda copy: copy.wait_recv())

    def drain(messages):
        each(messages, True, lambda copy: copy.wait_send())

    operands = (flow_in, drag_in, wet_in)
    first = [
        send(operands[source].at[source_at], halos[target].at[target_at], move)
        for source, source_at, target, target_at, move in halo_plan(rows, cols)
    ]
    first += [send(density_in, around.at[AROUND.index(opposite(move))], move) for move in AROUND]
    launch(first)

    def send_faces(step):
        pack_faces_y(force, face_y.at[step])
        far = [
            (face_y.at[step], got_face_y.at[step, ASIDE.index(opposite(move))], move) for move in ASIDE
        ]
        copies = [send(*message) for message in far]
        launch(copies)
        pack_faces_x(force, face_x.at[step])
        near = [
            send(face_x.at[step, 0], got_face_x.at[step, 1], (-1, 0)),
            send(face_x.at[step, 1], got_face_x.at[step, 0], (1, 0)),
        ]
        launch(near)
        return near + copies

    def faces_of(step):
        return (
            [got_face_x.at[step, n] for n in range(2)],
            {move: got_face_y.at[step, n] for n, move in enumerate(ASIDE)},
        )

    for copy in reads[:3]:
        copy.wait()
    internal_open(u_zero, lame, shear, stress, force)
    internal_close(stress, force)
    faces = send_faces(0)
    for copy in reads[3:]:
        copy.wait()

    def arrive():
        finish(first)
        inverse_masses(density, {move: around.at[n] for n, move in enumerate(AROUND)}, inverse)

    surface(
        drag_own, wet_own, elem_own, node_own, arrive, (halos[0:5], halos[5:10], halos[10:15]),
        own, beyond, sides, ext, drag, buoy, scale, tract, row_slot, col_slot, table, store_fields,
    )
    loads = [send(beyond, got_beyond.at[1], (-1, 0)), send(beyond, got_beyond.at[0], (1, 0))]
    for move in ASIDE:
        loads.append(send(sides, got_sides.at[ASIDE.index(opposite(move))], move))
    launch(loads)
    add_faces(force, *faces_of(0), lambda a, b, c, f: f, lambda moves: finish(faces, [opposite(move) for move in moves]))
    advance_solid(force, None, inverse, u_zero, before, u_one)
    internal_open(u_one, lame, shear, stress, force)
    finish(loads)
    load_total(
        own,
        [got_beyond.at[n] for n in range(2)],
        {move: got_sides.at[n] for n, move in enumerate(ASIDE)},
        load,
    )
    kick_solid(load, inverse, u_one, kick)
    store_last.start()
    internal_kick(kick, lame, shear, force)
    internal_close(stress, force)
    last_faces = send_faces(1)
    advance_solid(force, load, inverse, u_one, u_zero, u_two)
    add_faces(
        u_two, *faces_of(1), lambda a, b, c, f: moved_by(inverse, a, b, c, f),
        lambda moves: finish(last_faces, [opposite(move) for move in moves]),
    )
    store_next.start()
    drain(first + faces + loads + last_faces)
    store_fields.wait()
    store_last.wait()
    store_next.wait()


def store_body(*refs):
    taken, given = refs[9:]
    reads, writes = [], []
    for n in range(3):
        source, target, held = refs[n], refs[3 + n], refs[6 + n]
        step = source.shape[0] // 3
        for m in range(3):
            part = pl.ds(m * step, step)
            at = 3 * n + m
            reads.append(pltpu.make_async_copy(source.at[part], held.at[part], taken.at[at]))
            writes.append(pltpu.make_async_copy(held.at[part], target.at[part], given.at[at]))
    for copy in reads:
        copy.start()
    for read, write in zip(reads, writes):
        read.wait()
        write.start()
    for copy in writes:
        copy.wait()


def per_device(
    flow_state,
    drag_coefficient,
    wet_mask,
    target_elem,
    target_node,
    displacement,
    previous,
    density,
    lame_first,
    shear_modulus,
):
    rows, cols = drag_coefficient.shape
    tall, wide = rows + 8, cols + 128
    grid = displacement.shape
    nodes = (375, 4, 128)
    halo_shapes = []
    for lead, kind_of in (((6,), jnp.float32), ((), jnp.float32), ((), jnp.int32)):
        for dims in ((8, cols), (rows, 128), (rows, 128), (8, 128), (8, 128)):
            halo_shapes.append(pltpu.VMEM((*lead, *dims), kind_of))

    def floats(*dims):
        return pltpu.VMEM(dims, jnp.float32)

    def integers(*dims):
        return pltpu.VMEM(dims, jnp.int32)

    scratch = [
        floats(2, 6, tall, wide), floats(tall, wide), floats(tall, wide), floats(tall, wide),
        floats(3, rows, cols), floats(rows, cols), floats(rows, cols), floats(320, 256),
        *halo_shapes,
        floats(rows, cols), integers(rows, cols), integers(rows, cols), integers(rows, cols),
        *[floats(*nodes)] * 6, floats(75, 4, 128), floats(27, 4, 128),
        floats(4, 128), floats(4, 128), floats(4, 128), floats(8, 4, 128),
        floats(2, 2, 39, 4, 128), floats(2, 2, 4, 128), floats(2, 2, 39, 4, 128), floats(2, 6, 2, 4, 128),
        floats(3, 56, 128), floats(3, 56, 128), floats(8, 128), floats(2, 3, 56, 128), floats(6, 8, 128), floats(75, 4, 128),
        pltpu.SemaphoreType.DMA((13,)), pltpu.SemaphoreType.DMA((56,)), pltpu.SemaphoreType.DMA((56,)),
    ]
    anywhere = pl.BlockSpec(memory_space=pl.ANY)
    results = pl.pallas_call(
        whole_body,
        out_shape=(shape(6, rows, cols), shape(*nodes), shape(*nodes)),
        in_specs=[anywhere] * 10,
        out_specs=(anywhere,) * 3,
        scratch_shapes=scratch,
        compiler_params=pltpu.CompilerParams(
            collective_id=1, has_side_effects=True, vmem_limit_bytes=56 * 2**20
        ),
    )(
        flow_state, drag_coefficient, wet_mask, target_elem, target_node,
        displacement.reshape(nodes), previous.reshape(nodes),
        *(x.reshape(4, 128) for x in (density, lame_first, shear_modulus)),
    )
    fields, u_two, u_one = pl.pallas_call(
        store_body,
        out_shape=tuple(shape(*x.shape) for x in results),
        in_specs=[anywhere] * 3,
        out_specs=(anywhere,) * 3,
        scratch_shapes=[
            *[pltpu.VMEM(x.shape, jnp.float32) for x in results],
            pltpu.SemaphoreType.DMA((9,)), pltpu.SemaphoreType.DMA((9,)),
        ],
        compiler_params=pltpu.CompilerParams(vmem_limit_bytes=60 * 2**20),
    )(*results)
    return (fields, u_two.reshape(grid), u_one.reshape(grid))


def solution(mesh):
    return jax.shard_map(
        per_device,
        mesh=mesh,
        in_specs=(
            P(None, "gx", "gy"),
            P("gx", "gy"),
            P("gx", "gy"),
            P("gx", "gy"),
            P("gx", "gy"),
            P(None, None, None, None, None, "gx", "gy"),
            P(None, None, None, None, None, "gx", "gy"),
            P(None, "gx", "gy"),
            P(None, "gx", "gy"),
            P(None, "gx", "gy"),
        ),
        out_specs=(
            P(None, "gx", "gy"),
            P(None, None, None, None, None, "gx", "gy"),
            P(None, None, None, None, None, "gx", "gy"),
        ),
        check_vma=False,
    )
```
